32 devices in a mesh: dp: 8 (over y, x, core), seq: 4 (over z).
Axes of the slice: x: 2, y: 2, z: 4, core: 2. Of those that a mesh axis runs over, the one named last changes fastest.
Arguments:
- frames: bfloat16 [16, 1024, 768], P('dp', 'seq'), may hold values from -6 to 6
- output_gradient: bfloat16 [16, 1024, 768], P('dp', 'seq'), may hold values from -6 to 6
- segments: int32 [16, 1024], replicated, may hold values from 0 to 4, as said below
- layer_keep: int32 [16], replicated, may hold values from 0 to 1, as said below
- conv_weight: bfloat16 [128, 768, 48], replicated, may hold values from -0.078125 to 0.078125
- convolution_bias: float32 [768], replicated, may hold values from -3 to 3
- query_matrix: bfloat16 [768, 768], replicated, may hold values from -0.21875 to 0.21875
- query_offset_bias: float32 [768], replicated, may hold values from -3 to 3
- key_matrix: bfloat16 [768, 768], replicated, may hold values from -0.21875 to 0.21875
- value_matrix: bfloat16 [768, 768], replicated, may hold values from -0.21875 to 0.21875
- value_offset_bias: float32 [768], replicated, may hold values from -3 to 3
- attn_weight: bfloat16 [768, 768], replicated, may hold values from -0.875 to 0.875
- attn_bias: float32 [768], replicated, may hold values from -2 to 2
- first_gain: float32 [768], replicated, may hold values from 0.25 to 1.75
- first_shift: float32 [768], replicated, may hold values from -2 to 2
- inner_weight: bfloat16 [768, 3072], replicated, may hold values from -0.21875 to 0.21875
- inner_bias: float32 [3072], replicated, may hold values from -2 to 2
- outer_weight: bfloat16 [3072, 768], replicated, may hold values from -0.109375 to 0.109375
- outer_bias: float32 [768], replicated, may hold values from -2 to 2
- second_gain: float32 [768], replicated, may hold values from 0.25 to 1.75
- second_shift: float32 [768], replicated, may hold values from -2 to 2
Outputs:
- layer_out: bfloat16 [16, 1024, 768], P('dp', 'seq')
- input_grad: bfloat16 [16, 1024, 768], P('dp', 'seq')
- conv_weight_grad: float32 [128, 768, 48], P(None, 'dp')
- conv_bias_grad: float32 [768], P('dp')
- query_weight_grad: float32 [768, 768], P(None, 'dp')
- query_bias_grad: float32 [768], P('dp')
- key_weight_grad: float32 [768, 768], P(None, 'dp')
- value_weight_grad: float32 [768, 768], P(None, 'dp')
- value_bias_grad: float32 [768], P('dp')
- attn_weight_grad: float32 [768, 768], P(None, 'dp')
- attn_bias_grad: float32 [768], P('dp')
- first_gain_grad: float32 [768], P('dp')
- first_shift_grad: float32 [768], P('dp')
- inner_weight_grad: float32 [768, 3072], P(None, 'dp')
- inner_bias_grad: float32 [3072], P('dp')
- outer_weight_grad: float32 [3072, 768], P(None, 'dp')
- outer_bias_grad: float32 [768], P('dp')
- second_gain_grad: float32 [768], P('dp')
- second_shift_grad: float32 [768], P('dp')
The draws below stay inside these ranges and needn't reach their ends.
Inputs may be any that keep to these rules, and one draw needn't show every extreme that they name: `segments`: in every row, 0 marks padding and the utterances are numbered 1, 2, ... from the row's start with padding only after the last; each utterance has 256 to 1024 frames. `layer_keep`: exactly max(1, 1) rows have 0, the others 1.
All inputs are finite; a program needn't handle non-finite values.
Results may differ from the reference program's by a relative error of at most 0.023.
Values may be sent and summed in bfloat16 or wider, within the bound.
No kernel may reach another device: no remote copies, remote signals or barrier semaphores. Data moves between devices by JAX's collectives and lax.ppermute only.
A program may use at most 512 MiB of HBM per device.

```python
import jax
import jax.numpy as jnp
from jax import lax

MODEL_WIDTH = 768
HEAD_SIZE = 64
FF = 3072
KW = 128
CONV_GROUP_COUNT = 16
ROW_FRAMES = 1024
ROW_TOTAL = 16
ATTENTION_HEADS = 12
GROUP_CHANNELS = 48
UTT_MIN = 256
UTT_MAX = 1024


def draw_segments(key, part):
    lengths = jax.random.randint(jax.random.fold_in(key, 11), (ROW_TOTAL, 4), UTT_MIN, UTT_MAX + 1)
    expected_result = jax.random.randint(jax.random.fold_in(key, 12), (ROW_TOTAL, 1), 1, 5)
    row_index = jnp.arange(ROW_TOTAL, dtype=jnp.int32)[:, None]
    position_index = jnp.arange(4, dtype=jnp.int32)[None, :]
    lengths = jnp.where((row_index == 0) & (position_index == 0), UTT_MAX, lengths)
    lengths = jnp.where(row_index == 1, UTT_MIN, lengths)
    expected_result = jnp.where(row_index == 1, 4, expected_result)
    segment_limits = jnp.cumsum(lengths, axis=1)
    active_flags = (position_index < expected_result) & (segment_limits <= ROW_FRAMES)
    frame_position = jnp.arange(ROW_FRAMES, dtype=jnp.int32)[None, :, None]
    passed = jnp.sum(((frame_position >= segment_limits[:, None, :]) & active_flags[:, None, :]).astype(jnp.int32), axis=2)
    live_count = jnp.sum(active_flags.astype(jnp.int32), axis=1)[:, None]
    return jnp.where(passed < live_count, passed + 1, 0).astype(jnp.int32)


def draw_layer_keep(key, part):
    order = jax.random.permutation(jax.random.fold_in(key, 21), ROW_TOTAL).astype(jnp.int32)
    dropped = max(1, ROW_TOTAL // 10)
    return jnp.where(order < dropped, 0, 1).astype(jnp.int32)


def block_levels(own_key, shape, shards, least, largest):
    def one(dim, blocks):
        heights = jax.random.uniform(jax.random.fold_in(jax.random.fold_in(own_key, 6), dim), (blocks,), jnp.float32, least / len(shards), largest / len(shards))
        return jnp.repeat(jnp.exp(heights), shape[dim] // blocks).reshape((-1,) + (1,) * (len(shape) - dim - 1))

    loudness = one(*shards[0])
    for cut in shards[1:]:
        loudness = loudness * one(*cut)
    return loudness


def scatter_about(own_key, shape, deviation, most, cuts=(), kind=jnp.bfloat16):
    gain = block_levels(own_key, shape, cuts, -0.22, 0.18) if cuts else 1.0
    array = jax.random.normal(own_key, shape, jnp.float32) * deviation * gain
    return jnp.minimum(jnp.maximum(array, -most), most).astype(kind)


def setup_inputs(seed: int = 0) -> dict:
    key_list = jax.random.split(jax.random.key(seed), 22)
    frames = scatter_about(key_list[0], (ROW_TOTAL, ROW_FRAMES, MODEL_WIDTH), 1.0, 6.0, ((0, 8), (1, 4)))
    output_gradient = scatter_about(key_list[1], (ROW_TOTAL, ROW_FRAMES, MODEL_WIDTH), 1.0, 6.0, ((0, 8), (1, 4)))
    segments = draw_segments(jax.random.fold_in(key_list[21], 71), 0)
    layer_keep = draw_layer_keep(jax.random.fold_in(key_list[21], 71), 0)
    conv_weight = scatter_about(key_list[4], (KW, MODEL_WIDTH, GROUP_CHANNELS), (GROUP_CHANNELS * KW) ** -0.5, 0.078125)
    convolution_bias = scatter_about(key_list[5], (MODEL_WIDTH,), 0.5, 3.0, (), jnp.float32)
    query_matrix = scatter_about(key_list[6], (MODEL_WIDTH, MODEL_WIDTH), MODEL_WIDTH ** -0.5, 0.21875)
    query_offset_bias = scatter_about(key_list[7], (MODEL_WIDTH,), 0.5, 3.0, (), jnp.float32)
    key_matrix = scatter_about(key_list[8], (MODEL_WIDTH, MODEL_WIDTH), MODEL_WIDTH ** -0.5, 0.21875)
    value_matrix = scatter_about(key_list[9], (MODEL_WIDTH, MODEL_WIDTH), MODEL_WIDTH ** -0.5, 0.21875)
    value_offset_bias = scatter_about(key_list[10], (MODEL_WIDTH,), 0.5, 3.0, (), jnp.float32)
    attn_weight = scatter_about(key_list[11], (MODEL_WIDTH, MODEL_WIDTH), (MODEL_WIDTH // 16) ** -0.5, 0.875)
    attn_bias = scatter_about(key_list[12], (MODEL_WIDTH,), 0.3, 2.0, (), jnp.float32)
    first_gain = jnp.clip(1.0 + 0.15 * jax.random.normal(key_list[13], (MODEL_WIDTH,), jnp.float32), 0.25, 1.75)
    first_shift = scatter_about(key_list[14], (MODEL_WIDTH,), 0.3, 2.0, (), jnp.float32)
    inner_weight = scatter_about(key_list[15], (MODEL_WIDTH, FF), MODEL_WIDTH ** -0.5, 0.21875)
    inner_bias = scatter_about(key_list[16], (FF,), 0.3, 2.0, (), jnp.float32)
    outer_weight = scatter_about(key_list[17], (FF, MODEL_WIDTH), FF ** -0.5, 0.109375)
    outer_bias = scatter_about(key_list[18], (MODEL_WIDTH,), 0.3, 2.0, (), jnp.float32)
    second_gain = jnp.clip(1.0 + 0.15 * jax.random.normal(key_list[19], (MODEL_WIDTH,), jnp.float32), 0.25, 1.75)
    second_shift = scatter_about(key_list[20], (MODEL_WIDTH,), 0.3, 2.0, (), jnp.float32)
    return {"frames": frames, "output_gradient": output_gradient, "segments": segments, "layer_keep": layer_keep, "conv_weight": conv_weight, "convolution_bias": convolution_bias, "query_matrix": query_matrix, "query_offset_bias": query_offset_bias, "key_matrix": key_matrix, "value_matrix": value_matrix, "value_offset_bias": value_offset_bias, "attn_weight": attn_weight, "attn_bias": attn_bias, "first_gain": first_gain, "first_shift": first_shift, "inner_weight": inner_weight, "inner_bias": inner_bias, "outer_weight": outer_weight, "outer_bias": outer_bias, "second_gain": second_gain, "second_shift": second_shift}


@jax.custom_vjp
def lowered_value(v):
    return lax.optimization_barrier(v.astype(jnp.bfloat16)).astype(jnp.float32)

@jax.custom_vjp
def lowered_gradient(v):
    return v

def low_keep(v):
    return (lowered_value(v), None)

def low_pass(kept, grad):
    return (grad,)

def back_keep(v):
    return (v, None)

def back_low(kept, grad):
    return (lowered_value(grad),)
lowered_value.defvjp(low_keep, low_pass)
lowered_gradient.defvjp(back_keep, back_low)
highest_precision = lax.Precision.HIGHEST
neg_big = -1e+30

def matrix_product(left_side, right_side):
    return jnp.dot(left_side, right_side, precision=highest_precision, preferred_element_type=jnp.float32)

def layer_norm(hidden):
    centred = hidden - lax.optimization_barrier(jnp.mean(hidden, axis=-1, keepdims=True))
    return centred * lax.rsqrt(lax.optimization_barrier(jnp.mean(centred * centred, axis=-1, keepdims=True)) + 1e-05)

def gelu_exact(entries):
    return jax.nn.gelu(entries, approximate=False)

def row_forward(params, row_frames, row_segment, keep_flag):
    conv_weight, convolution_bias, query_matrix, query_offset_bias, key_matrix, value_matrix, value_offset_bias, attn_weight, attn_bias, first_gain, first_shift, inner_weight, inner_bias, outer_weight, outer_bias, second_gain, second_shift = params
    active_mask = row_segment > 0
    masked = jnp.where(active_mask[:, None], row_frames, 0.0)
    half_kernel = KW // 2
    padded_frames = jnp.pad(masked, ((half_kernel, half_kernel), (0, 0)))
    segment_padded = jnp.pad(row_segment, (half_kernel, half_kernel))
    grouped = conv_weight.reshape(KW, CONV_GROUP_COUNT, GROUP_CHANNELS, GROUP_CHANNELS)
    kernel_tap_block = min(16, KW)
    convolution_total = jnp.zeros((ROW_FRAMES, CONV_GROUP_COUNT, GROUP_CHANNELS), jnp.float32)
    for block_index in range(KW // kernel_tap_block):
        sliding_windows = []
        for kernel_tap_index in range(block_index * kernel_tap_block, (block_index + 1) * kernel_tap_block):
            same_segment = (segment_padded[kernel_tap_index:kernel_tap_index + ROW_FRAMES] == row_segment) & active_mask
            sliding_windows.append(jnp.where(same_segment[:, None], padded_frames[kernel_tap_index:kernel_tap_index + ROW_FRAMES], 0.0))
        stacked_arrays = jnp.stack(sliding_windows, 0).reshape(kernel_tap_block, ROW_FRAMES, CONV_GROUP_COUNT, GROUP_CHANNELS)
        convolution_total = convolution_total + jnp.einsum('ktgi,kgio->tgo', stacked_arrays, grouped[block_index * kernel_tap_block:(block_index + 1) * kernel_tap_block], precision=highest_precision)
    convolution_before = lowered_gradient(convolution_total.reshape(ROW_FRAMES, MODEL_WIDTH) + convolution_bias)
    pos_out = masked + gelu_exact(convolution_before)
    position_lowered = lowered_value(pos_out)
    projected_queries = lowered_value(lowered_gradient(matrix_product(position_lowered, query_matrix) + query_offset_bias)).reshape(ROW_FRAMES, ATTENTION_HEADS, HEAD_SIZE)
    projected_keys = lowered_value(lowered_gradient(matrix_product(position_lowered, key_matrix))).reshape(ROW_FRAMES, ATTENTION_HEADS, HEAD_SIZE)
    projected_values = lowered_value(lowered_gradient(matrix_product(position_lowered, value_matrix) + value_offset_bias)).reshape(ROW_FRAMES, ATTENTION_HEADS, HEAD_SIZE)
    scores = lowered_gradient(jnp.einsum('qhd,khd->hqk', projected_queries, projected_keys, precision=highest_precision) * HEAD_SIZE ** (-0.5))
    allowed = (row_segment[:, None] == row_segment[None, :]) & active_mask[:, None]
    masked_scores = jnp.where(allowed[None], scores, neg_big)
    row_max = lax.optimization_barrier(jnp.max(masked_scores, axis=-1, keepdims=True))
    exp_scores = jnp.where(allowed[None], jnp.exp(masked_scores - row_max), 0.0)
    probabilities = exp_scores / jnp.maximum(lax.optimization_barrier(jnp.sum(exp_scores, axis=-1, keepdims=True)), 1.0)
    attended_output = jnp.einsum('ugo,ouf->guf', lowered_value(probabilities), projected_values, precision=highest_precision).reshape(ROW_FRAMES, MODEL_WIDTH)
    attn_low = lowered_value(lowered_gradient(attended_output))
    attn_out = lowered_gradient(matrix_product(attn_low, attn_weight) + attn_bias)
    first_out = layer_norm(pos_out + attn_out) * first_gain + first_shift
    first_low = lowered_value(first_out)
    inner_pre = lowered_gradient(matrix_product(first_low, inner_weight) + inner_bias)
    inner_low = lowered_value(gelu_exact(inner_pre))
    outer_out = lowered_gradient(matrix_product(inner_low, outer_weight) + outer_bias)
    second_out = layer_norm(first_out + outer_out) * second_gain + second_shift
    return keep_flag * second_out + (1.0 - keep_flag) * pos_out

def reference(frames, output_gradient, segments, layer_keep, conv_weight, convolution_bias, query_matrix, query_offset_bias, key_matrix, value_matrix, value_offset_bias, attn_weight, attn_bias, first_gain, first_shift, inner_weight, inner_bias, outer_weight, outer_bias, second_gain, second_shift):
    keep_flags = (layer_keep > 0).astype(jnp.float32)
    params = (conv_weight.astype(jnp.float32), convolution_bias.astype(jnp.float32), query_matrix.astype(jnp.float32), query_offset_bias.astype(jnp.float32), key_matrix.astype(jnp.float32), value_matrix.astype(jnp.float32), value_offset_bias.astype(jnp.float32), attn_weight.astype(jnp.float32), attn_bias.astype(jnp.float32), first_gain.astype(jnp.float32), first_shift.astype(jnp.float32), inner_weight.astype(jnp.float32), inner_bias.astype(jnp.float32), outer_weight.astype(jnp.float32), outer_bias.astype(jnp.float32), second_gain.astype(jnp.float32), second_shift.astype(jnp.float32))

    def forward(frames_float, weights):

        def one_row(row_triple):
            return jax.checkpoint(row_forward)(weights, row_triple[0], row_triple[1], row_triple[2])
        return lax.map(one_row, (frames_float, segments, keep_flags))
    result, pull_back = jax.vjp(forward, frames.astype(jnp.float32), params)
    frames_grad, weight_grads = pull_back(output_gradient.astype(jnp.float32))
    conv_weight_grad, conv_bias_grad, query_weight_grad, query_bias_grad, key_weight_grad, value_weight_grad, value_bias_grad, attn_weight_grad, attn_bias_grad, first_gain_grad, first_shift_grad, inner_weight_grad, inner_bias_grad, outer_weight_grad, outer_bias_grad, second_gain_grad, second_shift_grad = weight_grads
    return (result.astype(jnp.bfloat16), frames_grad.astype(jnp.bfloat16), conv_weight_grad, conv_bias_grad, query_weight_grad, query_bias_grad, key_weight_grad, value_weight_grad, value_bias_grad, attn_weight_grad, attn_bias_grad, first_gain_grad, first_shift_grad, inner_weight_grad, inner_bias_grad, outer_weight_grad, outer_bias_grad, second_gain_grad, second_shift_grad)
```

```python
import functools
import jax
import jax.numpy as jnp
from jax import lax
from jax.experimental import pallas as pl
from jax.experimental.pallas import tpu as pltpu
from jax.sharding import PartitionSpec as P


DK = 16

def prep_kernel(w_ref, wn_ref, wt_ref):
    gw = w_ref.shape[1]
    nb = w_ref.shape[0] // DK
    parts = [w_ref[DK*b:DK*(b+1)].reshape(DK*gw, gw) for b in range(nb)]
    wn = jnp.concatenate(parts, axis=1)
    wn_ref[0] = wn
    wt_ref[0] = wn.T

def prep(w):
    k, width, gw = w.shape
    g = width // gw
    nb = k // DK
    return pl.pallas_call(
        prep_kernel,
        grid=(g,),
        in_specs=[pl.BlockSpec((k, gw, gw), lambda i: (0, i, 0))],
        out_specs=[pl.BlockSpec((1, DK*gw, nb*gw), lambda i: (i, 0, 0)),
                   pl.BlockSpec((1, nb*gw, DK*gw), lambda i: (i, 0, 0))],
        out_shape=[jax.ShapeDtypeStruct((g, DK*gw, nb*gw), w.dtype),
                   jax.ShapeDtypeStruct((g, nb*gw, DK*gw), w.dtype)],
        name="prep",
    )(w)

def conv_kernel(xt_ref, wt_ref, sel_ref, out_ref, a0_ref, z_ref, *, nb, gw, F, nbound, roll32):
    tin = xt_ref.shape[1]
    x = xt_ref[...]
    if roll32:
        x = x.astype(jnp.float32)
    for dk in range(DK):
        r = x if dk == 0 else pltpu.roll(x, tin - dk, 1)
        a0_ref[gw*dk:gw*(dk+1), :] = r.astype(a0_ref.dtype)
    z_ref[...] = jnp.dot(wt_ref[0], a0_ref[...], preferred_element_type=jnp.float32)
    acc = z_ref[0:gw, :]
    for b in range(1, nb):
        acc = acc + pltpu.roll(z_ref[gw*b:gw*(b+1), :], tin - DK*b, 1)
    out = acc[:, :F]
    for n in range(1, nbound+1):
        sh = pltpu.roll(acc, tin - 64*n, 1)[:, :F]
        out = jnp.where(sel_ref[n:n+1, :] > 0, sh, out)
    out_ref[...] = out

def conv(xt, wt, sel, F, roll32=False):
    width, tin = xt.shape
    g, nbgw, dkgw = wt.shape
    gw = width // g
    nb = nbgw // gw
    nbound = sel.shape[0] - 1
    return pl.pallas_call(
        functools.partial(conv_kernel, nb=nb, gw=gw, F=F, nbound=nbound, roll32=roll32),
        grid=(g,),
        in_specs=[pl.BlockSpec((gw, tin), lambda i: (i, 0)),
                  pl.BlockSpec((1, nbgw, dkgw), lambda i: (i, 0, 0)),
                  pl.BlockSpec(sel.shape, lambda i: (0, 0))],
        out_specs=pl.BlockSpec((gw, F), lambda i: (i, 0)),
        out_shape=jax.ShapeDtypeStruct((width, F), jnp.float32),
        scratch_shapes=[pltpu.VMEM((dkgw, tin), jnp.bfloat16), pltpu.VMEM((nbgw, tin), jnp.float32)],
        name="conv_fwd",
    )(xt, wt, sel)

def dx_kernel(dt_ref, wn_ref, sel_ref, out_ref, ds_ref, y_ref, *, nb, gw, F, nbound, roll32):
    tin = dt_ref.shape[1]
    d = dt_ref[...]
    if roll32:
        d = d.astype(jnp.float32)
    for b in range(nb):
        r = d if b == 0 else pltpu.roll(d, DK*b, 1)
        ds_ref[gw*b:gw*(b+1), :] = r.astype(ds_ref.dtype)
    y_ref[...] = jnp.dot(wn_ref[0], ds_ref[...], preferred_element_type=jnp.float32)
    acc = y_ref[0:gw, :]
    for dk in range(1, DK):
        acc = acc + pltpu.roll(y_ref[gw*dk:gw*(dk+1), :], dk, 1)
    acc = acc[:, 128:]
    out = acc[:, :F]
    for n in range(1, nbound+1):
        sh = pltpu.roll(acc, acc.shape[1] - 64*n, 1)[:, :F]
        out = jnp.where(sel_ref[n:n+1, :] > 0, sh, out)
    out_ref[...] = out

def conv_dx(dt, wn, sel, F, roll32=False):
    width, tin = dt.shape
    g, dkgw, nbgw = wn.shape
    gw = width // g
    nb = nbgw // gw
    nbound = sel.shape[0] - 1
    return pl.pallas_call(
        functools.partial(dx_kernel, nb=nb, gw=gw, F=F, nbound=nbound, roll32=roll32),
        grid=(g,),
        in_specs=[pl.BlockSpec((gw, tin), lambda i: (i, 0)),
                  pl.BlockSpec((1, dkgw, nbgw), lambda i: (i, 0, 0)),
                  pl.BlockSpec(sel.shape, lambda i: (0, 0))],
        out_specs=pl.BlockSpec((gw, F), lambda i: (i, 0)),
        out_shape=jax.ShapeDtypeStruct((width, F), jnp.float32),
        scratch_shapes=[pltpu.VMEM((nbgw, tin), jnp.bfloat16), pltpu.VMEM((dkgw, tin), jnp.float32)],
        name="conv_dx",
    )(dt, wn, sel)

def dw_kernel(xt_ref, dt_ref, out_ref, a0_ref, ds_ref, *, nb, gw, roll32):
    tin = xt_ref.shape[2]
    tout = dt_ref.shape[2]
    x = xt_ref[0]
    d = dt_ref[0]
    if roll32:
        x = x.astype(jnp.float32); d = d.astype(jnp.float32)
    d = jnp.concatenate([d, jnp.zeros((gw, tin - tout), d.dtype)], axis=1)
    for dk in range(DK):
        r = x if dk == 0 else pltpu.roll(x, tin - dk, 1)
        a0_ref[gw*dk:gw*(dk+1), :] = r.astype(a0_ref.dtype)
    for b in range(nb):
        r = d if b == 0 else pltpu.roll(d, DK*b, 1)
        ds_ref[gw*b:gw*(b+1), :] = r.astype(ds_ref.dtype)
    p = lax.dot_general(ds_ref[...], a0_ref[...], (((1,), (1,)), ((), ())), preferred_element_type=jnp.float32)
    first = pl.program_id(1) == 0
    @pl.when(first)
    def _():
        out_ref[0] = p
    @pl.when(jnp.logical_not(first))
    def _():
        out_ref[0] += p

def conv_dw(xt, dt, gw, nb, roll32=False):
    m, chans, tin = xt.shape
    tout = dt.shape[2]
    g = chans // gw
    return pl.pallas_call(
        functools.partial(dw_kernel, nb=nb, gw=gw, roll32=roll32),
        grid=(g, m),
        in_specs=[pl.BlockSpec((1, gw, tin), lambda i, j: (j, i, 0)),
                  pl.BlockSpec((1, gw, tout), lambda i, j: (j, i, 0))],
        out_specs=pl.BlockSpec((1, nb*gw, DK*gw), lambda i, j: (i, 0, 0)),
        out_shape=jax.ShapeDtypeStruct((g, nb*gw, DK*gw), jnp.float32),
        scratch_shapes=[pltpu.VMEM((DK*gw, tin), jnp.bfloat16), pltpu.VMEM((nb*gw, tin), jnp.bfloat16)],
        name="conv_dw",
    )(xt, dt)


def finish_kernel(p_ref, out_ref, e_ref, q_ref, *, nb, gw):
    dkgw = DK * gw

    @pl.when(pl.program_id(0) == 0)
    def _():
        row = lax.broadcasted_iota(jnp.int32, (dkgw, dkgw), 0)
        col = lax.broadcasted_iota(jnp.int32, (1, dkgw), 1)
        e_ref[...] = (row == (col % DK) * gw + col // DK).astype(e_ref.dtype)

    q_ref[...] = jnp.dot(p_ref[0], e_ref[...], preferred_element_type=jnp.float32)
    per = 128 // DK
    lane_block = lax.broadcasted_iota(jnp.int32, (gw, 128), 1) // DK
    for tile in range(dkgw // 128):
        outs = [None] * per
        for b in range(nb):
            piece = q_ref[gw*b:gw*(b+1), 128*tile:128*(tile+1)]
            for i in range(per):
                turn = (b - i) % per
                moved = piece if turn == 0 else pltpu.roll(piece, DK * turn, 1)
                outs[i] = moved if outs[i] is None else jnp.where(lane_block == b, moved, outs[i])
        for i in range(per):
            out_ref[tile * per + i] = outs[i]

def finish_dw(p, gw, nb):
    g = p.shape[0]
    assert nb * DK == 128
    out = pl.pallas_call(
        functools.partial(finish_kernel, nb=nb, gw=gw),
        grid=(g,),
        in_specs=[pl.BlockSpec((1, nb*gw, DK*gw), lambda i: (i, 0, 0))],
        out_specs=pl.BlockSpec((gw, gw, 128), lambda i: (i, 0, 0)),
        out_shape=jax.ShapeDtypeStruct((g*gw, gw, 128), jnp.float32),
        scratch_shapes=[pltpu.VMEM((DK*gw, DK*gw), jnp.bfloat16), pltpu.VMEM((nb*gw, DK*gw), jnp.float32)],
        name="finish_dw",
    )(p)
    return jnp.transpose(out, (2, 0, 1))

HEAD = 64

def nt(a, b):
    return lax.dot_general(a, b, (((1,), (1,)), ((), ())), preferred_element_type=jnp.float32)

def attn_fwd_kernel(*refs, P, chunk):
    q_ref, qc_ref, kc_ref = refs[:3]
    k_refs = refs[3:3+P]
    v_refs = refs[3+P:3+2*P]
    o_ref, lse_ref = refs[3+2*P:5+2*P]
    ka_ref, = refs[5+2*P:]
    F = q_ref.shape[0]
    low_k = lax.broadcasted_iota(jnp.int32, (F, 128), 1) < HEAD
    low_q = lax.broadcasted_iota(jnp.int32, (chunk, 128), 1) < HEAD
    for h in range(2):
        pick = low_k if h == 0 else jnp.logical_not(low_k)
        for p in range(P):
            ka_ref[h, p*F:(p+1)*F, :] = jnp.where(pick, k_refs[p][...], kc_ref[p*F:(p+1)*F, :])
    for c in range(F // chunk):
        rows = slice(c*chunk, (c+1)*chunk)
        q = q_ref[rows, :] * jnp.asarray(0.125, jnp.bfloat16)
        outs, lses = [], []
        for h in range(2):
            pick = low_q if h == 0 else jnp.logical_not(low_q)
            qa = jnp.where(pick, q, qc_ref[rows, :])
            s = nt(qa, ka_ref[h])
            m = jnp.maximum(jnp.max(s, axis=1, keepdims=True), -1e20)
            e = jnp.exp(s - m)
            l = jnp.maximum(jnp.sum(e, axis=1, keepdims=True), 1.0)
            pb = (e * (1.0 / l)).astype(jnp.bfloat16)
            o = sum(jnp.dot(pb[:, p*F:(p+1)*F], v_refs[p][...], preferred_element_type=jnp.float32) for p in range(P))
            outs.append(o)
            lses.append(m + jnp.log(l))
        o_ref[rows, :] = jnp.where(low_q, outs[0], outs[1]).astype(o_ref.dtype)
        lse_ref[rows, :] = jnp.where(low_q, lses[0], lses[1])

def attn_fwd(q, kvs, qc, kc, chunk=128):
    F, W = q.shape
    P = len(kvs)
    T = P * F
    npair = W // 128
    return pl.pallas_call(
        functools.partial(attn_fwd_kernel, P=P, chunk=min(chunk, F)),
        grid=(npair,),
        in_specs=[pl.BlockSpec((F, 128), lambda a: (0, a)),
                  pl.BlockSpec((F, 128), lambda a: (0, 0)),
                  pl.BlockSpec((T, 128), lambda a: (0, 0))]
                 + [pl.BlockSpec((F, 128), lambda a: (0, a))] * P
                 + [pl.BlockSpec((F, 128), lambda a, n=npair: (0, a + n))] * P,
        out_specs=[pl.BlockSpec((F, 128), lambda a: (0, a)), pl.BlockSpec((F, 128), lambda a: (0, a))],
        out_shape=[jax.ShapeDtypeStruct((F, W), jnp.bfloat16), jax.ShapeDtypeStruct((F, W), jnp.float32)],
        scratch_shapes=[pltpu.VMEM((2, T, 128), jnp.bfloat16)],
        name="attn_fwd",
    )(q, qc, kc, *kvs, *kvs)

def attn_bwd_kernel(*refs, P, chunk):
    q_ref, do_ref, o_ref, lse_ref, qc_ref, kc_ref = refs[:6]
    k_refs = refs[6:6+P]
    v_refs = refs[6+P:6+2*P]
    dq_ref = refs[6+2*P]
    dk_refs = refs[7+2*P:7+3*P]
    dv_refs = refs[7+3*P:7+4*P]
    F = q_ref.shape[0]
    low_q = lax.broadcasted_iota(jnp.int32, (F, 128), 1) < HEAD
    low_c = lax.broadcasted_iota(jnp.int32, (chunk, 128), 1) < HEAD
    q = q_ref[...] * jnp.asarray(0.125, jnp.bfloat16)
    do = do_ref[...]
    lse_t = lse_ref[...].T
    prod_t = (do.astype(jnp.float32) * o_ref[...].astype(jnp.float32)).T
    lse_row = [lse_t[h*HEAD:h*HEAD+1, :] for h in range(2)]
    delta_row = [jnp.sum(prod_t[h*HEAD:(h+1)*HEAD, :], axis=0, keepdims=True) for h in range(2)]
    qa = [jnp.where(low_q if h == 0 else jnp.logical_not(low_q), q, qc_ref[...]) for h in range(2)]
    zero = jnp.zeros((), jnp.bfloat16)
    dqt = [jnp.zeros((HEAD, F), jnp.float32) for _ in range(2)]
    for p in range(P):
        for c in range(F // chunk):
            rows = slice(c*chunk, (c+1)*chunk)
            k = k_refs[p][rows, :]
            v = v_refs[p][rows, :]
            kc = kc_ref[p*F + c*chunk: p*F + (c+1)*chunk, :]
            kt = k.T
            dks, dvs = [], []
            for h in range(2):
                pick = low_c if h == 0 else jnp.logical_not(low_c)
                st = nt(jnp.where(pick, k, kc), qa[h])
                pt = jnp.exp(st - lse_row[h])
                dpt = nt(jnp.where(pick, v, zero), do)
                dst = (pt * (dpt - delta_row[h])).astype(jnp.bfloat16)
                dvs.append(jnp.dot(pt.astype(jnp.bfloat16), do, preferred_element_type=jnp.float32))
                dks.append(jnp.dot(dst, q, preferred_element_type=jnp.float32))
                dqt[h] = dqt[h] + jnp.dot(kt[h*HEAD:(h+1)*HEAD, :], dst, preferred_element_type=jnp.float32)
            dk_refs[p][rows, :] = jnp.where(low_c, dks[0], dks[1]).astype(dk_refs[p].dtype)
            dv_refs[p][rows, :] = jnp.where(low_c, dvs[0], dvs[1]).astype(dv_refs[p].dtype)
    dq = jnp.concatenate(dqt, axis=0).T * 0.125
    dq_ref[...] = dq.astype(dq_ref.dtype)

def attn_bwd(q, do, o, lse, kvs, qc, kc, chunk=128):
    F, W = q.shape
    P = len(kvs)
    T = P * F
    npair = W // 128
    own = pl.BlockSpec((F, 128), lambda a: (0, a))
    dts = [jnp.float32] + [jnp.bfloat16] * (P - 1)
    return pl.pallas_call(
        functools.partial(attn_bwd_kernel, P=P, chunk=min(chunk, F)),
        grid=(npair,),
        in_specs=[own, own, own, own,
                  pl.BlockSpec((F, 128), lambda a: (0, 0)),
                  pl.BlockSpec((T, 128), lambda a: (0, 0))]
                 + [own] * P
                 + [pl.BlockSpec((F, 128), lambda a, n=npair: (0, a + n))] * P,
        out_specs=[own] * (1 + 2*P),
        out_shape=[jax.ShapeDtypeStruct((F, W), jnp.bfloat16)] + [jax.ShapeDtypeStruct((F, W), t) for t in dts + dts],
        name="attn_bwd",
    )(q, do, o, lse, qc, kc, *kvs, *kvs)

HALO = 64
UTT_LEAST = 256
root_half = 0.7071067811865476
inv_root_two_pi = 0.3989422804014327
f32 = jnp.float32
bf16 = jnp.bfloat16


def layer_norm(hidden):
    centred = hidden - jnp.mean(hidden, axis=-1, keepdims=True)
    inv_scale = lax.rsqrt(jnp.mean(centred * centred, axis=-1, keepdims=True) + 1e-05)
    return (centred * inv_scale, inv_scale)


def norm_back(grad_normed, normed, inv_scale):
    return inv_scale * (
        grad_normed
        - jnp.mean(grad_normed, axis=-1, keepdims=True)
        - normed * jnp.mean(grad_normed * normed, axis=-1, keepdims=True)
    )


def gelu_slope(entries):
    return (
        0.5 * (1.0 + lax.erf(entries * root_half))
        + entries * jnp.exp(-0.5 * entries * entries) * inv_root_two_pi
    )


def mm(a, b):
    return jnp.dot(a, b, preferred_element_type=f32)


def mm_back(a, b):
    return lax.dot_general(a, b, (((1,), (1,)), ((), ())), preferred_element_type=f32)


def wgrad(a, b):
    return lax.dot_general(a, b, (((0,), (0,)), ((), ())), preferred_element_type=f32)


class Plan:
    def __init__(self, dp, seq, rows_dev):
        self.dp, self.seq, self.n = dp, seq, rows_dev
        self.q = seq // (2 * rows_dev)
        self.P = 2 * self.q
        assert dp % 2 == 0 and self.q * 2 * rows_dev == seq

    def out_pairs(self, m):
        pairs = []
        for d in range(self.dp):
            for z in range(self.seq):
                rho = self.n * (d % 2) + (z + m) % self.n
                u = z // self.n
                pairs.append((d * self.seq + z, self.member(d // 2, rho, u)))
        return pairs

    def member(self, e, rho, u):
        return (2 * e + u % 2) * self.seq + rho * self.q + u // 2

    def team_pairs(self, shift, wrap):
        pairs = []
        for e in range(self.dp // 2):
            for rho in range(2 * self.n):
                for u in range(self.P):
                    to = u + shift
                    if wrap or 0 <= to < self.P:
                        pairs.append((self.member(e, rho, u), self.member(e, rho, to % self.P)))
        return pairs


BOTH = ("dp", "seq")


def on_device(
    frames,
    output_gradient,
    segments,
    layer_keep,
    conv_weight,
    convolution_bias,
    query_matrix,
    query_offset_bias,
    key_matrix,
    value_matrix,
    value_offset_bias,
    attn_weight,
    attn_bias,
    first_gain,
    first_shift,
    inner_weight,
    inner_bias,
    outer_weight,
    outer_bias,
    second_gain,
    second_shift,
):
    rows_dev, local_len, width = frames.shape
    total_rows, row_len = segments.shape
    dp_count, seq_count = lax.axis_size("dp"), lax.axis_size("seq")
    dp_index, seq_index = lax.axis_index("dp"), lax.axis_index("seq")
    plan = Plan(dp_count, seq_count, rows_dev)
    n, q, team = plan.n, plan.q, plan.P
    F = row_len // team
    taps, _, gw = conv_weight.shape
    tap_blocks = taps // DK
    rho = seq_index // q
    member = (seq_index % q) * 2 + dp_index % 2
    row_id = (dp_index // 2) * (2 * n) + rho

    def to_team(a):
        got = []
        for m in range(n):
            sent = lax.dynamic_index_in_dim(a, (seq_index + m) % n, 0, keepdims=False)
            got.append(lax.ppermute(sent, BOTH, plan.out_pairs(m)))
        j = rho % n
        parts = []
        for w in range(n):
            part = got[0]
            for m in range(1, n):
                part = jnp.where((j - m) % n == w, got[m], part)
            parts.append(part)
        return jnp.concatenate(parts, 0)

    def from_team(a):
        blocks = a.reshape(n, local_len, width)
        j = rho % n
        back = []
        for m in range(n):
            sent = lax.dynamic_index_in_dim(blocks, (j - m) % n, 0, keepdims=False)
            back.append(
                lax.ppermute(sent, BOTH, [(t, s) for s, t in plan.out_pairs(m)])
            )
        parts = []
        for row in range(n):
            part = back[0]
            for m in range(1, n):
                part = jnp.where((seq_index + m) % n == row, back[m], part)
            parts.append(part)
        return jnp.stack(parts, 0)

    def with_halo(a):
        low = lax.ppermute(a[F - HALO :], BOTH, plan.team_pairs(1, False))
        high = lax.ppermute(a[:HALO], BOTH, plan.team_pairs(-1, False))
        return jnp.concatenate([low, a, high], 0)

    weight_nat, weight_tr = prep(conv_weight)

    x = to_team(frames)
    grad_out = to_team(output_gradient)

    seg_row = lax.dynamic_index_in_dim(segments, row_id, 0, keepdims=False)
    keep = (lax.dynamic_index_in_dim(layer_keep, row_id, 0, keepdims=False) > 0).astype(f32)
    ordinal = jnp.where(seg_row > 0, seg_row, jnp.max(seg_row) + 1)
    padded = jnp.pad(jnp.stack([seg_row, ordinal]), ((0, 0), (HALO, HALO)))
    around = lax.dynamic_slice_in_dim(padded, member * F, F + 2 * HALO, 1)
    seg_ext, ord_ext = around[0], around[1]
    seg_loc = seg_ext[HALO : HALO + F]
    ord_loc = ord_ext[HALO : HALO + F]
    live = seg_loc > 0
    gaps = 1 + max(F - 2, 0) // UTT_LEAST
    spread = -(-(F + 2 * HALO + HALO * gaps) // 128) * 128
    out_spread = -(-(F + HALO * gaps) // 128) * 128
    before_loc = ord_loc - ord_loc[0]
    before_ext = jnp.concatenate(
        [
            jnp.where(ord_ext[:HALO] == ord_loc[0], 0, -1),
            before_loc,
            jnp.where(ord_ext[HALO + F :] == ord_loc[F - 1], before_loc[F - 1], -1),
        ]
    )
    select = jnp.stack([(before_loc == k).astype(f32) for k in range(gaps + 1)])

    def pull_apart(a, before, length):
        total = None
        for k in range(gaps + 1):
            tail = length - a.shape[0] - HALO * k
            rows = jnp.pad(a, ((HALO * k, max(tail, 0)), (0, 0)))[:length]
            here = jnp.pad(
                before, (HALO * k, max(tail, 0)), constant_values=-1
            )[:length] == k
            total = jnp.where(here[:, None], rows, 0 if total is None else total)
        return total

    masked_frames = jnp.where(live[:, None], x, jnp.zeros((), x.dtype))
    spread_x = pull_apart(with_halo(masked_frames), before_ext, spread).T
    conv_t = conv(spread_x, weight_tr, select, F)
    x_shares = lax.all_to_all(
        spread_x.reshape(dp_count, width // dp_count, spread), "dp", 0, 0, tiled=True
    )

    conv_before = conv_t.T + convolution_bias
    pos_out = masked_frames.astype(f32) + jax.nn.gelu(conv_before, approximate=False)
    pos_low = pos_out.astype(bf16)
    kv = jnp.concatenate(
        [mm(pos_low, key_matrix), mm(pos_low, value_matrix) + value_offset_bias], 1
    ).astype(bf16)
    kvs = [kv] + [lax.ppermute(kv, BOTH, plan.team_pairs(s, True)) for s in range(1, team)]
    query = (mm(pos_low, query_matrix) + query_offset_bias).astype(bf16)
    seg_blocks = [
        lax.dynamic_slice_in_dim(seg_row, ((member - s) % team) * F, F, 0) for s in range(team)
    ]
    seg_keys = jnp.concatenate(seg_blocks, 0)
    classes = jnp.arange(128, dtype=jnp.int32) % HEAD
    q_codes = (seg_loc[:, None] == classes).astype(bf16)
    k_codes = jnp.where(
        (seg_keys[:, None] == classes) & (classes > 0), 0.0, -1e30
    ).astype(bf16)
    attn_low, lse = attn_fwd(query, kvs, q_codes, k_codes, 256)

    attn_out = mm(attn_low, attn_weight) + attn_bias
    first_normed, first_scale = layer_norm(pos_out + attn_out)
    first_out = first_normed * first_gain + first_shift
    first_low = first_out.astype(bf16)
    inner_pre = mm(first_low, inner_weight) + inner_bias
    inner_low = jax.nn.gelu(inner_pre, approximate=False).astype(bf16)
    outer_out = mm(inner_low, outer_weight) + outer_bias
    second_normed, second_scale = layer_norm(first_out + outer_out)
    second_out = second_normed * second_gain + second_shift
    layer_out = from_team((keep * second_out + (1.0 - keep) * pos_out).astype(bf16))

    grad_win = grad_out.astype(f32)
    grad_layer = keep * grad_win
    grad_second_gain = jnp.sum(grad_layer * second_normed, 0)
    grad_second_shift = jnp.sum(grad_layer, 0)
    grad_second_sum = norm_back(grad_layer * second_gain, second_normed, second_scale)
    grad_outer_low = grad_second_sum.astype(bf16)
    grad_outer_bias = jnp.sum(grad_outer_low.astype(f32), 0)
    grad_outer_t = wgrad(grad_outer_low, inner_low).astype(bf16)
    grad_inner_low = (mm_back(grad_outer_low, outer_weight) * gelu_slope(inner_pre)).astype(bf16)
    grad_inner_bias = jnp.sum(grad_inner_low.astype(f32), 0)
    grad_inner_t = wgrad(grad_inner_low, first_low).astype(bf16)
    grad_first_out = grad_second_sum + mm_back(grad_inner_low, inner_weight)
    grad_first_gain = jnp.sum(grad_first_out * first_normed, 0)
    grad_first_shift = jnp.sum(grad_first_out, 0)
    grad_first_sum = norm_back(grad_first_out * first_gain, first_normed, first_scale)
    grad_attn_low = grad_first_sum.astype(bf16)
    grad_attn_bias = jnp.sum(grad_attn_low.astype(f32), 0)
    grad_attn_t = wgrad(grad_attn_low, attn_low).astype(bf16)
    grad_heads = mm_back(grad_attn_low, attn_weight).astype(bf16)

    grads = attn_bwd(query, grad_heads, attn_low, lse, kvs, q_codes, k_codes, 256)
    grad_query_low = grads[0]
    key_sum, value_sum = grads[1], grads[1 + team]
    for s in range(1, team):
        back = plan.team_pairs(-s, True)
        key_sum = key_sum + lax.ppermute(grads[1 + s], BOTH, back).astype(f32)
        value_sum = value_sum + lax.ppermute(grads[1 + team + s], BOTH, back).astype(f32)
    grad_key_low, grad_value_low = key_sum.astype(bf16), value_sum.astype(bf16)
    grad_query_bias = jnp.sum(grad_query_low.astype(f32), 0)
    grad_value_bias = jnp.sum(grad_value_low.astype(f32), 0)
    grad_query_t = wgrad(grad_query_low, pos_low).astype(bf16)
    grad_key_t = wgrad(grad_key_low, pos_low).astype(bf16)
    grad_value_t = wgrad(grad_value_low, pos_low).astype(bf16)
    grad_pos = (
        grad_first_sum
        + (1.0 - keep) * grad_win
        + mm_back(grad_query_low, query_matrix)
        + mm_back(grad_key_low, key_matrix)
        + mm_back(grad_value_low, value_matrix)
    )
    grad_conv_low = (grad_pos * gelu_slope(conv_before)).astype(bf16)
    grad_conv_bias = jnp.sum(grad_conv_low.astype(f32), 0)

    d_shares = lax.all_to_all(
        pull_apart(grad_conv_low, before_loc, out_spread).T.reshape(
            dp_count, width // dp_count, out_spread
        ),
        "dp", 0, 0, tiled=True,
    )
    spread_d = pull_apart(with_halo(grad_conv_low), before_ext, spread).T
    conv_back = conv_dx(spread_d, weight_nat, select, F).T
    grad_input = from_team(jnp.where(live[:, None], grad_pos + conv_back, 0.0).astype(bf16))

    conv_part = conv_dw(x_shares, d_shares, gw, tap_blocks)
    conv_sum = lax.psum(conv_part.astype(bf16), "seq")
    grad_conv_weight = finish_dw(conv_sum, gw, tap_blocks)

    small = jnp.concatenate(
        [
            v.reshape(dp_count, -1)
            for v in (
                grad_inner_bias, grad_query_bias, grad_value_bias, grad_attn_bias, grad_first_gain,
                grad_first_shift, grad_outer_bias, grad_second_gain, grad_second_shift, grad_conv_bias,
            )
        ],
        1,
    ).astype(bf16)
    small = lax.psum(small, BOTH)
    small = lax.dynamic_index_in_dim(small, dp_index, 0, keepdims=False).astype(f32)
    share = width // dp_count
    ff_share = grad_inner_bias.shape[0] // dp_count
    inner_bias_share = small[:ff_share]
    vecs = [small[ff_share + share * i : ff_share + share * (i + 1)] for i in range(9)]

    def reduced(a):
        a = lax.psum_scatter(a, "dp", scatter_dimension=0, tiled=True)
        return lax.psum(a, "seq").astype(f32).T

    q_g, k_g, v_g, a_g, i_g, o_g = map(
        reduced,
        (grad_query_t, grad_key_t, grad_value_t, grad_attn_t, grad_inner_t, grad_outer_t),
    )
    return (
        layer_out,
        grad_input,
        grad_conv_weight,
        vecs[8],
        q_g,
        vecs[0],
        k_g,
        v_g,
        vecs[1],
        a_g,
        vecs[2],
        vecs[3],
        vecs[4],
        i_g,
        inner_bias_share,
        o_g,
        vecs[5],
        vecs[6],
        vecs[7],
    )


def solution(mesh):
    rows = P("dp", "seq", None)
    by_col, vec = P(None, "dp"), P("dp")
    out_specs = (
        rows, rows, P(None, "dp", None), vec, by_col, vec, by_col, by_col, vec, by_col, vec, vec,
        vec, by_col, vec, by_col, vec, vec, vec,
    )
    return jax.shard_map(
        on_device, mesh=mesh, in_specs=(rows, rows) + (P(),) * 19, out_specs=out_specs, check_vma=False
    )
```

```python
import functools
import jax
import jax.numpy as jnp
from jax import lax
from jax.experimental import pallas as pl
from jax.experimental.pallas import tpu as pltpu
from jax.sharding import PartitionSpec as P


DK = 16
ANY = pl.BlockSpec(memory_space=pl.ANY)

def prep_kernel(w_ref, wt_ref):
    gw = w_ref.shape[1]
    slots = w_ref.shape[2] // gw
    lane = lax.broadcasted_iota(jnp.int32, (gw, 128), 1)
    tiles = w_ref.shape[2] // 128
    for half in range(DK // slots):
        sums = [[None] * tiles for _ in range(slots)]
        for slot in range(slots):
            w = w_ref[half * slots + slot]
            for g in range(slots):
                turn = (slot - g) % slots
                moved = w if turn == 0 else pltpu.roll(w, gw * turn, 1)
                for t in range(tiles):
                    lo, hi = gw * slot - 128 * t, gw * (slot + 1) - 128 * t
                    if hi <= 0 or lo >= 128:
                        continue
                    part = moved[:, 128 * t : 128 * (t + 1)]
                    old = sums[g][t]
                    sums[g][t] = part if old is None else jnp.where(lane >= lo, part, old)
        for g in range(slots):
            for t in range(tiles):
                at = half * slots * gw + 128 * t
                wt_ref[g, :, at : at + 128] = sums[g][t]


def prep(w):
    k, width, gw = w.shape
    groups = width // gw
    nb = k // DK
    slots = 8
    assert (slots * gw) % 128 == 0 and DK % slots == 0 and groups % slots == 0
    return pl.pallas_call(
        prep_kernel,
        grid=(groups // slots, nb),
        in_specs=[pl.BlockSpec((DK, gw, slots * gw), lambda i, b: (b, 0, i))],
        out_specs=pl.BlockSpec((slots, gw, DK * gw), lambda i, b: (i, b, 0)),
        out_shape=jax.ShapeDtypeStruct((groups, nb * gw, DK * gw), w.dtype),
        cost_estimate=pl.CostEstimate(flops=10**9, bytes_accessed=2 * k * width * gw * 2, transcendentals=0),
        name="prep",
    )(jnp.transpose(w, (0, 2, 1)))

def conv_kernel(xt_ref, wt_ref, sel_ref, out_ref, a0_ref, z_ref, *, nb, gw, F, nbound):
    tin = xt_ref.shape[1]
    x = xt_ref[...]
    for dk in range(DK):
        r = x if dk == 0 else pltpu.roll(x, tin - dk, 1)
        a0_ref[gw*dk:gw*(dk+1), :] = r.astype(a0_ref.dtype)
    z_ref[...] = jnp.dot(wt_ref[0], a0_ref[...], preferred_element_type=jnp.float32)
    acc = z_ref[0:gw, :]
    for b in range(1, nb):
        acc = acc + pltpu.roll(z_ref[gw*b:gw*(b+1), :], tin - DK*b, 1)
    out = acc[:, :F]
    for n in range(1, nbound+1):
        sh = pltpu.roll(acc, tin - 64*n, 1)[:, :F]
        out = jnp.where(sel_ref[n:n+1, :] > 0, sh, out)
    out_ref[...] = out

def conv(xt, wt, sel, F, nbound):
    width, tin = xt.shape
    g, nbgw, dkgw = wt.shape
    gw = width // g
    nb = nbgw // gw
    return pl.pallas_call(
        functools.partial(conv_kernel, nb=nb, gw=gw, F=F, nbound=nbound),
        grid=(g,),
        in_specs=[pl.BlockSpec((gw, tin), lambda i: (i, 0)),
                  pl.BlockSpec((1, nbgw, dkgw), lambda i: (i, 0, 0)),
                  pl.BlockSpec(sel.shape, lambda i: (0, 0))],
        out_specs=pl.BlockSpec((gw, F), lambda i: (i, 0)),
        out_shape=jax.ShapeDtypeStruct((width, F), jnp.float32),
        scratch_shapes=[pltpu.VMEM((dkgw, tin), jnp.bfloat16), pltpu.VMEM((nbgw, tin), jnp.float32)],
        cost_estimate=pl.CostEstimate(flops=2 * g * nbgw * dkgw * tin, bytes_accessed=2 * g * nbgw * dkgw, transcendentals=0),
        name="conv_fwd",
    )(xt, wt, sel)

def dx_kernel(dt_ref, wt_ref, sel_ref, *refs, nb, gw, F, nbound):
    out_ref, ds_ref, y_ref = refs[-3:]
    tin = dt_ref.shape[1]
    d = dt_ref[...]
    for b in range(nb):
        r = d if b == 0 else pltpu.roll(d, DK*b, 1)
        ds_ref[gw*b:gw*(b+1), :] = r.astype(ds_ref.dtype)
    y_ref[...] = jnp.dot(wt_ref[0].T, ds_ref[...], preferred_element_type=jnp.float32)
    acc = y_ref[0:gw, :]
    for dk in range(1, DK):
        acc = acc + pltpu.roll(y_ref[gw*dk:gw*(dk+1), :], dk, 1)
    acc = acc[:, 128:]
    out = acc[:, :F]
    for n in range(1, nbound+1):
        sh = pltpu.roll(acc, acc.shape[1] - 64*n, 1)[:, :F]
        out = jnp.where(sel_ref[n:n+1, :] > 0, sh, out)
    out_ref[...] = out

def conv_dx(dt, wt, sel, F, nbound, first, count, deps):
    width, tin = dt.shape
    g, nbgw, dkgw = wt.shape
    gw = width // g
    nb = nbgw // gw
    return pl.pallas_call(
        functools.partial(dx_kernel, nb=nb, gw=gw, F=F, nbound=nbound),
        grid=(count,),
        in_specs=[pl.BlockSpec((gw, tin), lambda i: (i + first, 0)),
                  pl.BlockSpec((1, nbgw, dkgw), lambda i: (i + first, 0, 0)),
                  pl.BlockSpec(sel.shape, lambda i: (0, 0))] + [ANY] * len(deps),
        out_specs=pl.BlockSpec((gw, F), lambda i: (i, 0)),
        out_shape=jax.ShapeDtypeStruct((count * gw, F), jnp.float32),
        scratch_shapes=[pltpu.VMEM((nbgw, tin), jnp.bfloat16), pltpu.VMEM((dkgw, tin), jnp.float32)],
        cost_estimate=pl.CostEstimate(flops=2 * count * nbgw * dkgw * tin, bytes_accessed=2 * count * nbgw * dkgw, transcendentals=0),
        name="conv_dx",
    )(dt, wt, sel, *deps)

def dw_kernel(*refs, nb, gw, m):
    x_refs, d_refs = refs[:m], refs[m : 2 * m]
    out_ref, a0_ref, ds_ref = refs[-3:]
    tin = x_refs[0].shape[2]
    tout = d_refs[0].shape[2]
    ones = jnp.ones((16, tout), jnp.bfloat16)
    bias = None
    for s in range(m):
        x, d = x_refs[s][0], d_refs[s][0]
        part = lax.dot_general(ones, d, (((1,), (1,)), ((), ())), preferred_element_type=jnp.float32)
        bias = part if bias is None else bias + part
        d = jnp.concatenate([d, jnp.zeros((gw, tin - tout), d.dtype)], axis=1)
        slot = s % 2
        for dk in range(DK):
            a0_ref[slot, gw*dk:gw*(dk+1), :] = x if dk == 0 else pltpu.roll(x, tin - dk, 1)
        for b in range(nb):
            ds_ref[slot, gw*b:gw*(b+1), :] = d if b == 0 else pltpu.roll(d, DK*b, 1)
        p = lax.dot_general(
            ds_ref[slot], a0_ref[slot], (((1,), (1,)), ((), ())), preferred_element_type=jnp.float32
        )
        if s == 0:
            out_ref[: nb*gw, :] = p
        else:
            out_ref[: nb*gw, :] += p
    out_ref[nb*gw :, :] = jnp.zeros((out_ref.shape[0] - nb*gw, out_ref.shape[1]), jnp.float32)
    out_ref[nb*gw : nb*gw + 16, :gw] = bias


def conv_dw(xs, ds, group, gw, nb, deps):
    m, _, tin = xs.shape
    tout = ds.shape[2]
    rows = nb*gw + 32
    flops = 2 * m * nb*gw * DK*gw * tin
    return pl.pallas_call(
        functools.partial(dw_kernel, nb=nb, gw=gw, m=m),
        grid=(1,),
        in_specs=[pl.BlockSpec((1, gw, tin), lambda i, k=k: (k, group, 0)) for k in range(m)]
        + [pl.BlockSpec((1, gw, tout), lambda i, k=k: (k, group, 0)) for k in range(m)]
        + [ANY] * len(deps),
        out_specs=pl.BlockSpec((rows, DK*gw), lambda i: (0, 0)),
        scratch_shapes=[pltpu.VMEM((2, DK*gw, tin), jnp.bfloat16), pltpu.VMEM((2, nb*gw, tin), jnp.bfloat16)],
        out_shape=jax.ShapeDtypeStruct((rows, DK*gw), jnp.float32),
        cost_estimate=pl.CostEstimate(flops=flops, bytes_accessed=4 * rows * DK*gw, transcendentals=0),
        name="conv_dw",
    )(*([xs] * m), *([ds] * m), *deps)


def join_kernel(mine_ref, ks_ref, kk_ref, gs_ref, gk_ref, *refs):
    sent_ref, kept_ref = refs[-2:]
    sent_ref[...] = (ks_ref[...].astype(jnp.float32) + gs_ref[...].astype(jnp.float32)).astype(sent_ref.dtype)
    kept_ref[...] = (kk_ref[...].astype(jnp.float32) + gk_ref[...].astype(jnp.float32)).astype(kept_ref.dtype)


def join_split(kept, got, mine, high, low, deps):
    n, rows, cols = kept.shape

    def half(other):
        def at(i, mine_ref):
            side = 1 - mine_ref[0] if other else mine_ref[0]
            return ((i // low * 2 + side) * low + i % low, 0, 0)

        return pl.BlockSpec((1, rows, cols), at)

    out = pl.BlockSpec((1, rows, cols), lambda i, mine_ref: (i, 0, 0))
    shape = jax.ShapeDtypeStruct((n // 2, rows, cols), kept.dtype)
    return pl.pallas_call(
        join_kernel,
        grid_spec=pltpu.PrefetchScalarGridSpec(
            num_scalar_prefetch=1,
            grid=(n // 2,),
            in_specs=[half(True), half(False), half(True), half(False)] + [ANY] * len(deps),
            out_specs=[out, out],
        ),
        out_shape=[shape, shape],
        cost_estimate=pl.CostEstimate(flops=n * rows * cols, bytes_accessed=6 * n * rows * cols, transcendentals=0),
        name="join",
    )(mine, kept, kept, got, got, *deps)


def join_last_kernel(k_ref, g_ref, *refs):
    refs[-1][...] = (k_ref[...].astype(jnp.float32) + g_ref[...].astype(jnp.float32)).astype(refs[-1].dtype)


def join_last(kept, got, deps):
    whole = pl.BlockSpec(memory_space=pltpu.VMEM)
    return pl.pallas_call(
        join_last_kernel,
        in_specs=[whole, whole] + [ANY] * len(deps),
        out_specs=whole,
        out_shape=jax.ShapeDtypeStruct(kept.shape, kept.dtype),
        cost_estimate=pl.CostEstimate(flops=kept.size, bytes_accessed=6 * kept.size, transcendentals=0),
        name="join_last",
    )(kept, got, *deps).reshape(-1, kept.shape[-1])


def finish_kernel(p_ref, *refs, nb, gw):
    out_ref, e_ref, q_ref = refs[-3:]
    dkgw = DK * gw
    row = lax.broadcasted_iota(jnp.int32, (dkgw, dkgw), 0)
    col = lax.broadcasted_iota(jnp.int32, (1, dkgw), 1)
    e_ref[...] = (row == (col % DK) * gw + col // DK).astype(e_ref.dtype)
    per = 128 // DK
    lane_block = lax.broadcasted_iota(jnp.int32, (gw, 128), 1) // DK
    q_ref[...] = jnp.dot(
        p_ref[: nb * gw, :], e_ref[...], preferred_element_type=jnp.float32
    ).astype(q_ref.dtype)
    for tile in range(dkgw // 128):
        outs = [None] * per
        for b in range(nb):
            piece = q_ref[gw*b:gw*(b+1), 128*tile:128*(tile+1)]
            for i in range(per):
                turn = (b - i) % per
                moved = piece if turn == 0 else pltpu.roll(piece, DK * turn, 1)
                outs[i] = moved if outs[i] is None else jnp.where(lane_block == b, moved, outs[i])
        for i in range(per):
            out_ref[tile * per + i] = outs[i].astype(out_ref.dtype)


def finish_dw(ps, gw, nb):
    assert nb * DK == 128
    g = len(ps)
    out = None
    for k, p in enumerate(ps):
        given = [] if out is None else [out]
        out = pl.pallas_call(
            functools.partial(finish_kernel, nb=nb, gw=gw),
            grid=(1,),
            in_specs=[pl.BlockSpec(p.shape, lambda i: (0, 0))] + [ANY] * len(given),
            out_specs=pl.BlockSpec((gw, gw, 128), lambda i, k=k: (k, 0, 0)),
            out_shape=jax.ShapeDtypeStruct((g*gw, gw, 128), jnp.float32),
            scratch_shapes=[pltpu.VMEM((DK*gw, DK*gw), jnp.bfloat16), pltpu.VMEM((nb*gw, DK*gw), jnp.bfloat16)],
            input_output_aliases={1: 0} if given else {},
            name="finish_dw",
        )(p, *given)
    return jnp.transpose(out, (2, 0, 1))


def wg_rows_kernel(mine_ref, lhs_ref, rhs_ref, *refs, many, dp, nextra, ndeps):
    extra_refs = refs[:nextra]
    sent_ref, kept_ref, lt_ref, ls_ref, lk_ref = refs[nextra + ndeps :]
    half = many * dp // 2
    share = lhs_ref.shape[1] // (many * dp)
    cols = sent_ref.shape[2]
    mine = mine_ref[0]

    @pl.when(pl.program_id(0) == 0)
    def _():
        lt_ref[...] = lhs_ref[...].T
        for i in range(half):
            for to_ref, side in ((ls_ref, 1 - mine), (lk_ref, mine)):
                at = pl.multiple_of((2 * i + side) * share, 16)
                to_ref[i * share : (i + 1) * share, :] = lt_ref[pl.ds(at, share), :]

    for out_ref, l_ref in ((sent_ref, ls_ref), (kept_ref, lk_ref)):
        total = jnp.dot(l_ref[...], rhs_ref[...], preferred_element_type=jnp.float32)
        for i in range(half):
            out_ref[i, :share, :] = total[i * share : (i + 1) * share, :].astype(out_ref.dtype)
    if nextra:
        for m in range(many):
            rows = []
            for r in extra_refs:
                if many > 1:
                    rows.append(r[0:1, m * cols : (m + 1) * cols])
                else:
                    rows += [r[0:1, k * cols : (k + 1) * cols] for k in range(r.shape[1] // cols)]
            rows.append(jnp.zeros((16 - len(rows), cols), jnp.float32))
            block = jnp.concatenate(rows, 0).astype(jnp.bfloat16)
            for i in range(dp // 2):
                sent_ref[m * dp // 2 + i, share:, :] = block
                kept_ref[m * dp // 2 + i, share:, :] = block


def wg_rows(mine, lhs, rhs, many, dp, chunks, extras=(), deps=(), slots=None, first=0, into=()):
    F, M = lhs.shape
    N = rhs.shape[1]
    share = M // (many * dp)
    half = many * dp // 2
    rows = share + (16 if extras else 0)
    out = pl.BlockSpec((half, rows, N // chunks), lambda i, m: (first, 0, i))
    shape = jax.ShapeDtypeStruct((slots or half, rows, N), jnp.bfloat16)
    deps = tuple(into) + tuple(deps)
    at = 3 + len(extras)
    return pl.pallas_call(
        functools.partial(wg_rows_kernel, many=many, dp=dp, nextra=len(extras), ndeps=len(deps)),
        input_output_aliases={at: 0, at + 1: 1} if into else {},
        grid_spec=pltpu.PrefetchScalarGridSpec(
            num_scalar_prefetch=1,
            grid=(chunks,),
            in_specs=[
                pl.BlockSpec((F, M), lambda i, m: (0, 0)),
                pl.BlockSpec((F, N // chunks), lambda i, m: (0, i)),
            ]
            + [pl.BlockSpec(e.shape, lambda i, m: (0, 0)) for e in extras]
            + [ANY] * len(deps),
            out_specs=[out, out],
            scratch_shapes=[
                pltpu.VMEM((M, F), jnp.bfloat16),
                pltpu.VMEM((half * share, F), jnp.bfloat16),
                pltpu.VMEM((half * share, F), jnp.bfloat16),
            ],
        ),
        out_shape=[shape, shape],
        cost_estimate=pl.CostEstimate(flops=2 * F * M * N, bytes_accessed=2 * M * N, transcendentals=0),
        name="wg_rows",
    )(mine, lhs, rhs, *extras, *deps)


def wg_cols_kernel(mine_ref, lhs_ref, rhs_ref, *refs):
    sent_ref, kept_ref, lt_ref = refs[-3:]
    half = pl.num_programs(0) // 2

    @pl.when(pl.program_id(0) == 0)
    def _():
        lt_ref[...] = lhs_ref[...].T

    total = jnp.dot(lt_ref[...], rhs_ref[...], preferred_element_type=jnp.float32).astype(jnp.bfloat16)

    @pl.when(pl.program_id(0) < half)
    def _():
        sent_ref[0] = total

    @pl.when(pl.program_id(0) >= half)
    def _():
        kept_ref[0] = total


def wg_cols(mine, lhs, rhs, dp, deps=()):
    F, M = lhs.shape
    share = rhs.shape[1] // dp
    half = dp // 2

    def of(s, m):
        side = jnp.where(s < half, 1 - m[0], m[0])
        return (0, 2 * lax.rem(s, half) + side)

    shape = jax.ShapeDtypeStruct((half, M, share), jnp.bfloat16)
    return pl.pallas_call(
        wg_cols_kernel,
        grid_spec=pltpu.PrefetchScalarGridSpec(
            num_scalar_prefetch=1,
            grid=(dp,),
            in_specs=[pl.BlockSpec((F, M), lambda s, m: (0, 0)), pl.BlockSpec((F, share), of)]
            + [ANY] * len(deps),
            out_specs=[
                pl.BlockSpec((1, M, share), lambda s, m: (jnp.minimum(s, half - 1), 0, 0)),
                pl.BlockSpec((1, M, share), lambda s, m: (jnp.maximum(s - half, 0), 0, 0)),
            ],
            scratch_shapes=[pltpu.VMEM((M, F), jnp.bfloat16)],
        ),
        out_shape=[shape, shape],
        cost_estimate=pl.CostEstimate(flops=2 * F * M * share * dp, bytes_accessed=2 * M * share * dp, transcendentals=0),
        name="wg_cols",
    )(mine, lhs, rhs, *deps)


def dpos_kernel(keep_ref, *refs, parts, far, ndeps):
    qs, ks, vs = refs[:parts], refs[parts : 2 * parts], refs[2 * parts : 3 * parts]
    far_refs, refs = refs[3 * parts : (3 + far) * parts], refs[(3 + far) * parts :]
    wq_ref, wk_ref, wv_ref, first_ref, g_ref, conv_ref = refs[:6]
    low_ref, lowv_ref, pos_ref, d_ref, qk_ref, v_ref = refs[6 + ndeps :]
    dq = jnp.concatenate([r[...] for r in qs], 1)
    dks, dvs = [], []
    for p in range(parts):
        dk, dv = ks[p][...], vs[p][...]
        for r in far_refs[p * far : (p + 1) * far]:
            dk = dk + r[0].astype(jnp.float32)
            dv = dv + r[1].astype(jnp.float32)
        dks.append(dk.astype(jnp.bfloat16))
        dvs.append(dv.astype(jnp.bfloat16))
    dk, dv = jnp.concatenate(dks, 1), jnp.concatenate(dvs, 1)
    width = dq.shape[1]
    low_ref[:, :width] = dq
    low_ref[:, width:] = dk
    lowv_ref[...] = dv
    total = first_ref[...] + (1.0 - keep_ref[0]) * g_ref[...].astype(jnp.float32)
    for low, w_ref in ((dq, wq_ref), (dk, wk_ref), (dv, wv_ref)):
        total = total + lax.dot_general(
            low, w_ref[...], (((1,), (1,)), ((), ())), preferred_element_type=jnp.float32
        )
    pos_ref[...] = total
    d_ref[...] = (total * gelu_slope(conv_ref[...])).astype(d_ref.dtype)
    sums = [jnp.sum(low.astype(jnp.float32), 0, keepdims=True) for low in (dq, dk, dv)]

    @pl.when(pl.program_id(0) == 0)
    def _():
        qk_ref[...] = jnp.zeros_like(qk_ref)
        v_ref[...] = jnp.zeros_like(v_ref)

    qk_ref[0:1, :width] += sums[0]
    qk_ref[0:1, width:] += sums[1]
    v_ref[0:1, :] += sums[2]


def dpos(keep, dqs, dks, dvs, fars, wq, wk, wv, first, g, conv_before, deps):
    F, W = first.shape
    rows = min(256, F)
    parts = len(dqs)
    part = pl.BlockSpec((rows, W // parts), lambda i, k: (i, 0))
    block = pl.BlockSpec((rows, W), lambda i, k: (i, 0))
    whole = pl.BlockSpec((W, W), lambda i, k: (0, 0))
    return pl.pallas_call(
        functools.partial(dpos_kernel, parts=parts, far=len(fars[0]), ndeps=len(deps)),
        grid_spec=pltpu.PrefetchScalarGridSpec(
            num_scalar_prefetch=1,
            grid=(F // rows,),
            in_specs=[part] * (3 * parts)
            + [pl.BlockSpec((2, rows, W // parts), lambda i, k: (0, i, 0))] * (parts * len(fars[0]))
            + [whole] * 3 + [block] * 3 + [ANY] * len(deps),
            out_specs=[
                pl.BlockSpec((rows, 2 * W), lambda i, k: (i, 0)), block, block, block,
                pl.BlockSpec((8, 2 * W), lambda i, k: (0, 0)),
                pl.BlockSpec((8, W), lambda i, k: (0, 0)),
            ],
        ),
        out_shape=[
            jax.ShapeDtypeStruct((F, 2 * W), jnp.bfloat16),
            jax.ShapeDtypeStruct((F, W), jnp.bfloat16),
            jax.ShapeDtypeStruct((F, W), jnp.float32),
            jax.ShapeDtypeStruct((F, W), jnp.bfloat16),
            jax.ShapeDtypeStruct((8, 2 * W), jnp.float32),
            jax.ShapeDtypeStruct((8, W), jnp.float32),
        ],
        cost_estimate=pl.CostEstimate(flops=6 * F * W * W, bytes_accessed=20 * F * W + 6 * W * W, transcendentals=0),
        name="dpos",
    )(keep, *dqs, *dks, *dvs, *[f for part in fars for f in part], wq, wk, wv, first, g, conv_before, *deps)


def front_kernel(conv_ref, bias_ref, x_ref, wq_ref, wk_ref, wv_ref, bq_ref, bv_ref, *refs):
    cb_ref, pos_ref, low_ref, q_ref, kv_ref = refs[-5:]
    before = conv_ref[...].T + bias_ref[...]
    cb_ref[...] = before
    pos = x_ref[...].astype(jnp.float32) + gelu(before)
    pos_ref[...] = pos
    low = pos.astype(jnp.bfloat16)
    low_ref[...] = low
    width = low.shape[1]
    q_ref[...] = (jnp.dot(low, wq_ref[...], preferred_element_type=jnp.float32) + bq_ref[...]).astype(jnp.bfloat16)
    kv_ref[:, :width] = jnp.dot(low, wk_ref[...], preferred_element_type=jnp.float32).astype(jnp.bfloat16)
    kv_ref[:, width:] = (
        jnp.dot(low, wv_ref[...], preferred_element_type=jnp.float32) + bv_ref[...]
    ).astype(jnp.bfloat16)


def front(conv_t, bias, x, wq, wk, wv, bq, bv, deps):
    W, F = conv_t.shape
    rows = min(256, F)
    block = pl.BlockSpec((rows, W), lambda i: (i, 0))
    whole = pl.BlockSpec((W, W), lambda i: (0, 0))
    vec = pl.BlockSpec((1, W), lambda i: (0, 0))
    return pl.pallas_call(
        front_kernel,
        grid=(F // rows,),
        in_specs=[pl.BlockSpec((W, rows), lambda i: (0, i)), vec, block]
        + [whole] * 3 + [vec] * 2 + [ANY] * len(deps),
        out_specs=[block] * 4 + [pl.BlockSpec((rows, 2 * W), lambda i: (i, 0))],
        out_shape=[
            jax.ShapeDtypeStruct((F, W), jnp.float32),
            jax.ShapeDtypeStruct((F, W), jnp.float32),
            jax.ShapeDtypeStruct((F, W), jnp.bfloat16),
            jax.ShapeDtypeStruct((F, W), jnp.bfloat16),
            jax.ShapeDtypeStruct((F, 2 * W), jnp.bfloat16),
        ],
        cost_estimate=pl.CostEstimate(flops=6 * F * W * W, bytes_accessed=20 * F * W + 6 * W * W, transcendentals=0),
        name="front",
    )(conv_t, bias.reshape(1, W), x, wq, wk, wv, bq.reshape(1, W), bv.reshape(1, W), *deps)


def mid_kernel(keep_ref, attn_ref, pos_ref, g_ref, wa_ref, wi_ref, wo_ref, ba_ref, g1_ref, s1_ref, bi_ref, bo_ref, g2_ref, s2_ref, *refs, ndeps, chunk):
    (
        out_ref, first_ref, inner_ref, douter_ref, dinner_ref, dattn_ref, dfirst_ref, dheads_ref,
        inner_sum_ref, sums_ref, slope_ref,
    ) = refs[ndeps:]
    keep = keep_ref[0]
    width = pos_ref.shape[1]
    ff = wi_ref.shape[1]
    pos = pos_ref[...]
    attn_out = jnp.dot(attn_ref[...], wa_ref[...], preferred_element_type=jnp.float32) + ba_ref[...]
    first_normed, first_scale = layer_norm(pos + attn_out)
    first_out = first_normed * g1_ref[...] + s1_ref[...]
    first_low = first_out.astype(jnp.bfloat16)
    first_ref[...] = first_low
    total = None
    for c in range(0, ff, chunk):
        cols = slice(c, c + chunk)
        pre = jnp.dot(first_low, wi_ref[:, cols], preferred_element_type=jnp.float32) + bi_ref[:, cols]
        phi = 0.5 * (1.0 + lax.erf(pre * root_half))
        slope_ref[:, cols] = phi + pre * jnp.exp(-0.5 * pre * pre) * inv_root_two_pi
        low = (pre * phi).astype(jnp.bfloat16)
        inner_ref[:, cols] = low
        part = jnp.dot(low, wo_ref[cols, :], preferred_element_type=jnp.float32)
        total = part if total is None else total + part
    second_normed, second_scale = layer_norm(first_out + (total + bo_ref[...]))
    second_out = second_normed * g2_ref[...] + s2_ref[...]
    out_ref[...] = (keep * second_out + (1.0 - keep) * pos).astype(jnp.bfloat16)

    grad_layer = keep * g_ref[...].astype(jnp.float32)
    d_second = norm_back(grad_layer * g2_ref[...], second_normed, second_scale)
    d_outer = d_second.astype(jnp.bfloat16)
    douter_ref[...] = d_outer

    @pl.when(pl.program_id(0) == 0)
    def _():
        inner_sum_ref[...] = jnp.zeros_like(inner_sum_ref)
        sums_ref[...] = jnp.zeros_like(sums_ref)

    d_first_out = d_second
    for c in range(0, ff, chunk):
        cols = slice(c, c + chunk)
        d_inner = (
            lax.dot_general(d_outer, wo_ref[cols, :], (((1,), (1,)), ((), ())), preferred_element_type=jnp.float32)
            * slope_ref[:, cols]
        ).astype(jnp.bfloat16)
        dinner_ref[:, cols] = d_inner
        inner_sum_ref[0:1, cols] += jnp.sum(d_inner.astype(jnp.float32), 0, keepdims=True)
        d_first_out = d_first_out + lax.dot_general(
            d_inner, wi_ref[:, cols], (((1,), (1,)), ((), ())), preferred_element_type=jnp.float32
        )
    d_first = norm_back(d_first_out * g1_ref[...], first_normed, first_scale)
    dfirst_ref[...] = d_first
    d_attn = d_first.astype(jnp.bfloat16)
    dattn_ref[...] = d_attn
    dheads_ref[...] = lax.dot_general(
        d_attn, wa_ref[...], (((1,), (1,)), ((), ())), preferred_element_type=jnp.float32
    ).astype(jnp.bfloat16)
    for k, v in enumerate((
        d_attn.astype(jnp.float32), d_first_out * first_normed, d_first_out,
        d_outer.astype(jnp.float32), grad_layer * second_normed, grad_layer,
    )):
        sums_ref[0:1, k * width : (k + 1) * width] += jnp.sum(v, 0, keepdims=True)


def mid(keep, attn_low, pos_out, g, wa, wi, wo, ba, g1, s1, bi, bo, g2, s2, deps):
    F, W = pos_out.shape
    ff = wi.shape[1]
    rows = min(256, F)
    block = pl.BlockSpec((rows, W), lambda i, k: (i, 0))
    wide = pl.BlockSpec((rows, ff), lambda i, k: (i, 0))

    def whole(*shape):
        return pl.BlockSpec(shape, lambda i, k: (0,) * len(shape))

    vec = whole(1, W)
    out = lambda cols, kind: jax.ShapeDtypeStruct((F, cols), kind)
    bf, fl = jnp.bfloat16, jnp.float32
    return pl.pallas_call(
        functools.partial(mid_kernel, ndeps=len(deps), chunk=min(768, ff)),
        grid_spec=pltpu.PrefetchScalarGridSpec(
            num_scalar_prefetch=1,
            grid=(F // rows,),
            in_specs=[block, block, block, whole(W, W), whole(W, ff), whole(ff, W), vec, vec, vec, whole(1, ff), vec, vec, vec]
            + [ANY] * len(deps),
            out_specs=[block, block, wide, block, wide, block, block, block, whole(8, ff), whole(8, 6 * W)],
            scratch_shapes=[pltpu.VMEM((rows, ff), jnp.float32)],
        ),
        out_shape=[
            out(W, bf), out(W, bf), out(ff, bf), out(W, bf), out(ff, bf), out(W, bf), out(W, fl), out(W, bf),
            jax.ShapeDtypeStruct((8, ff), fl), jax.ShapeDtypeStruct((8, 6 * W), fl),
        ],
        cost_estimate=pl.CostEstimate(flops=8 * F * W * ff + 4 * F * W * W, bytes_accessed=16 * W * ff, transcendentals=0),
        name="mid",
    )(
        keep, attn_low, pos_out, g, wa, wi, wo, ba.reshape(1, W), g1.reshape(1, W), s1.reshape(1, W),
        bi.reshape(1, ff), bo.reshape(1, W), g2.reshape(1, W), s2.reshape(1, W), *deps,
    )


def place(ext, before, gaps, length):
    rows, have = ext.shape
    ext = jnp.concatenate([ext, jnp.zeros((rows, length - have), ext.dtype)], 1) if length > have else ext
    if length > have:
        before = jnp.concatenate([before, jnp.full((before.shape[0], length - have), -1, before.dtype)], 1)
    total = None
    for k in range(gaps + 1):
        moved = ext if k == 0 else pltpu.roll(ext, HALO * k, 1)
        here = (before if k == 0 else pltpu.roll(before, HALO * k, 1))[0:1, :] == k
        total = jnp.where(here, moved, jnp.zeros((), ext.dtype) if total is None else total)
    return total


def window_of(seg_ref, wide_ref, row, member, F):
    T = seg_ref.shape[1]
    wide_ref[...] = jnp.zeros_like(wide_ref)
    wide_ref[:, 128 : 128 + T] = jnp.broadcast_to(seg_ref[pl.ds(row % 8, 1), :], (8, T))
    start = pl.multiple_of(member * F, 128)
    window = wide_ref[:, pl.ds(start, F + 256)]
    return pltpu.roll(window, F + 256 - HALO, 1)[:, : F + 2 * HALO]


def ordinals(window, F):
    lane = lax.broadcasted_iota(jnp.int32, window.shape, 1)
    local = (lane >= HALO) & (lane < HALO + F)
    most = jnp.max(jnp.where(local, window, 0), axis=1, keepdims=True)
    first = jnp.sum(jnp.where(lane == HALO, window, 0), axis=1, keepdims=True)
    last = jnp.sum(jnp.where(lane == HALO + F - 1, window, 0), axis=1, keepdims=True)
    number = jnp.where(window > 0, window, most + 1)
    number_first = jnp.where(first > 0, first, most + 1)
    number_last = jnp.where(last > 0, last, most + 1)
    before = number - number_first
    before = jnp.where((lane < HALO) & (window != first), -1, before)
    right = jnp.where(window == last, number_last - number_first, -1)
    return jnp.where(lane >= HALO + F, right, before)


def column(row):
    return row.astype(jnp.float32).T[:, 0:1]


def build_x_kernel(at_ref, seg_ref, *refs, n, nlow, nhigh, team, F, gaps, spread):
    row, member = at_ref[0], at_ref[1]
    j = at_ref[2]
    got, lows, highs = refs[:n], refs[n : n + nlow], refs[n + nlow : n + nlow + nhigh]
    x_ref, spread_ref, sel_ref, qc_ref, kc_ref, wide_ref = refs[-6:]
    zero = jnp.zeros((), jnp.bfloat16)
    blocks = []
    for w in range(n):
        part = got[0][...]
        for m in range(1, n):
            part = jnp.where((j - w + n) % n == m, got[m][...], part)
        blocks.append(part)

    def edge(parts, on):
        part = parts[0][...]
        for m in range(1, len(parts)):
            part = jnp.where(j == m, parts[m][...], part)
        return jnp.where(on, part, zero)

    window = window_of(seg_ref, wide_ref, row, member, F)
    before = ordinals(window, F)
    ext = jnp.concatenate([edge(lows, member > 0)] + blocks + [edge(highs, member < team - 1)], 0)
    ext_t = jnp.where(window[0:1, :] > 0, ext.T, zero)
    spread_ref[...] = place(ext_t, before, gaps, spread)
    local = pltpu.roll(window, F + 2 * HALO - HALO, 1)[:, :F]
    before_local = pltpu.roll(before, F + 2 * HALO - HALO, 1)[:, :F]
    which = lax.broadcasted_iota(jnp.int32, (8, F), 0)
    sel_ref[...] = (before_local == which).astype(jnp.float32)
    seg_col = column(local)
    length = F // n
    for w in range(n):
        rows = slice(w * length, (w + 1) * length)
        x_ref[rows, :] = jnp.where(seg_col[rows] > 0, blocks[w], zero)
    lane = lax.broadcasted_iota(jnp.int32, (1, 128), 1) % 64
    qc_ref[...] = (seg_col == lane.astype(jnp.float32)).astype(jnp.bfloat16)
    for s in range(team):
        start = pl.multiple_of(128 + (member - s + team) % team * F, 128)
        keys = column(wide_ref[:, pl.ds(start, F)])
        kc_ref[s * F : (s + 1) * F, :] = jnp.where(
            (keys == lane.astype(jnp.float32)) & (lane > 0), 0.0, -1e30
        ).astype(jnp.bfloat16)


def build_x(at, segments, got, lows, highs, team, F, gaps, spread, deps):
    n, W = len(got), got[0].shape[1]
    T = segments.shape[1]
    whole = pl.BlockSpec(memory_space=pltpu.VMEM)
    out = lambda r, c, kind: jax.ShapeDtypeStruct((r, c), kind)

    def full(r, c):
        return pl.BlockSpec((r, c), lambda i, at: (0, 0))

    return pl.pallas_call(
        functools.partial(
            build_x_kernel, n=n, nlow=len(lows), nhigh=len(highs), team=team, F=F, gaps=gaps, spread=spread
        ),
        grid_spec=pltpu.PrefetchScalarGridSpec(
            num_scalar_prefetch=1,
            grid=(1,),
            in_specs=[pl.BlockSpec((8, T), lambda i, at: (at[0] // 8, 0))]
            + [full(*a.shape) for a in (*got, *lows, *highs)] + [ANY] * len(deps),
            out_specs=[full(F, W), full(W, spread), full(8, F), full(F, 128), full(team * F, 128)],
            scratch_shapes=[pltpu.VMEM((8, T + 256), jnp.int32)],
        ),
        out_shape=[
            out(F, W, jnp.bfloat16), out(W, spread, jnp.bfloat16), out(8, F, jnp.float32),
            out(F, 128, jnp.bfloat16), out(team * F, 128, jnp.bfloat16),
        ],
        cost_estimate=pl.CostEstimate(flops=8 * W * spread, bytes_accessed=6 * W * spread, transcendentals=0),
        name="build_x",
    )(at, segments, *got, *lows, *highs, *deps)


def build_d_kernel(at_ref, seg_ref, d_ref, *refs, edges, team, F, gaps, length):
    row, member = at_ref[0], at_ref[1]
    out_ref, wide_ref = refs[-2:]
    window = window_of(seg_ref, wide_ref, row, member, F)
    before = ordinals(window, F)
    zero = jnp.zeros((), jnp.bfloat16)
    if edges:
        low, high = refs[0][...], refs[1][...]
        ext = jnp.concatenate(
            [jnp.where(member > 0, low, zero), d_ref[...], jnp.where(member < team - 1, high, zero)], 0
        ).T
    else:
        ext = d_ref[...].T
        before = pltpu.roll(before, F + 2 * HALO - HALO, 1)[:, :F]
    out_ref[...] = place(ext, before, gaps, length)


def build_d(at, segments, d, edges, team, gaps, length, deps=()):
    F, W = d.shape
    T = segments.shape[1]

    def full(r, c):
        return pl.BlockSpec((r, c), lambda i, at: (0, 0))

    return pl.pallas_call(
        functools.partial(build_d_kernel, edges=bool(edges), team=team, F=F, gaps=gaps, length=length),
        grid_spec=pltpu.PrefetchScalarGridSpec(
            num_scalar_prefetch=1,
            grid=(1,),
            in_specs=[pl.BlockSpec((8, T), lambda i, at: (at[0] // 8, 0)), full(F, W)]
            + [full(*a.shape) for a in edges] + [ANY] * len(deps),
            out_specs=full(W, length),
            scratch_shapes=[pltpu.VMEM((8, T + 256), jnp.int32)],
        ),
        out_shape=jax.ShapeDtypeStruct((W, length), jnp.bfloat16),
        cost_estimate=pl.CostEstimate(flops=8 * W * length, bytes_accessed=6 * W * length, transcendentals=0),
        name="build_d",
    )(at, segments, d, *edges, *deps)


def widen_kernel(*refs, n):
    for k in range(n):
        refs[len(refs) - n + k][...] = refs[k][...].astype(jnp.float32)


def widen(arrays, deps):
    whole = pl.BlockSpec(memory_space=pltpu.VMEM)
    size = sum(a.size for a in arrays)
    return pl.pallas_call(
        functools.partial(widen_kernel, n=len(arrays)),
        in_specs=[whole] * len(arrays) + [ANY] * len(deps),
        out_specs=[whole] * len(arrays),
        out_shape=[jax.ShapeDtypeStruct(a.shape, jnp.float32) for a in arrays],
        cost_estimate=pl.CostEstimate(flops=size, bytes_accessed=6 * size, transcendentals=0),
        name="widen",
    )(*arrays, *deps)

HEAD = 64

def nt(a, b):
    return lax.dot_general(a, b, (((1,), (1,)), ((), ())), preferred_element_type=jnp.float32)

def attn_fwd_kernel(*refs, P, chunk):
    q_ref, qc_ref, kc_ref = refs[:3]
    k_refs = refs[3:3+P]
    v_refs = refs[3+P:3+2*P]
    o_ref, lse_ref, ka_ref = refs[-3:]
    F = q_ref.shape[0]
    low_k = lax.broadcasted_iota(jnp.int32, (F, 128), 1) < HEAD
    low_q = lax.broadcasted_iota(jnp.int32, (chunk, 128), 1) < HEAD
    for h in range(2):
        pick = low_k if h == 0 else jnp.logical_not(low_k)
        for p in range(P):
            ka_ref[h, p*F:(p+1)*F, :] = jnp.where(pick, k_refs[p][...], kc_ref[p*F:(p+1)*F, :])
    for c in range(F // chunk):
        rows = slice(c*chunk, (c+1)*chunk)
        q = q_ref[rows, :] * jnp.asarray(0.125, jnp.bfloat16)
        outs, lses = [], []
        for h in range(2):
            pick = low_q if h == 0 else jnp.logical_not(low_q)
            qa = jnp.where(pick, q, qc_ref[rows, :])
            s = nt(qa, ka_ref[h])
            m = jnp.maximum(jnp.max(s, axis=1, keepdims=True), -1e20)
            e = jnp.exp(s - m)
            l = jnp.maximum(jnp.sum(e, axis=1, keepdims=True), 1.0)
            pb = (e * (1.0 / l)).astype(jnp.bfloat16)
            o = sum(jnp.dot(pb[:, p*F:(p+1)*F], v_refs[p][...], preferred_element_type=jnp.float32) for p in range(P))
            outs.append(o)
            lses.append(m + jnp.log(l))
        o_ref[rows, :] = jnp.where(low_q, outs[0], outs[1]).astype(o_ref.dtype)
        lse_ref[rows, :] = jnp.where(low_q, lses[0], lses[1])

def attn_fwd(q, kvs, qc, kc, deps, chunk=128):
    F, W = q.shape
    P = len(kvs)
    T = P * F
    npair = W // 128
    return pl.pallas_call(
        functools.partial(attn_fwd_kernel, P=P, chunk=min(chunk, F)),
        grid=(npair,),
        in_specs=[pl.BlockSpec((F, 128), lambda a: (0, a)),
                  pl.BlockSpec((F, 128), lambda a: (0, 0)),
                  pl.BlockSpec((T, 128), lambda a: (0, 0))]
                 + [pl.BlockSpec((F, 128), lambda a: (0, a))] * P
                 + [pl.BlockSpec((F, 128), lambda a, n=npair: (0, a + n))] * P
                 + [ANY] * len(deps),
        out_specs=[pl.BlockSpec((F, 128), lambda a: (0, a)), pl.BlockSpec((F, 128), lambda a: (0, a))],
        out_shape=[jax.ShapeDtypeStruct((F, W), jnp.bfloat16), jax.ShapeDtypeStruct((F, W), jnp.float32)],
        scratch_shapes=[pltpu.VMEM((2, T, 128), jnp.bfloat16)],
        cost_estimate=pl.CostEstimate(flops=16 * F * T * W, bytes_accessed=16 * T * W, transcendentals=0),
        name="attn_fwd",
    )(q, qc, kc, *kvs, *kvs, *deps)

def attn_bwd_kernel(*refs, P, chunk):
    q_ref, do_ref, o_ref, lse_ref, qc_ref, kc_ref = refs[:6]
    k_refs = refs[6:6+P]
    v_refs = refs[6+P:6+2*P]
    dq_ref, dk_ref, dv_ref = refs[-2-P:1-P]
    far_refs = refs[1-P:]
    F = q_ref.shape[0]
    low_q = lax.broadcasted_iota(jnp.int32, (F, 128), 1) < HEAD
    low_c = lax.broadcasted_iota(jnp.int32, (chunk, 128), 1) < HEAD
    q = q_ref[...] * jnp.asarray(0.125, jnp.bfloat16)
    do = do_ref[...]
    lse_t = lse_ref[...].T
    prod_t = (do.astype(jnp.float32) * o_ref[...].astype(jnp.float32)).T
    lse_row = [lse_t[h*HEAD:h*HEAD+1, :] for h in range(2)]
    delta_row = [jnp.sum(prod_t[h*HEAD:(h+1)*HEAD, :], axis=0, keepdims=True) for h in range(2)]
    qa = [jnp.where(low_q if h == 0 else jnp.logical_not(low_q), q, qc_ref[...]) for h in range(2)]
    zero = jnp.zeros((), jnp.bfloat16)
    dqt = [jnp.zeros((HEAD, F), jnp.float32) for _ in range(2)]
    for p in range(P):
        for c in range(F // chunk):
            rows = slice(c*chunk, (c+1)*chunk)
            k = k_refs[p][rows, :]
            v = v_refs[p][rows, :]
            kc = kc_ref[p*F + c*chunk: p*F + (c+1)*chunk, :]
            kt = k.T
            dks, dvs = [], []
            for h in range(2):
                pick = low_c if h == 0 else jnp.logical_not(low_c)
                st = nt(jnp.where(pick, k, kc), qa[h])
                pt = jnp.exp(st - lse_row[h])
                dpt = nt(jnp.where(pick, v, zero), do)
                dst = (pt * (dpt - delta_row[h])).astype(jnp.bfloat16)
                dvs.append(jnp.dot(pt.astype(jnp.bfloat16), do, preferred_element_type=jnp.float32))
                dks.append(jnp.dot(dst, q, preferred_element_type=jnp.float32))
                dqt[h] = dqt[h] + jnp.dot(kt[h*HEAD:(h+1)*HEAD, :], dst, preferred_element_type=jnp.float32)
            dk = jnp.where(low_c, dks[0], dks[1])
            dv = jnp.where(low_c, dvs[0], dvs[1])
            if p == 0:
                dk_ref[rows, :] = dk
                dv_ref[rows, :] = dv
            else:
                far_refs[p-1][0, rows, :] = dk.astype(jnp.bfloat16)
                far_refs[p-1][1, rows, :] = dv.astype(jnp.bfloat16)
    dq = jnp.concatenate(dqt, axis=0).T * 0.125
    dq_ref[...] = dq.astype(dq_ref.dtype)

def attn_bwd(q, do, o, lse, kvs, qc, kc, first, count, deps, chunk=128):
    F, W = q.shape
    P = len(kvs)
    T = P * F
    npair = W // 128
    own = pl.BlockSpec((F, 128), lambda a: (0, a + first))
    out = pl.BlockSpec((F, 128), lambda a: (0, a))
    return pl.pallas_call(
        functools.partial(attn_bwd_kernel, P=P, chunk=min(chunk, F)),
        grid=(count,),
        in_specs=[own, own, own, own,
                  pl.BlockSpec((F, 128), lambda a: (0, 0)),
                  pl.BlockSpec((T, 128), lambda a: (0, 0))]
                 + [own] * P
                 + [pl.BlockSpec((F, 128), lambda a, n=npair: (0, a + first + n))] * P
                 + [ANY] * len(deps),
        out_specs=[out] * 3 + [pl.BlockSpec((2, F, 128), lambda a: (0, 0, a))] * (P - 1),
        out_shape=[jax.ShapeDtypeStruct((F, 128 * count), t) for t in (jnp.bfloat16, jnp.float32, jnp.float32)]
                  + [jax.ShapeDtypeStruct((2, F, 128 * count), jnp.bfloat16)] * (P - 1),
        cost_estimate=pl.CostEstimate(flops=20 * F * T * 128 * count, bytes_accessed=16 * T * W, transcendentals=0),
        name="attn_bwd",
    )(q, do, o, lse, qc, kc, *kvs, *kvs, *deps)

HALO = 64
UTT_LEAST = 256
root_half = 0.7071067811865476
inv_root_two_pi = 0.3989422804014327
f32 = jnp.float32
bf16 = jnp.bfloat16


def layer_norm(hidden):
    centred = hidden - jnp.mean(hidden, axis=-1, keepdims=True)
    inv_scale = lax.rsqrt(jnp.mean(centred * centred, axis=-1, keepdims=True) + 1e-05)
    return (centred * inv_scale, inv_scale)


def norm_back(grad_normed, normed, inv_scale):
    return inv_scale * (
        grad_normed
        - jnp.mean(grad_normed, axis=-1, keepdims=True)
        - normed * jnp.mean(grad_normed * normed, axis=-1, keepdims=True)
    )


def gelu(entries):
    return 0.5 * entries * (1.0 + lax.erf(entries * root_half))


def gelu_slope(entries):
    return (
        0.5 * (1.0 + lax.erf(entries * root_half))
        + entries * jnp.exp(-0.5 * entries * entries) * inv_root_two_pi
    )


def mm(a, b):
    return jnp.dot(a, b, preferred_element_type=f32)


def mm_back(a, b):
    return lax.dot_general(a, b, (((1,), (1,)), ((), ())), preferred_element_type=f32)


def wgrad(a, b):
    return lax.dot_general(a, b, (((0,), (0,)), ((), ())), preferred_element_type=f32)


class Plan:
    def __init__(self, dp, seq, rows_dev):
        self.dp, self.seq, self.n = dp, seq, rows_dev
        self.q = seq // (2 * rows_dev)
        self.P = 2 * self.q
        assert dp % 2 == 0 and self.q * 2 * rows_dev == seq and rows_dev > 1

    def out_pairs(self, m):
        pairs = []
        for d in range(self.dp):
            for z in range(self.seq):
                rho = self.n * (d % 2) + (z + m) % self.n
                u = z // self.n
                pairs.append((d * self.seq + z, self.member(d // 2, rho, u)))
        return pairs

    def edge_pairs(self):
        heads = [[] for _ in range(self.n)]
        tails = [[] for _ in range(self.n)]
        for d in range(self.dp):
            for z in range(self.seq):
                u = z // self.n
                for j in range(self.n):
                    rho = self.n * (d % 2) + j
                    if z % self.n == self.n - 1 and u + 1 < self.P:
                        tails[j].append((d * self.seq + z, self.member(d // 2, rho, u + 1)))
                    if z % self.n == 0 and u > 0:
                        heads[j].append((d * self.seq + z, self.member(d // 2, rho, u - 1)))
        return heads, tails

    def member(self, e, rho, u):
        return (2 * e + u % 2) * self.seq + rho * self.q + u // 2

    def team_pairs(self, shift, wrap):
        pairs = []
        for e in range(self.dp // 2):
            for rho in range(2 * self.n):
                for u in range(self.P):
                    to = u + shift
                    if wrap or 0 <= to < self.P:
                        pairs.append((self.member(e, rho, u), self.member(e, rho, to % self.P)))
        return pairs


BOTH = ("dp", "seq")


def on_device(
    frames,
    output_gradient,
    segments,
    layer_keep,
    conv_weight,
    convolution_bias,
    query_matrix,
    query_offset_bias,
    key_matrix,
    value_matrix,
    value_offset_bias,
    attn_weight,
    attn_bias,
    first_gain,
    first_shift,
    inner_weight,
    inner_bias,
    outer_weight,
    outer_bias,
    second_gain,
    second_shift,
):
    rows_dev, local_len, width = frames.shape
    total_rows, row_len = segments.shape
    dp_count, seq_count = lax.axis_size("dp"), lax.axis_size("seq")
    dp_index, seq_index = lax.axis_index("dp"), lax.axis_index("seq")
    plan = Plan(dp_count, seq_count, rows_dev)
    n, q, team = plan.n, plan.q, plan.P
    F = row_len // team
    taps, _, gw = conv_weight.shape
    tap_blocks = taps // DK
    rho = seq_index // q
    member = (seq_index % q) * 2 + dp_index % 2
    row_id = (dp_index // 2) * (2 * n) + rho

    def pick(parts, index):
        out = parts[0]
        for k in range(1, len(parts)):
            out = jnp.where(index == k, parts[k], out)
        return out

    def blocks_to_team(a):
        got = []
        for m in range(n):
            sent = pick([a[j] for j in range(n)], (seq_index + m) % n)
            got.append(lax.ppermute(sent, BOTH, plan.out_pairs(m)))
        return got

    def to_team(a):
        got = blocks_to_team(a)
        j = rho % n
        return jnp.concatenate([pick(got, (j - w) % n) for w in range(n)], 0)

    def from_team(sent):
        back = [
            lax.ppermute(sent[m], BOTH, [(t, s) for s, t in plan.out_pairs(m)]) for m in range(n)
        ]
        return jnp.stack([pick(back, (row - seq_index) % n) for row in range(n)], 0)

    def edges_to_team(a):
        heads, tails = plan.edge_pairs()
        lows, highs = [], []
        for j in range(n):
            tail, head = a[j, local_len - HALO :], a[j, :HALO]
            if team == 2:
                got = lax.ppermute(
                    jnp.where(seq_index % n == 0, head, tail), BOTH, heads[j] + tails[j]
                )
                lows.append(got)
                highs.append(got)
            else:
                lows.append(lax.ppermute(tail, BOTH, tails[j]))
                highs.append(lax.ppermute(head, BOTH, heads[j]))
        return lows, highs

    def edges(a):
        if team == 2:
            got = lax.ppermute(
                jnp.where(member == 0, a[F - HALO :], a[:HALO]), BOTH, plan.team_pairs(1, True)
            )
            return got, got
        low = lax.ppermute(a[F - HALO :], BOTH, plan.team_pairs(1, False))
        high = lax.ppermute(a[:HALO], BOTH, plan.team_pairs(-1, False))
        return low, high

    def pairs_of(axis, bit):
        pairs = []
        for d in range(dp_count):
            for z in range(seq_count):
                to = (d ^ bit, z) if axis == "dp" else (d, z ^ bit)
                pairs.append((d * seq_count + z, to[0] * seq_count + to[1]))
        return pairs

    def halve(a, axis, index, bit, high, low):
        mine = (index // bit) % 2
        a = a.reshape((high, 2, low) + a.shape[1:])
        sent = pick([a[:, 0], a[:, 1]], 1 - mine).reshape((high * low,) + a.shape[3:])
        kept = pick([a[:, 0], a[:, 1]], mine).reshape(sent.shape)
        return kept, lax.ppermute(sent, BOTH, pairs_of(axis, bit)), sent

    class Scatter:
        def __init__(self, halves, swap, many=1):
            bits = [1 << i for i in range(dp_count.bit_length() - 1)]
            order = [1] + (bits[1:] if swap else bits[:0:-1])
            left = list(reversed(bits))
            self.steps = []
            for bit in order:
                at = left.index(bit)
                self.steps.append((bit, many * 2**at, 2 ** (len(left) - 1 - at)))
                left.remove(bit)
            self.steps.pop(0)
            self.sent, self.kept = halves
            self.got = lax.ppermute(self.sent, BOTH, pairs_of("dp", 1))

        def step(self, *deps):
            bit, high, low = self.steps.pop(0)
            mine = ((dp_index // bit) % 2).astype(jnp.int32).reshape(1)
            self.sent, self.kept = join_split(self.kept, self.got, mine, high, low, deps)
            self.got = lax.ppermute(self.sent, BOTH, pairs_of("dp", bit))

        def last(self, *deps):
            while self.steps:
                self.step(*deps)
            return join_last(self.kept, self.got, deps)

    class SeqSum:
        def __init__(self, a):
            self.shape = a.shape
            self.a = a.astype(bf16).reshape(seq_count, -1, a.shape[1])
            bits = [1 << i for i in range(seq_count.bit_length() - 1)]
            left = list(reversed(bits))
            self.steps = []
            for bit in bits:
                at = left.index(bit)
                self.steps.append((bit, 2**at, 2 ** (len(left) - 1 - at)))
                left.remove(bit)
            self.back = list(reversed(bits))
            bit, high, low = self.steps.pop(0)
            self.kept, self.got, self.sent = halve(self.a, "seq", seq_index, bit, high, low)

        def step(self, *deps):
            if self.steps:
                bit, high, low = self.steps.pop(0)
                mine = ((seq_index // bit) % 2).astype(jnp.int32).reshape(1)
                self.sent, self.kept = join_split(self.kept, self.got, mine, high, low, deps)
                self.got = lax.ppermute(self.sent, BOTH, pairs_of("seq", bit))

        def whole(self):
            self.add()
            return self.finish()

        def add(self, *deps):
            while self.steps:
                self.step(*deps)
            self.a = join_last(self.kept, self.got, deps).reshape(self.kept.shape)

        def finish(self, *deps):
            a = self.a
            for bit in self.back:
                other = lax.ppermute(a, BOTH, pairs_of("seq", bit))
                low_half = (seq_index // bit) % 2 == 0
                pair = jnp.where(low_half, jnp.stack([a, other], 1), jnp.stack([other, a], 1))
                a = pair.reshape((-1,) + a.shape[1:])
            return a.reshape(self.shape)

    def by_dp(a):
        return a.reshape(dp_count, -1, a.shape[-1])

    def by_share(a):
        a = a.reshape(dp_count, width // dp_count, a.shape[1])
        out, sent = [], []
        for k in range(dp_count):
            piece = lax.dynamic_index_in_dim(a, dp_index ^ k, 0, keepdims=False)
            sent.append(piece)
            out.append(piece if k == 0 else lax.ppermute(piece, BOTH, pairs_of("dp", k)))
        return out, sent

    weight_tr = prep(conv_weight)

    x_blocks = blocks_to_team(frames)
    x_lows, x_highs = edges_to_team(frames)
    grad_out = to_team(output_gradient)

    keep = (lax.dynamic_index_in_dim(layer_keep, row_id, 0, keepdims=False) > 0).astype(f32)
    gaps = 1 + max(F - 2, 0) // UTT_LEAST
    spread = -(-(F + 2 * HALO + HALO * gaps) // 128) * 128
    out_spread = -(-(F + HALO * gaps) // 128) * 128
    where_at = jnp.stack([row_id, member, rho % n]).astype(jnp.int32)
    x, spread_x, select, q_codes, k_codes = build_x(
        where_at, segments, x_blocks, x_lows, x_highs, team, F, gaps, spread, (weight_tr,)
    )
    conv_t = conv(spread_x, weight_tr, select, F, gaps)
    x_shares = lax.all_to_all(
        spread_x.reshape(dp_count, width // dp_count, spread), "dp", 0, 0, tiled=True
    )

    conv_before, pos_out, pos_low, query, kv = front(
        conv_t, convolution_bias, x, query_matrix, key_matrix, value_matrix, query_offset_bias,
        value_offset_bias, (),
    )
    kvs = [kv] + [lax.ppermute(kv, BOTH, plan.team_pairs(s, True)) for s in range(1, team)]
    attn_low, lse = attn_fwd(query, kvs, q_codes, k_codes, (x_shares,), 256)

    back_at = ((rho % n - jnp.arange(n, dtype=jnp.int32)) % n).astype(jnp.int32)
    (
        layer_sent, first_low, inner_low, grad_outer_low, grad_inner_low, grad_attn_low,
        grad_first_sum, grad_heads, inner_sums, mid_sums,
    ) = mid(
        keep.reshape(1), attn_low, pos_out, grad_out, attn_weight, inner_weight, outer_weight,
        attn_bias, first_gain, first_shift, inner_bias, outer_bias, second_gain, second_shift, (),
    )
    layer_sent = [layer_sent[k * local_len : (k + 1) * local_len] for k in range(n)]
    layer_sent = [pick(layer_sent, back_at[m]) for m in range(n)]
    layer_out = from_team(layer_sent)
    core = (dp_index % 2).astype(jnp.int32).reshape(1)
    outer_sum = Scatter(wg_rows(core, grad_outer_low, inner_low, 1, dp_count, 4, (), tuple(layer_sent)), False)
    by_rows = (inner_weight.shape[1] // dp_count) % 128 != 0
    if by_rows:
        halves = wg_rows(core, grad_inner_low, first_low, 1, dp_count, 1, (), (outer_sum.sent,))
    else:
        halves = wg_cols(core, first_low, grad_inner_low, dp_count, (outer_sum.sent,))
    inner_sum = Scatter(halves, True)
    extras = (inner_sums, mid_sums)
    pairs = width // 128
    grads = []
    deps = (outer_sum.sent, inner_sum.sent)
    for k in range(2):
        grads.append(
            attn_bwd(
                query, grad_heads, attn_low, lse, kvs, q_codes, k_codes, k * pairs // 2, pairs // 2,
                deps, 256,
            )
        )
        if k == 0:
            outer_sum.step(grads[0][0])
            inner_sum.step(outer_sum.sent)
            deps = (inner_sum.sent,)
    fars = [
        [lax.ppermute(g[2 + s], BOTH, plan.team_pairs(-s, True)) for s in range(1, team)]
        for g in grads
    ]
    low_qk, low_v, grad_pos, grad_conv_low, qk_sums, v_sums = dpos(
        keep.reshape(1), *[[g[k] for g in grads] for k in range(3)], fars, query_matrix,
        key_matrix, value_matrix, grad_first_sum, grad_out, conv_before, (),
    )

    d_pieces = build_d(where_at, segments, grad_conv_low, (), team, gaps, out_spread).reshape(
        dp_count, width // dp_count, out_spread
    )
    d_shares = lax.all_to_all(d_pieces, "dp", 0, 0, tiled=True)
    low, high = edges(grad_conv_low)
    outer_sum.step(d_pieces)
    inner_sum.step(outer_sum.sent)
    slots = 2 * dp_count // 2
    qk_sum = Scatter(
        wg_rows(core, low_qk, pos_low, 2, dp_count, 1, (qk_sums,), (inner_sum.sent,)), True, 2
    )
    halves = wg_rows(core, low_v, pos_low, 1, dp_count, 1, (v_sums,), (qk_sum.sent,), slots)
    halves = wg_rows(core, grad_attn_low, attn_low, 1, dp_count, 1, extras, (), slots, 1, halves)
    va_sum = Scatter(halves, False, 2)
    spread_d = build_d(
        where_at, segments, grad_conv_low, (low, high), team, gaps, spread, (va_sum.sent,)
    )
    outer_share = outer_sum.last(va_sum.sent)
    inner_share = inner_sum.last(outer_share)
    o_g, i_g = lax.psum((outer_share, inner_share), "seq")

    group_count = width // dp_count // gw
    deps = (inner_share, spread_d)
    conv_sums = []
    for group in range(group_count):
        part = conv_dw(x_shares, d_shares, group, gw, tap_blocks, deps)
        conv_sums.append(SeqSum(part))
        deps = (conv_sums[-1].sent,)
        if group == 0:
            qk_sum.step(*deps)
            va_sum.step(qk_sum.sent)
            deps = (va_sum.sent,)
    groups = width // gw
    back_a = conv_dx(spread_d, weight_tr, select, F, gaps, 0, groups // 2, deps)
    deps = (back_a,)
    for c in conv_sums:
        c.step(*deps)
        deps = (c.sent,)
    qk_sum.step(*deps)
    va_sum.step(qk_sum.sent)
    deps = (va_sum.sent,)
    back_b = conv_dx(spread_d, weight_tr, select, F, gaps, groups // 2, groups - groups // 2, deps)
    deps = (back_b,)
    for c in conv_sums:
        c.add(*deps)
        deps = (c.a,)
    qk_share = qk_sum.last(*deps)
    va_share = va_sum.last(qk_share)
    conv_back = jnp.concatenate([back_a, back_b], 0)
    seg_row = lax.dynamic_index_in_dim(segments, row_id, 0, keepdims=False)
    live = lax.dynamic_slice_in_dim(seg_row, member * F, F) > 0
    grad_in = jnp.where(live[:, None], grad_pos + conv_back.T, 0.0).astype(bf16)
    grad_in = [grad_in[k * local_len : (k + 1) * local_len] for k in range(n)]
    grad_in = [pick(grad_in, back_at[m]) for m in range(n)]
    grad_input = from_team(grad_in)
    proj = SeqSum(jnp.concatenate([qk_share, va_share], 0))
    conv_sums = [c.finish() for c in conv_sums]
    proj_pack = proj.whole().astype(f32)
    o_g, i_g = widen((o_g, i_g), tuple(conv_sums))
    o_g = o_g.T
    i_g = i_g.T if by_rows else i_g
    grad_conv_weight = finish_dw(conv_sums, gw, tap_blocks)
    grad_conv_bias = jnp.concatenate([c[tap_blocks * gw, :gw] for c in conv_sums]).astype(f32)

    share = width // dp_count
    ff = inner_bias.shape[0]
    pieces = proj_pack.reshape(4, -1, width)
    q_g, k_g, v_g, a_g = (pieces[k, :share].T for k in range(4))
    small = pieces[3, share : share + ff // width + 6]
    inner_bias_share = lax.dynamic_slice_in_dim(
        small[: ff // width].reshape(-1), dp_index * (ff // dp_count), ff // dp_count
    )
    rows_ = jnp.concatenate(
        [small[ff // width :], pieces[0, share : share + 1], pieces[2, share : share + 1]]
    )
    rows_ = lax.dynamic_slice_in_dim(rows_, dp_index * share, share, 1)
    vecs = [rows_[6], rows_[7]] + [rows_[k] for k in range(6)] + [grad_conv_bias]
    return (
        layer_out,
        grad_input,
        grad_conv_weight,
        vecs[8],
        q_g,
        vecs[0],
        k_g,
        v_g,
        vecs[1],
        a_g,
        vecs[2],
        vecs[3],
        vecs[4],
        i_g,
        inner_bias_share,
        o_g,
        vecs[5],
        vecs[6],
        vecs[7],
    )


def solution(mesh):
    rows = P("dp", "seq", None)
    by_col, vec = P(None, "dp"), P("dp")
    out_specs = (
        rows, rows, P(None, "dp", None), vec, by_col, vec, by_col, by_col, vec, by_col, vec, vec,
        vec, by_col, vec, by_col, vec, vec, vec,
    )
    return jax.shard_map(
        on_device, mesh=mesh, in_specs=(rows, rows) + (P(),) * 19, out_specs=out_specs, check_vma=False
    )
```

```python
import functools
import jax
import jax.numpy as jnp
from jax import lax
from jax.experimental import pallas as pl
from jax.experimental.pallas import tpu as pltpu
from jax.sharding import PartitionSpec as P


DK = 16
COST = pl.CostEstimate(flops=1000, bytes_accessed=1000, transcendentals=0)
ANY = pl.BlockSpec(memory_space=pl.ANY)

def prep_kernel(w_ref, wt_ref):
    gw = w_ref.shape[1]
    slots = w_ref.shape[2] // gw
    lane = lax.broadcasted_iota(jnp.int32, (gw, 128), 1)
    tiles = w_ref.shape[2] // 128
    for half in range(DK // slots):
        sums = [[None] * tiles for _ in range(slots)]
        for slot in range(slots):
            w = w_ref[half * slots + slot]
            for g in range(slots):
                turn = (slot - g) % slots
                moved = w if turn == 0 else pltpu.roll(w, gw * turn, 1)
                for t in range(tiles):
                    lo, hi = gw * slot - 128 * t, gw * (slot + 1) - 128 * t
                    if hi <= 0 or lo >= 128:
                        continue
                    part = moved[:, 128 * t : 128 * (t + 1)]
                    old = sums[g][t]
                    sums[g][t] = part if old is None else jnp.where(lane >= lo, part, old)
        for g in range(slots):
            for t in range(tiles):
                at = half * slots * gw + 128 * t
                wt_ref[g, :, at : at + 128] = sums[g][t]


def prep(w):
    k, width, gw = w.shape
    groups = width // gw
    nb = k // DK
    slots = 8
    assert (slots * gw) % 128 == 0 and DK % slots == 0 and groups % slots == 0
    return pl.pallas_call(
        prep_kernel,
        grid=(groups // slots, nb),
        in_specs=[pl.BlockSpec((DK, gw, slots * gw), lambda i, b: (b, 0, i))],
        out_specs=pl.BlockSpec((slots, gw, DK * gw), lambda i, b: (i, b, 0)),
        out_shape=jax.ShapeDtypeStruct((groups, nb * gw, DK * gw), w.dtype),
        cost_estimate=COST,
        name="prep",
    )(jnp.transpose(w, (0, 2, 1)))

def ungap(acc, sel_ref, F, nbound):
    out = acc[:, :F]
    for n in range(1, nbound + 1):
        moved = pltpu.roll(acc, acc.shape[1] - HALO * n, 1)[:, :F]
        out = jnp.where(sel_ref[n : n + 1, :] > 0, moved, out)
    return out


def conv_kernel(xt_ref, wt_ref, sel_ref, out_ref, *refs, nb, gw, F, nbound, G):
    stacks, sums = refs[:G], refs[G:]
    tin = xt_ref.shape[1]
    for g in range(G):
        x = xt_ref[g*gw:(g+1)*gw, :]
        for dk in range(DK):
            stacks[g][gw*dk:gw*(dk+1), :] = x if dk == 0 else pltpu.roll(x, tin - dk, 1)
    for g in range(G):
        sums[g][...] = jnp.dot(wt_ref[g], stacks[g][...], preferred_element_type=jnp.float32)
    for g in range(G):
        acc = sums[g][0:gw, :]
        for b in range(1, nb):
            acc = acc + pltpu.roll(sums[g][gw*b:gw*(b+1), :], tin - DK*b, 1)
        out_ref[g*gw:(g+1)*gw, :] = ungap(acc, sel_ref, F, nbound)


def conv(xt, wt, sel, F, nbound, G=2):
    width, tin = xt.shape
    g, nbgw, dkgw = wt.shape
    gw = width // g
    return pl.pallas_call(
        functools.partial(conv_kernel, nb=nbgw // gw, gw=gw, F=F, nbound=nbound, G=G),
        grid=(g // G,),
        in_specs=[pl.BlockSpec((G*gw, tin), lambda i: (i, 0)),
                  pl.BlockSpec((G, nbgw, dkgw), lambda i: (i, 0, 0)),
                  pl.BlockSpec(sel.shape, lambda i: (0, 0))],
        out_specs=pl.BlockSpec((G*gw, F), lambda i: (i, 0)),
        out_shape=jax.ShapeDtypeStruct((width, F), jnp.float32),
        scratch_shapes=[pltpu.VMEM((dkgw, tin), jnp.bfloat16)] * G + [pltpu.VMEM((nbgw, tin), jnp.float32)] * G,
        cost_estimate=COST,
        name="conv_fwd",
    )(xt, wt, sel)


def dx_kernel(dt_ref, wt_ref, sel_ref, *refs, nb, gw, F, nbound, G):
    out_ref, refs = refs[-1 - 2*G], refs[-2*G:]
    stacks, sums = refs[:G], refs[G:]
    tin = dt_ref.shape[1]
    for g in range(G):
        d = dt_ref[g*gw:(g+1)*gw, :]
        for b in range(nb):
            stacks[g][gw*b:gw*(b+1), :] = d if b == 0 else pltpu.roll(d, DK*b, 1)
    for g in range(G):
        sums[g][...] = jnp.dot(wt_ref[g].T, stacks[g][...], preferred_element_type=jnp.float32)
    for g in range(G):
        acc = sums[g][0:gw, :]
        for dk in range(1, DK):
            acc = acc + pltpu.roll(sums[g][gw*dk:gw*(dk+1), :], dk, 1)
        out_ref[g*gw:(g+1)*gw, :] = ungap(acc[:, 2*HALO:], sel_ref, F, nbound)


def conv_dx(dt, wt, sel, F, nbound, first, count, deps, G=2):
    width, tin = dt.shape
    g, nbgw, dkgw = wt.shape
    gw = width // g
    first = first // G
    return pl.pallas_call(
        functools.partial(dx_kernel, nb=nbgw // gw, gw=gw, F=F, nbound=nbound, G=G),
        grid=(count // G,),
        in_specs=[pl.BlockSpec((G*gw, tin), lambda i: (i + first, 0)),
                  pl.BlockSpec((G, nbgw, dkgw), lambda i: (i + first, 0, 0)),
                  pl.BlockSpec(sel.shape, lambda i: (0, 0))] + [ANY] * len(deps),
        out_specs=pl.BlockSpec((G*gw, F), lambda i: (i, 0)),
        out_shape=jax.ShapeDtypeStruct((count * gw, F), jnp.float32),
        scratch_shapes=[pltpu.VMEM((nbgw, tin), jnp.bfloat16)] * G + [pltpu.VMEM((dkgw, tin), jnp.float32)] * G,
        cost_estimate=COST,
        name="conv_dx",
    )(dt, wt, sel, *deps)


def dw_kernel(*refs, nb, gw, m):
    x_refs, d_refs = refs[:m], refs[m : 2 * m]
    out_ref, a0_ref, ds_ref = refs[-3:]
    tin = x_refs[0].shape[2]
    tout = d_refs[0].shape[2]
    ones = jnp.ones((16, tout), jnp.bfloat16)
    bias = None
    for s in range(m):
        x, d = x_refs[s][0], d_refs[s][0]
        part = lax.dot_general(ones, d, (((1,), (1,)), ((), ())), preferred_element_type=jnp.float32)
        bias = part if bias is None else bias + part
        d = jnp.concatenate([d, jnp.zeros((gw, tin - tout), d.dtype)], axis=1)
        slot = s % 2
        for dk in range(DK):
            a0_ref[slot, gw*dk:gw*(dk+1), :] = x if dk == 0 else pltpu.roll(x, tin - dk, 1)
        for b in range(nb):
            ds_ref[slot, gw*b:gw*(b+1), :] = d if b == 0 else pltpu.roll(d, DK*b, 1)
        p = lax.dot_general(
            ds_ref[slot], a0_ref[slot], (((1,), (1,)), ((), ())), preferred_element_type=jnp.float32
        )
        if s == 0:
            out_ref[: nb*gw, :] = p
        else:
            out_ref[: nb*gw, :] += p
    out_ref[nb*gw :, :] = jnp.zeros((out_ref.shape[0] - nb*gw, out_ref.shape[1]), jnp.float32)
    out_ref[nb*gw : nb*gw + 16, :gw] = bias


def conv_dw(xs, ds, gw, nb, deps):
    m, channels, tin = xs.shape
    tout = ds.shape[2]
    rows = nb*gw + 32
    flops = 2 * m * nb*gw * DK*gw * tin
    return pl.pallas_call(
        functools.partial(dw_kernel, nb=nb, gw=gw, m=m),
        grid=(channels // gw,),
        in_specs=[pl.BlockSpec((1, gw, tin), lambda i, k=k: (k, i, 0)) for k in range(m)]
        + [pl.BlockSpec((1, gw, tout), lambda i, k=k: (k, i, 0)) for k in range(m)]
        + [ANY] * len(deps),
        out_specs=pl.BlockSpec((rows, DK*gw), lambda i: (i, 0)),
        scratch_shapes=[pltpu.VMEM((2, DK*gw, tin), jnp.bfloat16), pltpu.VMEM((2, nb*gw, tin), jnp.bfloat16)],
        out_shape=jax.ShapeDtypeStruct((channels // gw * rows, DK*gw), jnp.float32),
        cost_estimate=COST,
        name="conv_dw",
    )(*([xs] * m), *([ds] * m), *deps)


def join_kernel(mine_ref, ks_ref, kk_ref, gs_ref, gk_ref, *refs):
    sent_ref, kept_ref = refs[-2:]
    sent_ref[...] = (ks_ref[...].astype(jnp.float32) + gs_ref[...].astype(jnp.float32)).astype(sent_ref.dtype)
    kept_ref[...] = (kk_ref[...].astype(jnp.float32) + gk_ref[...].astype(jnp.float32)).astype(kept_ref.dtype)


def pieces_of(rows, cols):
    while rows * cols > 640 * 1024 and rows % 32 == 0:
        rows //= 2
    while rows * cols > 640 * 1024 and cols % 256 == 0:
        cols //= 2
    return rows, cols


def join_split(kept, got, mine, high, low, deps):
    n, rows, cols = kept.shape
    r, c = pieces_of(rows, cols)

    def half(other):
        def at(i, j, k, mine_ref):
            side = 1 - mine_ref[0] if other else mine_ref[0]
            return ((i // low * 2 + side) * low + i % low, j, k)

        return pl.BlockSpec((1, r, c), at)

    out = pl.BlockSpec((1, r, c), lambda i, j, k, mine_ref: (i, j, k))
    shape = jax.ShapeDtypeStruct((n // 2, rows, cols), kept.dtype)
    return pl.pallas_call(
        join_kernel,
        grid_spec=pltpu.PrefetchScalarGridSpec(
            num_scalar_prefetch=1,
            grid=(n // 2, rows // r, cols // c),
            in_specs=[half(True), half(False), half(True), half(False)] + [ANY] * len(deps),
            out_specs=[out, out],
        ),
        out_shape=[shape, shape],
        cost_estimate=COST,
        name="join",
    )(mine, kept, kept, got, got, *deps)


def join_last_kernel(k_ref, g_ref, *refs):
    refs[-1][...] = (k_ref[...].astype(jnp.float32) + g_ref[...].astype(jnp.float32)).astype(refs[-1].dtype)


def join_last(kept, got, deps):
    n, rows, cols = kept.shape
    r, c = pieces_of(rows, cols)
    block = pl.BlockSpec((1, r, c), lambda i, j, k: (i, j, k))
    return pl.pallas_call(
        join_last_kernel,
        grid=(n, rows // r, cols // c),
        in_specs=[block, block] + [ANY] * len(deps),
        out_specs=block,
        out_shape=jax.ShapeDtypeStruct(kept.shape, kept.dtype),
        cost_estimate=COST,
        name="join_last",
    )(kept, got, *deps).reshape(-1, kept.shape[-1])


def finish_kernel(p_ref, *refs, nb, gw):
    out_ref, e_ref, q_ref = refs[-3:]
    dkgw = DK * gw

    @pl.when(pl.program_id(0) == 0)
    def _():
        row = lax.broadcasted_iota(jnp.int32, (dkgw, dkgw), 0)
        col = lax.broadcasted_iota(jnp.int32, (1, dkgw), 1)
        e_ref[...] = (row == (col % DK) * gw + col // DK).astype(e_ref.dtype)

    per = 128 // DK
    lane_block = lax.broadcasted_iota(jnp.int32, (gw, 128), 1) // DK
    q_ref[...] = jnp.dot(
        p_ref[: nb * gw, :], e_ref[...], preferred_element_type=jnp.float32
    ).astype(q_ref.dtype)
    for tile in range(dkgw // 128):
        outs = [None] * per
        for b in range(nb):
            piece = q_ref[gw*b:gw*(b+1), 128*tile:128*(tile+1)]
            for i in range(per):
                turn = (b - i) % per
                moved = piece if turn == 0 else pltpu.roll(piece, DK * turn, 1)
                outs[i] = moved if outs[i] is None else jnp.where(lane_block == b, moved, outs[i])
        for i in range(per):
            out_ref[tile * per + i] = outs[i].astype(out_ref.dtype)


def finish_dw(p, gw, nb):
    assert nb * DK == 128
    rows = nb*gw + 32
    g = p.shape[0] // rows
    out = pl.pallas_call(
        functools.partial(finish_kernel, nb=nb, gw=gw),
        grid=(g,),
        in_specs=[pl.BlockSpec((rows, DK*gw), lambda i: (i, 0))],
        out_specs=pl.BlockSpec((gw, gw, 128), lambda i: (i, 0, 0)),
        out_shape=jax.ShapeDtypeStruct((g*gw, gw, 128), jnp.float32),
        scratch_shapes=[pltpu.VMEM((DK*gw, DK*gw), jnp.bfloat16), pltpu.VMEM((nb*gw, DK*gw), jnp.bfloat16)],
        cost_estimate=COST,
        name="finish_dw",
    )(p)
    return jnp.transpose(out, (2, 0, 1))


def wg_rows_kernel(mine_ref, lhs_ref, rhs_ref, *refs, many, dp, nextra, ndeps):
    extra_refs = refs[:nextra]
    sent_ref, kept_ref, lt_ref, ls_ref, lk_ref = refs[nextra + ndeps :]
    half = many * dp // 2
    share = lhs_ref.shape[1] // (many * dp)
    cols = sent_ref.shape[2]
    mine = mine_ref[0]

    @pl.when(pl.program_id(0) == 0)
    def _():
        lt_ref[...] = lhs_ref[...].T
        for i in range(half):
            for to_ref, side in ((ls_ref, 1 - mine), (lk_ref, mine)):
                at = pl.multiple_of((2 * i + side) * share, 16)
                to_ref[i * share : (i + 1) * share, :] = lt_ref[pl.ds(at, share), :]

    for out_ref, l_ref in ((sent_ref, ls_ref), (kept_ref, lk_ref)):
        total = jnp.dot(l_ref[...], rhs_ref[...], preferred_element_type=jnp.float32)
        for i in range(half):
            out_ref[i, :share, :] = total[i * share : (i + 1) * share, :].astype(out_ref.dtype)
    if nextra:
        for m in range(many):
            rows = []
            for r in extra_refs:
                if many > 1:
                    rows.append(r[0:1, m * cols : (m + 1) * cols])
                else:
                    rows += [r[0:1, k * cols : (k + 1) * cols] for k in range(r.shape[1] // cols)]
            rows.append(jnp.zeros((16 - len(rows), cols), jnp.float32))
            block = jnp.concatenate(rows, 0).astype(jnp.bfloat16)
            for i in range(dp // 2):
                sent_ref[m * dp // 2 + i, share:, :] = block
                kept_ref[m * dp // 2 + i, share:, :] = block


def wg_rows(mine, lhs, rhs, many, dp, chunks, extras=(), deps=(), slots=None, first=0, into=()):
    F, M = lhs.shape
    N = rhs.shape[1]
    share = M // (many * dp)
    half = many * dp // 2
    rows = share + (16 if extras else 0)
    out = pl.BlockSpec((half, rows, N // chunks), lambda i, m: (first, 0, i))
    shape = jax.ShapeDtypeStruct((slots or half, rows, N), jnp.bfloat16)
    deps = tuple(into) + tuple(deps)
    at = 3 + len(extras)
    return pl.pallas_call(
        functools.partial(wg_rows_kernel, many=many, dp=dp, nextra=len(extras), ndeps=len(deps)),
        input_output_aliases={at: 0, at + 1: 1} if into else {},
        grid_spec=pltpu.PrefetchScalarGridSpec(
            num_scalar_prefetch=1,
            grid=(chunks,),
            in_specs=[
                pl.BlockSpec((F, M), lambda i, m: (0, 0)),
                pl.BlockSpec((F, N // chunks), lambda i, m: (0, i)),
            ]
            + [pl.BlockSpec(e.shape, lambda i, m: (0, 0)) for e in extras]
            + [ANY] * len(deps),
            out_specs=[out, out],
            scratch_shapes=[
                pltpu.VMEM((M, F), jnp.bfloat16),
                pltpu.VMEM((half * share, F), jnp.bfloat16),
                pltpu.VMEM((half * share, F), jnp.bfloat16),
            ],
        ),
        out_shape=[shape, shape],
        cost_estimate=COST,
        name="wg_rows",
    )(mine, lhs, rhs, *extras, *deps)


def wg_plain_kernel(lhs_ref, rhs_ref, *refs, share):
    out_ref, lt_ref = refs[-2:]

    @pl.when(pl.program_id(0) == 0)
    def _():
        lt_ref[...] = lhs_ref[...].T

    total = jnp.dot(lt_ref[...], rhs_ref[...], preferred_element_type=jnp.float32).astype(jnp.bfloat16)
    if share:
        for k in range(out_ref.shape[0]):
            out_ref[k] = total[:, k * share : (k + 1) * share]
    else:
        out_ref[...] = total


def wg_plain(lhs, rhs, chunks, share, deps=()):
    F, M = lhs.shape
    N = rhs.shape[1]
    cols = N // chunks
    if share:
        spec = pl.BlockSpec((cols // share, M, share), lambda i: (i, 0, 0))
        shape = jax.ShapeDtypeStruct((N // share, M, share), jnp.bfloat16)
    else:
        spec = pl.BlockSpec((M, cols), lambda i: (0, i))
        shape = jax.ShapeDtypeStruct((M, N), jnp.bfloat16)
    return pl.pallas_call(
        functools.partial(wg_plain_kernel, share=share),
        grid=(chunks,),
        in_specs=[pl.BlockSpec((F, M), lambda i: (0, 0)), pl.BlockSpec((F, cols), lambda i: (0, i))]
        + [ANY] * len(deps),
        out_specs=spec,
        scratch_shapes=[pltpu.VMEM((M, F), jnp.bfloat16)],
        out_shape=shape,
        cost_estimate=COST,
        name="wg_plain",
    )(lhs, rhs, *deps)


def dpos_kernel(at_ref, keep_ref, *refs, parts, far, n, ndeps):
    qs, ks, vs = refs[:parts], refs[parts : 2 * parts], refs[2 * parts : 3 * parts]
    far_refs, refs = refs[3 * parts : (3 + far) * parts], refs[(3 + far) * parts :]
    wq_ref, wk_ref, wv_ref, first_ref, conv_ref = refs[:5]
    g_refs = refs[5 : 5 + n]
    low_ref, lowv_ref, pos_ref, d_ref, qk_ref, v_ref = refs[5 + n + ndeps :]
    turn = (at_ref[2] - pl.program_id(0) + n) % n
    dq = jnp.concatenate([r[...] for r in qs], 1)
    dks, dvs = [], []
    for p in range(parts):
        dk, dv = ks[p][...], vs[p][...]
        for r in far_refs[p * far : (p + 1) * far]:
            dk = dk + r[0].astype(jnp.float32)
            dv = dv + r[1].astype(jnp.float32)
        dks.append(dk.astype(jnp.bfloat16))
        dvs.append(dv.astype(jnp.bfloat16))
    dk, dv = jnp.concatenate(dks, 1), jnp.concatenate(dvs, 1)
    width = dq.shape[1]
    low_ref[:, :width] = dq
    low_ref[:, width:] = dk
    lowv_ref[...] = dv
    total = first_ref[...] + (1.0 - (keep_ref[at_ref[0]] > 0).astype(jnp.float32)) * picked(g_refs, turn).astype(jnp.float32)
    for low, w_ref in ((dq, wq_ref), (dk, wk_ref), (dv, wv_ref)):
        total = total + lax.dot_general(
            low, w_ref[...], (((1,), (1,)), ((), ())), preferred_element_type=jnp.float32
        )
    pos_ref[...] = total
    d_ref[...] = (total * gelu_slope(conv_ref[...])).astype(d_ref.dtype)
    sums = [jnp.sum(low.astype(jnp.float32), 0, keepdims=True) for low in (dq, dk, dv)]

    @pl.when(pl.program_id(0) == 0)
    def _():
        qk_ref[...] = jnp.zeros_like(qk_ref)
        v_ref[...] = jnp.zeros_like(v_ref)

    qk_ref[0:1, :width] += sums[0]
    qk_ref[0:1, width:] += sums[1]
    v_ref[0:1, :] += sums[2]


def dpos(at, keep, dqs, dks, dvs, fars, wq, wk, wv, first, gs, conv_before, deps):
    F, W = first.shape
    n = len(gs)
    rows = F // n
    parts = len(dqs)
    part = pl.BlockSpec((rows, W // parts), lambda i, at, k: (i, 0))
    block = pl.BlockSpec((rows, W), lambda i, at, k: (i, 0))
    whole = pl.BlockSpec((W, W), lambda i, at, k: (0, 0))
    return pl.pallas_call(
        functools.partial(dpos_kernel, parts=parts, far=len(fars[0]), n=n, ndeps=len(deps)),
        grid_spec=pltpu.PrefetchScalarGridSpec(
            num_scalar_prefetch=2,
            grid=(F // rows,),
            in_specs=[part] * (3 * parts)
            + [pl.BlockSpec((2, rows, W // parts), lambda i, at, k: (0, i, 0))] * (parts * len(fars[0]))
            + [whole] * 3 + [block] * 2 + [pl.BlockSpec((rows, W), lambda i, at, k: (0, 0))] * n + [ANY] * len(deps),
            out_specs=[
                pl.BlockSpec((rows, 2 * W), lambda i, at, k: (i, 0)), block, block, block,
                pl.BlockSpec((8, 2 * W), lambda i, at, k: (0, 0)),
                pl.BlockSpec((8, W), lambda i, at, k: (0, 0)),
            ],
        ),
        out_shape=[
            jax.ShapeDtypeStruct((F, 2 * W), jnp.bfloat16),
            jax.ShapeDtypeStruct((F, W), jnp.bfloat16),
            jax.ShapeDtypeStruct((F, W), jnp.float32),
            jax.ShapeDtypeStruct((F, W), jnp.bfloat16),
            jax.ShapeDtypeStruct((8, 2 * W), jnp.float32),
            jax.ShapeDtypeStruct((8, W), jnp.float32),
        ],
        cost_estimate=COST,
        name="dpos",
    )(at, keep, *dqs, *dks, *dvs, *[f for part in fars for f in part], wq, wk, wv, first, conv_before, *gs, *deps)


def front_kernel(conv_ref, bias_ref, x_ref, wq_ref, wk_ref, wv_ref, bq_ref, bv_ref, *refs):
    cb_ref, pos_ref, low_ref, q_ref, kv_ref = refs[-5:]
    before = conv_ref[...].T + bias_ref[...]
    cb_ref[...] = before
    pos = x_ref[...].astype(jnp.float32) + gelu(before)
    pos_ref[...] = pos
    low = pos.astype(jnp.bfloat16)
    low_ref[...] = low
    width = low.shape[1]
    q_ref[...] = (jnp.dot(low, wq_ref[...], preferred_element_type=jnp.float32) + bq_ref[...]).astype(jnp.bfloat16)
    kv_ref[:, :width] = jnp.dot(low, wk_ref[...], preferred_element_type=jnp.float32).astype(jnp.bfloat16)
    kv_ref[:, width:] = (
        jnp.dot(low, wv_ref[...], preferred_element_type=jnp.float32) + bv_ref[...]
    ).astype(jnp.bfloat16)


def front(conv_t, bias, x, wq, wk, wv, bq, bv, deps):
    W, F = conv_t.shape
    rows = min(256, F)
    block = pl.BlockSpec((rows, W), lambda i: (i, 0))
    whole = pl.BlockSpec((W, W), lambda i: (0, 0))
    vec = pl.BlockSpec((1, W), lambda i: (0, 0))
    return pl.pallas_call(
        front_kernel,
        grid=(F // rows,),
        in_specs=[pl.BlockSpec((W, rows), lambda i: (0, i)), vec, block]
        + [whole] * 3 + [vec] * 2 + [ANY] * len(deps),
        out_specs=[block] * 4 + [pl.BlockSpec((rows, 2 * W), lambda i: (i, 0))],
        out_shape=[
            jax.ShapeDtypeStruct((F, W), jnp.float32),
            jax.ShapeDtypeStruct((F, W), jnp.float32),
            jax.ShapeDtypeStruct((F, W), jnp.bfloat16),
            jax.ShapeDtypeStruct((F, W), jnp.bfloat16),
            jax.ShapeDtypeStruct((F, 2 * W), jnp.bfloat16),
        ],
        cost_estimate=COST,
        name="front",
    )(conv_t, bias.reshape(1, W), x, wq, wk, wv, bq.reshape(1, W), bv.reshape(1, W), *deps)


def picked(refs, index):
    out = refs[0][...]
    for m in range(1, len(refs)):
        out = jnp.where(index == m, refs[m][...], out)
    return out


def mid_kernel(at_ref, keep_ref, attn_ref, pos_ref, *refs, n, ndeps, chunk):
    g_refs, refs = refs[:n], refs[n:]
    (wa_ref, wi_ref, wo_ref, ba_ref, g1_ref, s1_ref, bi_ref, bo_ref, g2_ref, s2_ref), refs = refs[:10], refs[10:]
    out_refs, refs = refs[ndeps : ndeps + n], refs[ndeps + n :]
    (
        first_ref, inner_ref, douter_ref, dinner_ref, dattn_ref, dfirst_ref, dheads_ref,
        inner_sum_ref, sums_ref, slope_ref,
    ) = refs
    keep = (keep_ref[at_ref[0]] > 0).astype(jnp.float32)
    turn = (at_ref[2] - pl.program_id(0) + n) % n
    width = pos_ref.shape[1]
    ff = wi_ref.shape[1]
    pos = pos_ref[...]
    attn_out = jnp.dot(attn_ref[...], wa_ref[...], preferred_element_type=jnp.float32) + ba_ref[...]
    first_normed, first_scale = layer_norm(pos + attn_out)
    first_out = first_normed * g1_ref[...] + s1_ref[...]
    first_low = first_out.astype(jnp.bfloat16)
    first_ref[...] = first_low
    total = None
    for c in range(0, ff, chunk):
        cols = slice(c, c + chunk)
        pre = jnp.dot(first_low, wi_ref[:, cols], preferred_element_type=jnp.float32) + bi_ref[:, cols]
        phi = 0.5 * (1.0 + lax.erf(pre * root_half))
        slope_ref[:, cols] = phi + pre * jnp.exp(-0.5 * pre * pre) * inv_root_two_pi
        low = (pre * phi).astype(jnp.bfloat16)
        inner_ref[:, cols] = low
        part = jnp.dot(low, wo_ref[cols, :], preferred_element_type=jnp.float32)
        total = part if total is None else total + part
    second_normed, second_scale = layer_norm(first_out + (total + bo_ref[...]))
    second_out = second_normed * g2_ref[...] + s2_ref[...]
    layer = (keep * second_out + (1.0 - keep) * pos).astype(jnp.bfloat16)
    for m in range(n):
        @pl.when(turn == m)
        def _(m=m):
            out_refs[m][...] = layer

    grad_layer = keep * picked(g_refs, turn).astype(jnp.float32)
    d_second = norm_back(grad_layer * g2_ref[...], second_normed, second_scale)
    d_outer = d_second.astype(jnp.bfloat16)
    douter_ref[...] = d_outer

    @pl.when(pl.program_id(0) == 0)
    def _():
        inner_sum_ref[...] = jnp.zeros_like(inner_sum_ref)
        sums_ref[...] = jnp.zeros_like(sums_ref)

    d_first_out = d_second
    for c in range(0, ff, chunk):
        cols = slice(c, c + chunk)
        d_inner = (
            lax.dot_general(d_outer, wo_ref[cols, :], (((1,), (1,)), ((), ())), preferred_element_type=jnp.float32)
            * slope_ref[:, cols]
        ).astype(jnp.bfloat16)
        dinner_ref[:, cols] = d_inner
        inner_sum_ref[0:1, cols] += jnp.sum(d_inner.astype(jnp.float32), 0, keepdims=True)
        d_first_out = d_first_out + lax.dot_general(
            d_inner, wi_ref[:, cols], (((1,), (1,)), ((), ())), preferred_element_type=jnp.float32
        )
    d_first = norm_back(d_first_out * g1_ref[...], first_normed, first_scale)
    dfirst_ref[...] = d_first
    d_attn = d_first.astype(jnp.bfloat16)
    dattn_ref[...] = d_attn
    dheads_ref[...] = lax.dot_general(
        d_attn, wa_ref[...], (((1,), (1,)), ((), ())), preferred_element_type=jnp.float32
    ).astype(jnp.bfloat16)
    for k, v in enumerate((
        d_attn.astype(jnp.float32), d_first_out * first_normed, d_first_out,
        d_outer.astype(jnp.float32), grad_layer * second_normed, grad_layer,
    )):
        sums_ref[0:1, k * width : (k + 1) * width] += jnp.sum(v, 0, keepdims=True)


def mid(at, keep, attn_low, pos_out, gs, wa, wi, wo, ba, g1, s1, bi, bo, g2, s2, deps):
    F, W = pos_out.shape
    ff = wi.shape[1]
    n = len(gs)
    rows = F // n
    block = pl.BlockSpec((rows, W), lambda i, at, k: (i, 0))
    wide = pl.BlockSpec((rows, ff), lambda i, at, k: (i, 0))

    def whole(*shape):
        return pl.BlockSpec(shape, lambda i, at, k: (0,) * len(shape))

    vec = whole(1, W)
    out = lambda cols, kind: jax.ShapeDtypeStruct((F, cols), kind)
    bf, fl = jnp.bfloat16, jnp.float32
    return pl.pallas_call(
        functools.partial(mid_kernel, n=n, ndeps=len(deps), chunk=min(768, ff)),
        grid_spec=pltpu.PrefetchScalarGridSpec(
            num_scalar_prefetch=2,
            grid=(F // rows,),
            in_specs=[block, block] + [whole(rows, W)] * n + [whole(W, W), whole(W, ff), whole(ff, W), vec, vec, vec, whole(1, ff), vec, vec, vec]
            + [ANY] * len(deps),
            out_specs=[whole(rows, W)] * n + [block, wide, block, wide, block, block, block, whole(8, ff), whole(8, 6 * W)],
            scratch_shapes=[pltpu.VMEM((rows, ff), jnp.float32)],
        ),
        out_shape=[
            *[jax.ShapeDtypeStruct((rows, W), bf)] * n, out(W, bf), out(ff, bf), out(W, bf), out(ff, bf), out(W, bf), out(W, fl), out(W, bf),
            jax.ShapeDtypeStruct((8, ff), fl), jax.ShapeDtypeStruct((8, 6 * W), fl),
        ],
        cost_estimate=COST,
        name="mid",
    )(
        at, keep, attn_low, pos_out, *gs, wa, wi, wo, ba.reshape(1, W), g1.reshape(1, W), s1.reshape(1, W),
        bi.reshape(1, ff), bo.reshape(1, W), g2.reshape(1, W), s2.reshape(1, W), *deps,
    )


def place(ext, before, gaps, length):
    rows, have = ext.shape
    ext = jnp.concatenate([ext, jnp.zeros((rows, length - have), ext.dtype)], 1) if length > have else ext
    if length > have:
        before = jnp.concatenate([before, jnp.full((before.shape[0], length - have), -1, before.dtype)], 1)
    total = None
    for k in range(gaps + 1):
        moved = ext if k == 0 else pltpu.roll(ext, HALO * k, 1)
        here = (before if k == 0 else pltpu.roll(before, HALO * k, 1))[0:1, :] == k
        total = jnp.where(here, moved, jnp.zeros((), ext.dtype) if total is None else total)
    return total


def window_of(seg_ref, wide_ref, row, member, F):
    T = seg_ref.shape[1]
    wide_ref[...] = jnp.zeros_like(wide_ref)
    wide_ref[:, 128 : 128 + T] = jnp.broadcast_to(seg_ref[pl.ds(row % 8, 1), :], (8, T))
    start = pl.multiple_of(member * F, 128)
    window = wide_ref[:, pl.ds(start, F + 256)]
    return pltpu.roll(window, F + 256 - HALO, 1)[:, : F + 2 * HALO]


def ordinals(window, F):
    lane = lax.broadcasted_iota(jnp.int32, window.shape, 1)
    local = (lane >= HALO) & (lane < HALO + F)
    most = jnp.max(jnp.where(local, window, 0), axis=1, keepdims=True)
    first = jnp.sum(jnp.where(lane == HALO, window, 0), axis=1, keepdims=True)
    last = jnp.sum(jnp.where(lane == HALO + F - 1, window, 0), axis=1, keepdims=True)
    number = jnp.where(window > 0, window, most + 1)
    number_first = jnp.where(first > 0, first, most + 1)
    number_last = jnp.where(last > 0, last, most + 1)
    before = number - number_first
    before = jnp.where((lane < HALO) & (window != first), -1, before)
    right = jnp.where(window == last, number_last - number_first, -1)
    return jnp.where(lane >= HALO + F, right, before)


def column(row):
    return row.astype(jnp.float32).T[:, 0:1]


def build_x_kernel(at_ref, seg_ref, *refs, n, nlow, nhigh, team, F, gaps, spread):
    row, member = at_ref[0], at_ref[1]
    j = at_ref[2]
    got, lows, highs = refs[:n], refs[n : n + nlow], refs[n + nlow : n + nlow + nhigh]
    x_ref, spread_ref, sel_ref, qc_ref, kc_ref, wide_ref = refs[-6:]
    zero = jnp.zeros((), jnp.bfloat16)
    blocks = []
    for w in range(n):
        part = got[0][...]
        for m in range(1, n):
            part = jnp.where((j - w + n) % n == m, got[m][...], part)
        blocks.append(part)

    def edge(parts, on):
        part = parts[0][...]
        for m in range(1, len(parts)):
            part = jnp.where(j == m, parts[m][...], part)
        return jnp.where(on, part, zero)

    window = window_of(seg_ref, wide_ref, row, member, F)
    before = ordinals(window, F)
    ext = jnp.concatenate([edge(lows, member > 0)] + blocks + [edge(highs, member < team - 1)], 0)
    ext_t = jnp.where(window[0:1, :] > 0, ext.T, zero)
    spread_ref[...] = place(ext_t, before, gaps, spread)
    local = pltpu.roll(window, F + 2 * HALO - HALO, 1)[:, :F]
    before_local = pltpu.roll(before, F + 2 * HALO - HALO, 1)[:, :F]
    which = lax.broadcasted_iota(jnp.int32, (8, F), 0)
    sel_ref[...] = (before_local == which).astype(jnp.float32)
    seg_col = column(local)
    length = F // n
    for w in range(n):
        rows = slice(w * length, (w + 1) * length)
        x_ref[rows, :] = jnp.where(seg_col[rows] > 0, blocks[w], zero)
    lane = lax.broadcasted_iota(jnp.int32, (1, 128), 1) % 64
    qc_ref[...] = (seg_col == lane.astype(jnp.float32)).astype(jnp.bfloat16)
    for s in range(team):
        start = pl.multiple_of(128 + (member - s + team) % team * F, 128)
        keys = column(wide_ref[:, pl.ds(start, F)])
        kc_ref[s * F : (s + 1) * F, :] = jnp.where(
            (keys == lane.astype(jnp.float32)) & (lane > 0), 0.0, -1e30
        ).astype(jnp.bfloat16)


def build_x(at, segments, got, lows, highs, team, F, gaps, spread, deps):
    n, W = len(got), got[0].shape[1]
    T = segments.shape[1]
    whole = pl.BlockSpec(memory_space=pltpu.VMEM)
    out = lambda r, c, kind: jax.ShapeDtypeStruct((r, c), kind)

    def full(r, c):
        return pl.BlockSpec((r, c), lambda i, at: (0, 0))

    return pl.pallas_call(
        functools.partial(
            build_x_kernel, n=n, nlow=len(lows), nhigh=len(highs), team=team, F=F, gaps=gaps, spread=spread
        ),
        grid_spec=pltpu.PrefetchScalarGridSpec(
            num_scalar_prefetch=1,
            grid=(1,),
            in_specs=[pl.BlockSpec((8, T), lambda i, at: (at[0] // 8, 0))]
            + [full(*a.shape) for a in (*got, *lows, *highs)] + [ANY] * len(deps),
            out_specs=[full(F, W), full(W, spread), full(8, F), full(F, 128), full(team * F, 128)],
            scratch_shapes=[pltpu.VMEM((8, T + 256), jnp.int32)],
        ),
        out_shape=[
            out(F, W, jnp.bfloat16), out(W, spread, jnp.bfloat16), out(8, F, jnp.float32),
            out(F, 128, jnp.bfloat16), out(team * F, 128, jnp.bfloat16),
        ],
        cost_estimate=COST,
        name="build_x",
    )(at, segments, *got, *lows, *highs, *deps)


def build_d_kernel(at_ref, seg_ref, d_ref, *refs, edges, team, F, gaps, length):
    row, member = at_ref[0], at_ref[1]
    out_ref, wide_ref = refs[-2:]
    window = window_of(seg_ref, wide_ref, row, member, F)
    before = ordinals(window, F)
    zero = jnp.zeros((), jnp.bfloat16)
    if edges:
        low, high = refs[0][...], refs[1][...]
        ext = jnp.concatenate(
            [jnp.where(member > 0, low, zero), d_ref[...], jnp.where(member < team - 1, high, zero)], 0
        ).T
    else:
        ext = d_ref[...].T
        before = pltpu.roll(before, F + 2 * HALO - HALO, 1)[:, :F]
    out_ref[...] = place(ext, before, gaps, length)


def build_d(at, segments, d, edges, team, gaps, length, deps=()):
    F, W = d.shape
    T = segments.shape[1]

    def full(r, c):
        return pl.BlockSpec((r, c), lambda i, at: (0, 0))

    return pl.pallas_call(
        functools.partial(build_d_kernel, edges=bool(edges), team=team, F=F, gaps=gaps, length=length),
        grid_spec=pltpu.PrefetchScalarGridSpec(
            num_scalar_prefetch=1,
            grid=(1,),
            in_specs=[pl.BlockSpec((8, T), lambda i, at: (at[0] // 8, 0)), full(F, W)]
            + [full(*a.shape) for a in edges] + [ANY] * len(deps),
            out_specs=full(W, length),
            scratch_shapes=[pltpu.VMEM((8, T + 256), jnp.int32)],
        ),
        out_shape=jax.ShapeDtypeStruct((W, length), jnp.bfloat16),
        cost_estimate=COST,
        name="build_d",
    )(at, segments, d, *edges, *deps)


def widen_kernel(*refs, n):
    for k in range(n):
        refs[len(refs) - n + k][...] = refs[k][...].astype(jnp.float32)


def widen(arrays, deps):
    whole = pl.BlockSpec(memory_space=pltpu.VMEM)
    size = sum(a.size for a in arrays)
    return pl.pallas_call(
        functools.partial(widen_kernel, n=len(arrays)),
        in_specs=[whole] * len(arrays) + [ANY] * len(deps),
        out_specs=[whole] * len(arrays),
        out_shape=[jax.ShapeDtypeStruct(a.shape, jnp.float32) for a in arrays],
        cost_estimate=COST,
        name="widen",
    )(*arrays, *deps)


def grad_in_kernel(at_ref, seg_ref, pos_ref, *refs, n, nback, F):
    backs, out_refs, wide_ref = refs[:nback], refs[-1 - n : -1], refs[-1]
    window = window_of(seg_ref, wide_ref, at_ref[0], at_ref[1], F)
    live = column(pltpu.roll(window, F + 2 * HALO - HALO, 1)[:, :F]) > 0
    back = jnp.concatenate([b[...] for b in backs], 0).T
    total = jnp.where(live, pos_ref[...] + back, 0.0).astype(jnp.bfloat16)
    rows = F // n
    for w in range(n):
        for m in range(n):
            @pl.when((at_ref[2] - w + n) % n == m)
            def _(w=w, m=m):
                out_refs[m][...] = total[w * rows : (w + 1) * rows, :]


def grad_in(at, segments, pos, backs, n, deps):
    F, W = pos.shape
    T = segments.shape[1]

    def full(r, c):
        return pl.BlockSpec((r, c), lambda i, at: (0, 0))

    return pl.pallas_call(
        functools.partial(grad_in_kernel, n=n, nback=len(backs), F=F),
        grid_spec=pltpu.PrefetchScalarGridSpec(
            num_scalar_prefetch=1,
            grid=(1,),
            in_specs=[pl.BlockSpec((8, T), lambda i, at: (at[0] // 8, 0)), full(F, W)]
            + [full(*b.shape) for b in backs] + [ANY] * len(deps),
            out_specs=[full(F // n, W)] * n,
            scratch_shapes=[pltpu.VMEM((8, T + 256), jnp.int32)],
        ),
        out_shape=[jax.ShapeDtypeStruct((F // n, W), jnp.bfloat16)] * n,
        cost_estimate=COST,
        name="grad_in",
    )(at, segments, pos, *backs, *deps)

HEAD = 64

def nt(a, b):
    return lax.dot_general(a, b, (((1,), (1,)), ((), ())), preferred_element_type=jnp.float32)

def attn_fwd_kernel(*refs, P, chunk):
    q_ref, qc_ref, kc_ref = refs[:3]
    k_refs = refs[3:3+P]
    v_refs = refs[3+P:3+2*P]
    o_ref, lse_ref, ka_ref, va_ref = refs[-4:]
    F = q_ref.shape[0]
    low_k = lax.broadcasted_iota(jnp.int32, (F, 128), 1) < HEAD
    low_q = lax.broadcasted_iota(jnp.int32, (chunk, 128), 1) < HEAD
    one = jnp.ones((), jnp.bfloat16)
    for h in range(2):
        pick = low_k if h == 0 else jnp.logical_not(low_k)
        for p in range(P):
            ka_ref[h, p*F:(p+1)*F, :] = jnp.where(pick, k_refs[p][...], kc_ref[p*F:(p+1)*F, :])
            va_ref[h, p*F:(p+1)*F, :] = jnp.where(pick, v_refs[p][...], one)
    for c in range(F // chunk):
        rows = slice(c*chunk, (c+1)*chunk)
        q = q_ref[rows, :] * jnp.asarray(0.125, jnp.bfloat16)
        outs, lses = [], []
        for h in range(2):
            pick = low_q if h == 0 else jnp.logical_not(low_q)
            qa = jnp.where(pick, q, qc_ref[rows, :])
            s = nt(qa, ka_ref[h])
            m = jnp.maximum(jnp.max(s, axis=1, keepdims=True), -1e20)
            e = jnp.exp(s - m).astype(jnp.bfloat16)
            o = jnp.dot(e, va_ref[h], preferred_element_type=jnp.float32)
            l = jnp.maximum(o[:, HEAD:HEAD+1] if h == 0 else o[:, 0:1], 1.0)
            outs.append(o * (1.0 / l))
            lses.append(m + jnp.log(l))
        o_ref[rows, :] = jnp.where(low_q, outs[0], outs[1]).astype(o_ref.dtype)
        lse_ref[rows, :] = jnp.where(low_q, lses[0], lses[1])

def attn_fwd(q, kvs, qc, kc, deps, chunk=128):
    F, W = q.shape
    P = len(kvs)
    T = P * F
    npair = W // 128
    return pl.pallas_call(
        functools.partial(attn_fwd_kernel, P=P, chunk=min(chunk, F)),
        grid=(npair,),
        in_specs=[pl.BlockSpec((F, 128), lambda a: (0, a)),
                  pl.BlockSpec((F, 128), lambda a: (0, 0)),
                  pl.BlockSpec((T, 128), lambda a: (0, 0))]
                 + [pl.BlockSpec((F, 128), lambda a: (0, a))] * P
                 + [pl.BlockSpec((F, 128), lambda a, n=npair: (0, a + n))] * P
                 + [ANY] * len(deps),
        out_specs=[pl.BlockSpec((F, 128), lambda a: (0, a)), pl.BlockSpec((F, 128), lambda a: (0, a))],
        out_shape=[jax.ShapeDtypeStruct((F, W), jnp.bfloat16), jax.ShapeDtypeStruct((F, W), jnp.float32)],
        scratch_shapes=[pltpu.VMEM((2, T, 128), jnp.bfloat16), pltpu.VMEM((2, T, 128), jnp.bfloat16)],
        cost_estimate=COST,
        name="attn_fwd",
    )(q, qc, kc, *kvs, *kvs, *deps)

def attn_bwd_kernel(*refs, P, chunk):
    q_ref, do_ref, o_ref, lse_ref, qc_ref, kc_ref = refs[:6]
    k_refs = refs[6:6+P]
    v_refs = refs[6+P:6+2*P]
    dq_ref, dk_ref, dv_ref = refs[-2-P:1-P]
    far_refs = refs[1-P:]
    F = q_ref.shape[0]
    low_q = lax.broadcasted_iota(jnp.int32, (F, 128), 1) < HEAD
    low_c = lax.broadcasted_iota(jnp.int32, (chunk, 128), 1) < HEAD
    q = q_ref[...] * jnp.asarray(0.125, jnp.bfloat16)
    do = do_ref[...]
    lse_t = lse_ref[...].T
    prod_t = (do.astype(jnp.float32) * o_ref[...].astype(jnp.float32)).T
    lse_row = [lse_t[h*HEAD:h*HEAD+1, :] for h in range(2)]
    delta_row = [jnp.sum(prod_t[h*HEAD:(h+1)*HEAD, :], axis=0, keepdims=True) for h in range(2)]
    qa = [jnp.where(low_q if h == 0 else jnp.logical_not(low_q), q, qc_ref[...]) for h in range(2)]
    zero = jnp.zeros((), jnp.bfloat16)
    dqt = [jnp.zeros((HEAD, F), jnp.float32) for _ in range(2)]
    for p in range(P):
        for c in range(F // chunk):
            rows = slice(c*chunk, (c+1)*chunk)
            k = k_refs[p][rows, :]
            v = v_refs[p][rows, :]
            kc = kc_ref[p*F + c*chunk: p*F + (c+1)*chunk, :]
            kt = k.T
            dks, dvs = [], []
            for h in range(2):
                pick = low_c if h == 0 else jnp.logical_not(low_c)
                st = nt(jnp.where(pick, k, kc), qa[h])
                pt = jnp.exp(st - lse_row[h])
                dpt = nt(jnp.where(pick, v, zero), do)
                dst = (pt * (dpt - delta_row[h])).astype(jnp.bfloat16)
                dvs.append(jnp.dot(pt.astype(jnp.bfloat16), do, preferred_element_type=jnp.float32))
                dks.append(jnp.dot(dst, q, preferred_element_type=jnp.float32))
                dqt[h] = dqt[h] + jnp.dot(kt[h*HEAD:(h+1)*HEAD, :], dst, preferred_element_type=jnp.float32)
            dk = jnp.where(low_c, dks[0], dks[1])
            dv = jnp.where(low_c, dvs[0], dvs[1])
            if p == 0:
                dk_ref[rows, :] = dk
                dv_ref[rows, :] = dv
            else:
                far_refs[p-1][0, rows, :] = dk.astype(jnp.bfloat16)
                far_refs[p-1][1, rows, :] = dv.astype(jnp.bfloat16)
    dq = jnp.concatenate(dqt, axis=0).T * 0.125
    dq_ref[...] = dq.astype(dq_ref.dtype)

def attn_bwd(q, do, o, lse, kvs, qc, kc, first, count, deps, chunk=128):
    F, W = q.shape
    P = len(kvs)
    T = P * F
    npair = W // 128
    own = pl.BlockSpec((F, 128), lambda a: (0, a + first))
    out = pl.BlockSpec((F, 128), lambda a: (0, a))
    return pl.pallas_call(
        functools.partial(attn_bwd_kernel, P=P, chunk=min(chunk, F)),
        grid=(count,),
        in_specs=[own, own, own, own,
                  pl.BlockSpec((F, 128), lambda a: (0, 0)),
                  pl.BlockSpec((T, 128), lambda a: (0, 0))]
                 + [own] * P
                 + [pl.BlockSpec((F, 128), lambda a, n=npair: (0, a + first + n))] * P
                 + [ANY] * len(deps),
        out_specs=[out] * 3 + [pl.BlockSpec((2, F, 128), lambda a: (0, 0, a))] * (P - 1),
        out_shape=[jax.ShapeDtypeStruct((F, 128 * count), t) for t in (jnp.bfloat16, jnp.float32, jnp.float32)]
                  + [jax.ShapeDtypeStruct((2, F, 128 * count), jnp.bfloat16)] * (P - 1),
        cost_estimate=COST,
        name="attn_bwd",
    )(q, do, o, lse, qc, kc, *kvs, *kvs, *deps)

HALO = 64
UTT_LEAST = 256
root_half = 0.7071067811865476
inv_root_two_pi = 0.3989422804014327
f32 = jnp.float32
bf16 = jnp.bfloat16


def layer_norm(hidden):
    centred = hidden - jnp.mean(hidden, axis=-1, keepdims=True)
    inv_scale = lax.rsqrt(jnp.mean(centred * centred, axis=-1, keepdims=True) + 1e-05)
    return (centred * inv_scale, inv_scale)


def norm_back(grad_normed, normed, inv_scale):
    return inv_scale * (
        grad_normed
        - jnp.mean(grad_normed, axis=-1, keepdims=True)
        - normed * jnp.mean(grad_normed * normed, axis=-1, keepdims=True)
    )


def gelu(entries):
    return 0.5 * entries * (1.0 + lax.erf(entries * root_half))


def gelu_slope(entries):
    return (
        0.5 * (1.0 + lax.erf(entries * root_half))
        + entries * jnp.exp(-0.5 * entries * entries) * inv_root_two_pi
    )


def mm(a, b):
    return jnp.dot(a, b, preferred_element_type=f32)


def mm_back(a, b):
    return lax.dot_general(a, b, (((1,), (1,)), ((), ())), preferred_element_type=f32)


def wgrad(a, b):
    return lax.dot_general(a, b, (((0,), (0,)), ((), ())), preferred_element_type=f32)


class Plan:
    def __init__(self, dp, seq, rows_dev):
        self.dp, self.seq, self.n = dp, seq, rows_dev
        self.q = seq // (2 * rows_dev)
        self.P = 2 * self.q
        assert dp % 2 == 0 and self.q * 2 * rows_dev == seq and rows_dev > 1

    def out_pairs(self, m):
        pairs = []
        for d in range(self.dp):
            for z in range(self.seq):
                rho = self.n * (d % 2) + (z + m) % self.n
                u = z // self.n
                pairs.append((d * self.seq + z, self.member(d // 2, rho, u)))
        return pairs

    def edge_pairs(self):
        heads = [[] for _ in range(self.n)]
        tails = [[] for _ in range(self.n)]
        for d in range(self.dp):
            for z in range(self.seq):
                u = z // self.n
                for j in range(self.n):
                    rho = self.n * (d % 2) + j
                    if z % self.n == self.n - 1 and u + 1 < self.P:
                        tails[j].append((d * self.seq + z, self.member(d // 2, rho, u + 1)))
                    if z % self.n == 0 and u > 0:
                        heads[j].append((d * self.seq + z, self.member(d // 2, rho, u - 1)))
        return heads, tails

    def member(self, e, rho, u):
        return (2 * e + u % 2) * self.seq + rho * self.q + u // 2

    def team_pairs(self, shift, wrap):
        pairs = []
        for e in range(self.dp // 2):
            for rho in range(2 * self.n):
                for u in range(self.P):
                    to = u + shift
                    if wrap or 0 <= to < self.P:
                        pairs.append((self.member(e, rho, u), self.member(e, rho, to % self.P)))
        return pairs


BOTH = ("dp", "seq")


def on_device(
    frames,
    output_gradient,
    segments,
    layer_keep,
    conv_weight,
    convolution_bias,
    query_matrix,
    query_offset_bias,
    key_matrix,
    value_matrix,
    value_offset_bias,
    attn_weight,
    attn_bias,
    first_gain,
    first_shift,
    inner_weight,
    inner_bias,
    outer_weight,
    outer_bias,
    second_gain,
    second_shift,
):
    rows_dev, local_len, width = frames.shape
    total_rows, row_len = segments.shape
    dp_count, seq_count = lax.axis_size("dp"), lax.axis_size("seq")
    dp_index, seq_index = lax.axis_index("dp"), lax.axis_index("seq")
    plan = Plan(dp_count, seq_count, rows_dev)
    n, q, team = plan.n, plan.q, plan.P
    F = row_len // team
    taps, _, gw = conv_weight.shape
    tap_blocks = taps // DK
    rho = seq_index // q
    member = (seq_index % q) * 2 + dp_index % 2
    row_id = (dp_index // 2) * (2 * n) + rho

    def pick(parts, index):
        out = parts[0]
        for k in range(1, len(parts)):
            out = jnp.where(index == k, parts[k], out)
        return out

    def blocks_to_team(a):
        got = []
        for m in range(n):
            sent = pick([a[j] for j in range(n)], (seq_index + m) % n)
            got.append(lax.ppermute(sent, BOTH, plan.out_pairs(m)))
        return got

    def from_team(sent):
        back = [
            lax.ppermute(sent[m], BOTH, [(t, s) for s, t in plan.out_pairs(m)]) for m in range(n)
        ]
        return jnp.stack([pick(back, (row - seq_index) % n) for row in range(n)], 0)

    def edges_to_team(a):
        heads, tails = plan.edge_pairs()
        lows, highs = [], []
        for j in range(n):
            tail, head = a[j, local_len - HALO :], a[j, :HALO]
            if team == 2:
                got = lax.ppermute(
                    jnp.where(seq_index % n == 0, head, tail), BOTH, heads[j] + tails[j]
                )
                lows.append(got)
                highs.append(got)
            else:
                lows.append(lax.ppermute(tail, BOTH, tails[j]))
                highs.append(lax.ppermute(head, BOTH, heads[j]))
        return lows, highs

    def edges(a):
        if team == 2:
            got = lax.ppermute(
                jnp.where(member == 0, a[F - HALO :], a[:HALO]), BOTH, plan.team_pairs(1, True)
            )
            return got, got
        low = lax.ppermute(a[F - HALO :], BOTH, plan.team_pairs(1, False))
        high = lax.ppermute(a[:HALO], BOTH, plan.team_pairs(-1, False))
        return low, high

    def pairs_of(axis, bit):
        pairs = []
        for d in range(dp_count):
            for z in range(seq_count):
                to = (d ^ bit, z) if axis == "dp" else (d, z ^ bit)
                pairs.append((d * seq_count + z, to[0] * seq_count + to[1]))
        return pairs

    def halve(a, axis, index, bit, high, low):
        mine = (index // bit) % 2
        a = a.reshape((high, 2, low) + a.shape[1:])
        sent = pick([a[:, 0], a[:, 1]], 1 - mine).reshape((high * low,) + a.shape[3:])
        kept = pick([a[:, 0], a[:, 1]], mine).reshape(sent.shape)
        return kept, lax.ppermute(sent, BOTH, pairs_of(axis, bit)), sent

    class Scatter:
        def __init__(self, halves, swap, many=1):
            bits = [1 << i for i in range(dp_count.bit_length() - 1)]
            order = [1] + (bits[1:] if swap else bits[:0:-1])
            left = list(reversed(bits))
            self.steps = []
            for bit in order:
                at = left.index(bit)
                self.steps.append((bit, many * 2**at, 2 ** (len(left) - 1 - at)))
                left.remove(bit)
            self.steps.pop(0)
            self.sent, self.kept = halves
            self.got = lax.ppermute(self.sent, BOTH, pairs_of("dp", 1))

        def step(self, *deps):
            bit, high, low = self.steps.pop(0)
            mine = ((dp_index // bit) % 2).astype(jnp.int32).reshape(1)
            self.sent, self.kept = join_split(self.kept, self.got, mine, high, low, deps)
            self.got = lax.ppermute(self.sent, BOTH, pairs_of("dp", bit))

        def last(self, *deps):
            while self.steps:
                self.step(*deps)
            return join_last(self.kept, self.got, deps)

    class SeqSum:
        def __init__(self, a):
            self.shape = a.shape
            self.a = a.astype(bf16).reshape(seq_count, -1, a.shape[1])
            bits = [1 << i for i in range(seq_count.bit_length() - 1)]
            left = list(reversed(bits))
            self.steps = []
            for bit in bits:
                at = left.index(bit)
                self.steps.append((bit, 2**at, 2 ** (len(left) - 1 - at)))
                left.remove(bit)
            self.back = list(reversed(bits))
            bit, high, low = self.steps.pop(0)
            self.kept, self.got, self.sent = halve(self.a, "seq", seq_index, bit, high, low)

        def step(self, *deps):
            if self.steps:
                bit, high, low = self.steps.pop(0)
                mine = ((seq_index // bit) % 2).astype(jnp.int32).reshape(1)
                self.sent, self.kept = join_split(self.kept, self.got, mine, high, low, deps)
                self.got = lax.ppermute(self.sent, BOTH, pairs_of("seq", bit))

        def whole(self):
            self.add()
            return self.finish()

        def add(self, *deps):
            while self.steps:
                self.step(*deps)
            self.a = join_last(self.kept, self.got, deps).reshape(self.kept.shape)

        def finish(self, *deps):
            a = self.a
            for bit in self.back:
                other = lax.ppermute(a, BOTH, pairs_of("seq", bit))
                low_half = (seq_index // bit) % 2 == 0
                pair = jnp.where(low_half, jnp.stack([a, other], 1), jnp.stack([other, a], 1))
                a = pair.reshape((-1,) + a.shape[1:])
            return a.reshape(self.shape)

    def by_dp(a):
        return a.reshape(dp_count, -1, a.shape[-1])

    def by_share(a):
        a = a.reshape(dp_count, width // dp_count, a.shape[1])
        out, sent = [], []
        for k in range(dp_count):
            piece = lax.dynamic_index_in_dim(a, dp_index ^ k, 0, keepdims=False)
            sent.append(piece)
            out.append(piece if k == 0 else lax.ppermute(piece, BOTH, pairs_of("dp", k)))
        return out, sent

    weight_tr = prep(conv_weight)

    x_blocks = blocks_to_team(frames)
    x_lows, x_highs = edges_to_team(frames)
    g_blocks = blocks_to_team(output_gradient)

    gaps = 1 + max(F - 2, 0) // UTT_LEAST
    spread = -(-(F + 2 * HALO + HALO * gaps) // 128) * 128
    out_spread = -(-(F + HALO * gaps) // 128) * 128
    (
        convolution_bias, query_offset_bias, value_offset_bias, attn_bias, first_gain, first_shift,
        inner_bias, outer_bias, second_gain, second_shift,
    ) = vectors = [
        v.reshape(1, -1)
        for v in (
            convolution_bias, query_offset_bias, value_offset_bias, attn_bias, first_gain, first_shift,
            inner_bias, outer_bias, second_gain, second_shift,
        )
    ]
    where_at = jnp.stack([row_id, member, rho % n]).astype(jnp.int32)
    x, spread_x, select, q_codes, k_codes = build_x(
        where_at, segments, x_blocks, x_lows, x_highs, team, F, gaps, spread, (weight_tr, *vectors)
    )
    conv_t = conv(spread_x, weight_tr, select, F, gaps)
    x_shares = lax.all_to_all(
        spread_x.reshape(dp_count, width // dp_count, spread), "dp", 0, 0, tiled=True
    )

    conv_before, pos_out, pos_low, query, kv = front(
        conv_t, convolution_bias, x, query_matrix, key_matrix, value_matrix, query_offset_bias,
        value_offset_bias, (x_shares, *g_blocks),
    )
    kvs = [kv] + [lax.ppermute(kv, BOTH, plan.team_pairs(s, True)) for s in range(1, team)]
    attn_low, lse = attn_fwd(query, kvs, q_codes, k_codes, (), 256)

    outs = mid(
        where_at, layer_keep, attn_low, pos_out, g_blocks, attn_weight, inner_weight, outer_weight,
        attn_bias, first_gain, first_shift, inner_bias, outer_bias, second_gain, second_shift, (),
    )
    layer_out = from_team(outs[:n])
    (
        first_low, inner_low, grad_outer_low, grad_inner_low, grad_attn_low, grad_first_sum,
        grad_heads, inner_sums, mid_sums,
    ) = outs[n:]
    core = (dp_index % 2).astype(jnp.int32).reshape(1)
    ff_share = inner_weight.shape[1] // dp_count
    by_rows = ff_share % 128 != 0
    outer_t = wg_plain(grad_outer_low, inner_low, 4, 0)
    if by_rows:
        inner_t = wg_plain(grad_inner_low, first_low, 1, 0, (outer_t,))
    else:
        inner_t = wg_plain(first_low, grad_inner_low, 4, ff_share, (outer_t,)).reshape(-1, ff_share)
    outer_share = lax.psum_scatter(outer_t, "dp", scatter_dimension=0, tiled=True)
    inner_share = lax.psum_scatter(inner_t, "dp", scatter_dimension=0, tiled=True)
    extras = (inner_sums, mid_sums)
    pairs = width // 128
    grads = []
    deps = (outer_t, inner_t)
    grads.append(attn_bwd(query, grad_heads, attn_low, lse, kvs, q_codes, k_codes, 0, pairs, deps, 256))
    fars = [
        [lax.ppermute(g[2 + s], BOTH, plan.team_pairs(-s, True)) for s in range(1, team)]
        for g in grads
    ]
    low_qk, low_v, grad_pos, grad_conv_low, qk_sums, v_sums = dpos(
        where_at, layer_keep, *[[g[k] for g in grads] for k in range(3)], fars, query_matrix,
        key_matrix, value_matrix, grad_first_sum, g_blocks, conv_before, (),
    )

    d_pieces = build_d(where_at, segments, grad_conv_low, (), team, gaps, out_spread).reshape(
        dp_count, width // dp_count, out_spread
    )
    d_shares = lax.all_to_all(d_pieces, "dp", 0, 0, tiled=True)
    low, high = edges(grad_conv_low)
    slots = 2 * dp_count // 2
    qk_sum = Scatter(
        wg_rows(core, low_qk, pos_low, 2, dp_count, 1, (qk_sums,), (d_pieces,)), True, 2
    )
    halves = wg_rows(core, low_v, pos_low, 1, dp_count, 1, (v_sums,), (qk_sum.sent,), slots)
    halves = wg_rows(core, grad_attn_low, attn_low, 1, dp_count, 1, extras, (), slots, 1, halves)
    va_sum = Scatter(halves, False, 2)
    part = conv_dw(x_shares, d_shares, gw, tap_blocks, (va_sum.sent,))
    conv_sum = SeqSum(part)
    qk_sum.step(conv_sum.sent)
    va_sum.step(qk_sum.sent)
    spread_d = build_d(
        where_at, segments, grad_conv_low, (low, high), team, gaps, spread, (va_sum.sent,)
    )
    groups = width // gw
    outer_z = SeqSum(outer_share)
    back_a = conv_dx(
        spread_d, weight_tr, select, F, gaps, 0, groups // 2, (outer_z.sent,)
    )
    conv_sum.step(back_a)
    inner_z = SeqSum(inner_share)
    outer_z.step(conv_sum.sent)
    qk_sum.step(outer_z.sent)
    va_sum.step(qk_sum.sent)
    back_b = conv_dx(
        spread_d, weight_tr, select, F, gaps, groups // 2, groups - groups // 2,
        (va_sum.sent, inner_z.sent),
    )
    conv_sum.add(back_b, layer_out)
    outer_z.add(conv_sum.a)
    sent = grad_in(where_at, segments, grad_pos, (back_a, back_b), n, (outer_z.a,))
    qk_share = qk_sum.last(sent[0])
    va_share = va_sum.last(qk_share)
    proj = SeqSum(jnp.concatenate([qk_share, va_share], 0))
    grad_input = from_team(sent)
    inner_z.step(proj.sent)
    proj.step(inner_z.sent)
    outer_sum = outer_z.finish()
    conv_sum = conv_sum.finish()
    inner_z.add(proj.sent)
    proj.add(inner_z.a)
    grad_conv_weight = finish_dw(conv_sum, gw, tap_blocks)
    proj_pack = proj.finish().astype(f32)
    grad_conv_bias = conv_sum.reshape(-1, tap_blocks * gw + 32, DK * gw)[:, tap_blocks * gw, :gw].reshape(-1).astype(f32)
    o_g, i_g = widen((outer_sum, inner_z.finish()), (grad_conv_bias,))
    o_g = o_g.T
    i_g = i_g.T if by_rows else i_g

    share = width // dp_count
    ff = inner_bias.shape[1]
    pieces = proj_pack.reshape(4, -1, width)
    q_g, k_g, v_g, a_g = (pieces[k, :share].T for k in range(4))
    small = pieces[3, share : share + ff // width + 6]
    inner_bias_share = lax.dynamic_slice_in_dim(
        small[: ff // width].reshape(-1), dp_index * (ff // dp_count), ff // dp_count
    )
    rows_ = jnp.concatenate(
        [small[ff // width :], pieces[0, share : share + 1], pieces[2, share : share + 1]]
    )
    rows_ = lax.dynamic_slice_in_dim(rows_, dp_index * share, share, 1)
    vecs = [rows_[6], rows_[7]] + [rows_[k] for k in range(6)] + [grad_conv_bias]
    return (
        layer_out,
        grad_input,
        grad_conv_weight,
        vecs[8],
        q_g,
        vecs[0],
        k_g,
        v_g,
        vecs[1],
        a_g,
        vecs[2],
        vecs[3],
        vecs[4],
        i_g,
        inner_bias_share,
        o_g,
        vecs[5],
        vecs[6],
        vecs[7],
    )


def solution(mesh):
    rows = P("dp", "seq", None)
    by_col, vec = P(None, "dp"), P("dp")
    out_specs = (
        rows, rows, P(None, "dp", None), vec, by_col, vec, by_col, by_col, vec, by_col, vec, vec,
        vec, by_col, vec, by_col, vec, vec, vec,
    )
    return jax.shard_map(
        on_device, mesh=mesh, in_specs=(rows, rows) + (P(),) * 19, out_specs=out_specs, check_vma=False
    )
```

```python
import functools
import jax
import jax.numpy as jnp
from jax import lax
from jax.experimental import pallas as pl
from jax.experimental.pallas import tpu as pltpu
from jax.sharding import PartitionSpec as P


DK = 16
COST = pl.CostEstimate(flops=1000, bytes_accessed=1000, transcendentals=0)
ANY = pl.BlockSpec(memory_space=pl.ANY)

def prep_kernel(w_ref, wt_ref):
    gw = w_ref.shape[1]
    slots = w_ref.shape[2] // gw
    lane = lax.broadcasted_iota(jnp.int32, (gw, 128), 1)
    tiles = w_ref.shape[2] // 128
    for half in range(DK // slots):
        sums = [[None] * tiles for _ in range(slots)]
        for slot in range(slots):
            w = w_ref[half * slots + slot]
            for g in range(slots):
                turn = (slot - g) % slots
                moved = w if turn == 0 else pltpu.roll(w, gw * turn, 1)
                for t in range(tiles):
                    lo, hi = gw * slot - 128 * t, gw * (slot + 1) - 128 * t
                    if hi <= 0 or lo >= 128:
                        continue
                    part = moved[:, 128 * t : 128 * (t + 1)]
                    old = sums[g][t]
                    sums[g][t] = part if old is None else jnp.where(lane >= lo, part, old)
        for g in range(slots):
            for t in range(tiles):
                at = half * slots * gw + 128 * t
                wt_ref[g, :, at : at + 128] = sums[g][t]


def prep(w):
    k, width, gw = w.shape
    groups = width // gw
    nb = k // DK
    slots = 8
    assert (slots * gw) % 128 == 0 and DK % slots == 0 and groups % slots == 0
    return pl.pallas_call(
        prep_kernel,
        grid=(groups // slots, nb),
        in_specs=[pl.BlockSpec((DK, gw, slots * gw), lambda i, b: (b, 0, i))],
        out_specs=pl.BlockSpec((slots, gw, DK * gw), lambda i, b: (i, b, 0)),
        out_shape=jax.ShapeDtypeStruct((groups, nb * gw, DK * gw), w.dtype),
        cost_estimate=COST,
        name="prep",
    )(jnp.transpose(w, (0, 2, 1)))

def ungap(acc, sel_ref, F, nbound):
    out = acc[:, :F]
    for n in range(1, nbound + 1):
        moved = pltpu.roll(acc, acc.shape[1] - HALO * n, 1)[:, :F]
        out = jnp.where(sel_ref[n : n + 1, :] > 0, moved, out)
    return out


def conv_kernel(xt_ref, wt_ref, sel_ref, out_ref, *refs, nb, gw, F, nbound, G):
    stacks, sums = refs[:G], refs[G:]
    tin = xt_ref.shape[1]
    for g in range(G):
        x = xt_ref[g*gw:(g+1)*gw, :]
        for dk in range(DK):
            stacks[g][gw*dk:gw*(dk+1), :] = x if dk == 0 else pltpu.roll(x, tin - dk, 1)
    for g in range(G):
        sums[g][...] = jnp.dot(wt_ref[g], stacks[g][...], preferred_element_type=jnp.float32)
    for g in range(G):
        acc = sums[g][0:gw, :]
        for b in range(1, nb):
            acc = acc + pltpu.roll(sums[g][gw*b:gw*(b+1), :], tin - DK*b, 1)
        out_ref[g*gw:(g+1)*gw, :] = ungap(acc, sel_ref, F, nbound)


def conv(xt, wt, sel, F, nbound, G=2):
    width, tin = xt.shape
    g, nbgw, dkgw = wt.shape
    gw = width // g
    return pl.pallas_call(
        functools.partial(conv_kernel, nb=nbgw // gw, gw=gw, F=F, nbound=nbound, G=G),
        grid=(g // G,),
        in_specs=[pl.BlockSpec((G*gw, tin), lambda i: (i, 0)),
                  pl.BlockSpec((G, nbgw, dkgw), lambda i: (i, 0, 0)),
                  pl.BlockSpec(sel.shape, lambda i: (0, 0))],
        out_specs=pl.BlockSpec((G*gw, F), lambda i: (i, 0)),
        out_shape=jax.ShapeDtypeStruct((width, F), jnp.float32),
        scratch_shapes=[pltpu.VMEM((dkgw, tin), jnp.bfloat16)] * G + [pltpu.VMEM((nbgw, tin), jnp.float32)] * G,
        cost_estimate=COST,
        name="conv_fwd",
    )(xt, wt, sel)


def dx_kernel(dt_ref, wt_ref, sel_ref, *refs, nb, gw, F, nbound, G):
    out_ref, refs = refs[-1 - 2*G], refs[-2*G:]
    stacks, sums = refs[:G], refs[G:]
    tin = dt_ref.shape[1]
    for g in range(G):
        d = dt_ref[g*gw:(g+1)*gw, :]
        for b in range(nb):
            stacks[g][gw*b:gw*(b+1), :] = d if b == 0 else pltpu.roll(d, DK*b, 1)
    for g in range(G):
        sums[g][...] = jnp.dot(wt_ref[g].T, stacks[g][...], preferred_element_type=jnp.float32)
    for g in range(G):
        acc = sums[g][0:gw, :]
        for dk in range(1, DK):
            acc = acc + pltpu.roll(sums[g][gw*dk:gw*(dk+1), :], dk, 1)
        out_ref[g*gw:(g+1)*gw, :] = ungap(acc[:, 2*HALO:], sel_ref, F, nbound)


def conv_dx(dt, wt, sel, F, nbound, first, count, deps, G=2):
    width, tin = dt.shape
    g, nbgw, dkgw = wt.shape
    gw = width // g
    first = first // G
    return pl.pallas_call(
        functools.partial(dx_kernel, nb=nbgw // gw, gw=gw, F=F, nbound=nbound, G=G),
        grid=(count // G,),
        in_specs=[pl.BlockSpec((G*gw, tin), lambda i: (i + first, 0)),
                  pl.BlockSpec((G, nbgw, dkgw), lambda i: (i + first, 0, 0)),
                  pl.BlockSpec(sel.shape, lambda i: (0, 0))] + [ANY] * len(deps),
        out_specs=pl.BlockSpec((G*gw, F), lambda i: (i, 0)),
        out_shape=jax.ShapeDtypeStruct((count * gw, F), jnp.float32),
        scratch_shapes=[pltpu.VMEM((nbgw, tin), jnp.bfloat16)] * G + [pltpu.VMEM((dkgw, tin), jnp.float32)] * G,
        cost_estimate=COST,
        name="conv_dx",
    )(dt, wt, sel, *deps)


def dw_kernel(*refs, nb, gw, m):
    x_refs, d_refs = refs[:m], refs[m : 2 * m]
    out_ref, a0_ref, ds_ref = refs[-3:]
    tin = x_refs[0].shape[2]
    tout = d_refs[0].shape[2]
    ones = jnp.ones((16, tout), jnp.bfloat16)
    bias = None
    for s in range(m):
        x, d = x_refs[s][0], d_refs[s][0]
        part = lax.dot_general(ones, d, (((1,), (1,)), ((), ())), preferred_element_type=jnp.float32)
        bias = part if bias is None else bias + part
        d = jnp.concatenate([d, jnp.zeros((gw, tin - tout), d.dtype)], axis=1)
        slot = s % 2
        for dk in range(DK):
            a0_ref[slot, gw*dk:gw*(dk+1), :] = x if dk == 0 else pltpu.roll(x, tin - dk, 1)
        for b in range(nb):
            ds_ref[slot, gw*b:gw*(b+1), :] = d if b == 0 else pltpu.roll(d, DK*b, 1)
        p = lax.dot_general(
            ds_ref[slot], a0_ref[slot], (((1,), (1,)), ((), ())), preferred_element_type=jnp.float32
        )
        if s == 0:
            out_ref[: nb*gw, :] = p
        else:
            out_ref[: nb*gw, :] += p
    out_ref[nb*gw :, :] = jnp.zeros((out_ref.shape[0] - nb*gw, out_ref.shape[1]), jnp.float32)
    out_ref[nb*gw : nb*gw + 16, :gw] = bias


def conv_dw(xs, ds, gw, nb, deps):
    m, channels, tin = xs.shape
    tout = ds.shape[2]
    rows = nb*gw + 32
    flops = 2 * m * nb*gw * DK*gw * tin
    return pl.pallas_call(
        functools.partial(dw_kernel, nb=nb, gw=gw, m=m),
        grid=(channels // gw,),
        in_specs=[pl.BlockSpec((1, gw, tin), lambda i, k=k: (k, i, 0)) for k in range(m)]
        + [pl.BlockSpec((1, gw, tout), lambda i, k=k: (k, i, 0)) for k in range(m)]
        + [ANY] * len(deps),
        out_specs=pl.BlockSpec((rows, DK*gw), lambda i: (i, 0)),
        scratch_shapes=[pltpu.VMEM((2, DK*gw, tin), jnp.bfloat16), pltpu.VMEM((2, nb*gw, tin), jnp.bfloat16)],
        out_shape=jax.ShapeDtypeStruct((channels // gw * rows, DK*gw), jnp.float32),
        cost_estimate=COST,
        name="conv_dw",
    )(*([xs] * m), *([ds] * m), *deps)


def join_kernel(mine_ref, ks_ref, kk_ref, gs_ref, gk_ref, *refs):
    sent_ref, kept_ref = refs[-2:]
    sent_ref[...] = (ks_ref[...].astype(jnp.float32) + gs_ref[...].astype(jnp.float32)).astype(sent_ref.dtype)
    kept_ref[...] = (kk_ref[...].astype(jnp.float32) + gk_ref[...].astype(jnp.float32)).astype(kept_ref.dtype)


def pieces_of(rows, cols):
    while rows * cols > 640 * 1024 and rows % 32 == 0:
        rows //= 2
    while rows * cols > 640 * 1024 and cols % 256 == 0:
        cols //= 2
    return rows, cols


def join_split(kept, got, mine, high, low, deps):
    n, rows, cols = kept.shape
    r, c = pieces_of(rows, cols)

    def half(other):
        def at(i, j, k, mine_ref):
            side = 1 - mine_ref[0] if other else mine_ref[0]
            return ((i // low * 2 + side) * low + i % low, j, k)

        return pl.BlockSpec((1, r, c), at)

    out = pl.BlockSpec((1, r, c), lambda i, j, k, mine_ref: (i, j, k))
    shape = jax.ShapeDtypeStruct((n // 2, rows, cols), kept.dtype)
    return pl.pallas_call(
        join_kernel,
        grid_spec=pltpu.PrefetchScalarGridSpec(
            num_scalar_prefetch=1,
            grid=(n // 2, rows // r, cols // c),
            in_specs=[half(True), half(False), half(True), half(False)] + [ANY] * len(deps),
            out_specs=[out, out],
        ),
        out_shape=[shape, shape],
        cost_estimate=COST,
        name="join",
    )(mine, kept, kept, got, got, *deps)


def join_last_kernel(k_ref, g_ref, *refs):
    refs[-1][...] = (k_ref[...].astype(jnp.float32) + g_ref[...].astype(jnp.float32)).astype(refs[-1].dtype)


def join_last(kept, got, deps):
    n, rows, cols = kept.shape
    r, c = pieces_of(rows, cols)
    block = pl.BlockSpec((1, r, c), lambda i, j, k: (i, j, k))
    return pl.pallas_call(
        join_last_kernel,
        grid=(n, rows // r, cols // c),
        in_specs=[block, block] + [ANY] * len(deps),
        out_specs=block,
        out_shape=jax.ShapeDtypeStruct(kept.shape, kept.dtype),
        cost_estimate=COST,
        name="join_last",
    )(kept, got, *deps).reshape(-1, kept.shape[-1])


def finish_kernel(p_ref, *refs, nb, gw):
    out_ref, e_ref, q_ref = refs[-3:]
    dkgw = DK * gw

    @pl.when(pl.program_id(0) == 0)
    def _():
        row = lax.broadcasted_iota(jnp.int32, (dkgw, dkgw), 0)
        col = lax.broadcasted_iota(jnp.int32, (1, dkgw), 1)
        e_ref[...] = (row == (col % DK) * gw + col // DK).astype(e_ref.dtype)

    per = 128 // DK
    lane_block = lax.broadcasted_iota(jnp.int32, (gw, 128), 1) // DK
    q_ref[...] = jnp.dot(
        p_ref[: nb * gw, :], e_ref[...], preferred_element_type=jnp.float32
    ).astype(q_ref.dtype)
    for tile in range(dkgw // 128):
        outs = [None] * per
        for b in range(nb):
            piece = q_ref[gw*b:gw*(b+1), 128*tile:128*(tile+1)]
            for i in range(per):
                turn = (b - i) % per
                moved = piece if turn == 0 else pltpu.roll(piece, DK * turn, 1)
                outs[i] = moved if outs[i] is None else jnp.where(lane_block == b, moved, outs[i])
        for i in range(per):
            out_ref[tile * per + i] = outs[i].astype(out_ref.dtype)


def finish_dw(p, gw, nb):
    assert nb * DK == 128
    rows = nb*gw + 32
    g = p.shape[0] // rows
    out = pl.pallas_call(
        functools.partial(finish_kernel, nb=nb, gw=gw),
        grid=(g,),
        in_specs=[pl.BlockSpec((rows, DK*gw), lambda i: (i, 0))],
        out_specs=pl.BlockSpec((gw, gw, 128), lambda i: (i, 0, 0)),
        out_shape=jax.ShapeDtypeStruct((g*gw, gw, 128), jnp.float32),
        scratch_shapes=[pltpu.VMEM((DK*gw, DK*gw), jnp.bfloat16), pltpu.VMEM((nb*gw, DK*gw), jnp.bfloat16)],
        cost_estimate=COST,
        name="finish_dw",
    )(p)
    return jnp.transpose(out, (2, 0, 1))


def wg_rows_kernel(mine_ref, lhs_ref, rhs_ref, *refs, many, dp, nextra, ndeps):
    extra_refs = refs[:nextra]
    sent_ref, kept_ref, lt_ref, ls_ref, lk_ref = refs[nextra + ndeps :]
    half = many * dp // 2
    share = lhs_ref.shape[1] // (many * dp)
    cols = sent_ref.shape[2]
    mine = mine_ref[0]

    @pl.when(pl.program_id(0) == 0)
    def _():
        lt_ref[...] = lhs_ref[...].T
        for i in range(half):
            for to_ref, side in ((ls_ref, 1 - mine), (lk_ref, mine)):
                at = pl.multiple_of((2 * i + side) * share, 16)
                to_ref[i * share : (i + 1) * share, :] = lt_ref[pl.ds(at, share), :]

    for out_ref, l_ref in ((sent_ref, ls_ref), (kept_ref, lk_ref)):
        total = jnp.dot(l_ref[...], rhs_ref[...], preferred_element_type=jnp.float32)
        for i in range(half):
            out_ref[i, :share, :] = total[i * share : (i + 1) * share, :].astype(out_ref.dtype)
    if nextra:
        for m in range(many):
            rows = []
            for r in extra_refs:
                if many > 1:
                    rows.append(r[0:1, m * cols : (m + 1) * cols])
                else:
                    rows += [r[0:1, k * cols : (k + 1) * cols] for k in range(r.shape[1] // cols)]
            rows.append(jnp.zeros((16 - len(rows), cols), jnp.float32))
            block = jnp.concatenate(rows, 0).astype(jnp.bfloat16)
            for i in range(dp // 2):
                sent_ref[m * dp // 2 + i, share:, :] = block
                kept_ref[m * dp // 2 + i, share:, :] = block


def wg_rows(mine, lhs, rhs, many, dp, chunks, extras=(), deps=(), slots=None, first=0, into=()):
    F, M = lhs.shape
    N = rhs.shape[1]
    share = M // (many * dp)
    half = many * dp // 2
    rows = share + (16 if extras else 0)
    out = pl.BlockSpec((half, rows, N // chunks), lambda i, m: (first, 0, i))
    shape = jax.ShapeDtypeStruct((slots or half, rows, N), jnp.bfloat16)
    deps = tuple(into) + tuple(deps)
    at = 3 + len(extras)
    return pl.pallas_call(
        functools.partial(wg_rows_kernel, many=many, dp=dp, nextra=len(extras), ndeps=len(deps)),
        input_output_aliases={at: 0, at + 1: 1} if into else {},
        grid_spec=pltpu.PrefetchScalarGridSpec(
            num_scalar_prefetch=1,
            grid=(chunks,),
            in_specs=[
                pl.BlockSpec((F, M), lambda i, m: (0, 0)),
                pl.BlockSpec((F, N // chunks), lambda i, m: (0, i)),
            ]
            + [pl.BlockSpec(e.shape, lambda i, m: (0, 0)) for e in extras]
            + [ANY] * len(deps),
            out_specs=[out, out],
            scratch_shapes=[
                pltpu.VMEM((M, F), jnp.bfloat16),
                pltpu.VMEM((half * share, F), jnp.bfloat16),
                pltpu.VMEM((half * share, F), jnp.bfloat16),
            ],
        ),
        out_shape=[shape, shape],
        cost_estimate=COST,
        name="wg_rows",
    )(mine, lhs, rhs, *extras, *deps)


def wg_plain_kernel(lhs_ref, rhs_ref, *refs, share):
    out_ref, lt_ref = refs[-2:]

    @pl.when(pl.program_id(0) == 0)
    def _():
        lt_ref[...] = lhs_ref[...].T

    total = jnp.dot(lt_ref[...], rhs_ref[...], preferred_element_type=jnp.float32).astype(jnp.bfloat16)
    if share:
        for k in range(out_ref.shape[0]):
            out_ref[k] = total[:, k * share : (k + 1) * share]
    else:
        out_ref[...] = total


def wg_plain(lhs, rhs, chunks, share, deps=()):
    F, M = lhs.shape
    N = rhs.shape[1]
    cols = N // chunks
    if share:
        spec = pl.BlockSpec((cols // share, M, share), lambda i: (i, 0, 0))
        shape = jax.ShapeDtypeStruct((N // share, M, share), jnp.bfloat16)
    else:
        spec = pl.BlockSpec((M, cols), lambda i: (0, i))
        shape = jax.ShapeDtypeStruct((M, N), jnp.bfloat16)
    return pl.pallas_call(
        functools.partial(wg_plain_kernel, share=share),
        grid=(chunks,),
        in_specs=[pl.BlockSpec((F, M), lambda i: (0, 0)), pl.BlockSpec((F, cols), lambda i: (0, i))]
        + [ANY] * len(deps),
        out_specs=spec,
        scratch_shapes=[pltpu.VMEM((M, F), jnp.bfloat16)],
        out_shape=shape,
        cost_estimate=COST,
        name="wg_plain",
    )(lhs, rhs, *deps)


def dpos_kernel(at_ref, keep_ref, *refs, parts, far, n, ndeps):
    qs, ks, vs = refs[:parts], refs[parts : 2 * parts], refs[2 * parts : 3 * parts]
    far_refs, refs = refs[3 * parts : (3 + far) * parts], refs[(3 + far) * parts :]
    wq_ref, wk_ref, wv_ref, first_ref, conv_ref = refs[:5]
    g_refs = refs[5 : 5 + n]
    low_ref, lowv_ref, pos_ref, d_ref, qk_ref, v_ref = refs[5 + n + ndeps :]
    turn = (at_ref[2] - pl.program_id(0) + n) % n
    dq = jnp.concatenate([r[...] for r in qs], 1)
    dks, dvs = [], []
    for p in range(parts):
        dk, dv = ks[p][...], vs[p][...]
        for r in far_refs[p * far : (p + 1) * far]:
            dk = dk + r[0].astype(jnp.float32)
            dv = dv + r[1].astype(jnp.float32)
        dks.append(dk.astype(jnp.bfloat16))
        dvs.append(dv.astype(jnp.bfloat16))
    dk, dv = jnp.concatenate(dks, 1), jnp.concatenate(dvs, 1)
    width = dq.shape[1]
    low_ref[:, :width] = dq
    low_ref[:, width:] = dk
    lowv_ref[...] = dv
    total = first_ref[...] + (1.0 - (keep_ref[at_ref[0]] > 0).astype(jnp.float32)) * picked(g_refs, turn).astype(jnp.float32)
    for low, w_ref in ((dq, wq_ref), (dk, wk_ref), (dv, wv_ref)):
        total = total + lax.dot_general(
            low, w_ref[...], (((1,), (1,)), ((), ())), preferred_element_type=jnp.float32
        )
    pos_ref[...] = total
    d_ref[...] = (total * gelu_slope(conv_ref[...])).astype(d_ref.dtype)
    sums = [jnp.sum(low.astype(jnp.float32), 0, keepdims=True) for low in (dq, dk, dv)]

    @pl.when(pl.program_id(0) == 0)
    def _():
        qk_ref[...] = jnp.zeros_like(qk_ref)
        v_ref[...] = jnp.zeros_like(v_ref)

    qk_ref[0:1, :width] += sums[0]
    qk_ref[0:1, width:] += sums[1]
    v_ref[0:1, :] += sums[2]


def dpos(at, keep, dqs, dks, dvs, fars, wq, wk, wv, first, gs, conv_before, deps):
    F, W = first.shape
    n = len(gs)
    rows = F // n
    parts = len(dqs)
    part = pl.BlockSpec((rows, W // parts), lambda i, at, k: (i, 0))
    block = pl.BlockSpec((rows, W), lambda i, at, k: (i, 0))
    whole = pl.BlockSpec((W, W), lambda i, at, k: (0, 0))
    return pl.pallas_call(
        functools.partial(dpos_kernel, parts=parts, far=len(fars[0]), n=n, ndeps=len(deps)),
        grid_spec=pltpu.PrefetchScalarGridSpec(
            num_scalar_prefetch=2,
            grid=(F // rows,),
            in_specs=[part] * (3 * parts)
            + [pl.BlockSpec((2, rows, W // parts), lambda i, at, k: (0, i, 0))] * (parts * len(fars[0]))
            + [whole] * 3 + [block] * 2 + [pl.BlockSpec((rows, W), lambda i, at, k: (0, 0))] * n + [ANY] * len(deps),
            out_specs=[
                pl.BlockSpec((rows, 2 * W), lambda i, at, k: (i, 0)), block, block, block,
                pl.BlockSpec((8, 2 * W), lambda i, at, k: (0, 0)),
                pl.BlockSpec((8, W), lambda i, at, k: (0, 0)),
            ],
        ),
        out_shape=[
            jax.ShapeDtypeStruct((F, 2 * W), jnp.bfloat16),
            jax.ShapeDtypeStruct((F, W), jnp.bfloat16),
            jax.ShapeDtypeStruct((F, W), jnp.float32),
            jax.ShapeDtypeStruct((F, W), jnp.bfloat16),
            jax.ShapeDtypeStruct((8, 2 * W), jnp.float32),
            jax.ShapeDtypeStruct((8, W), jnp.float32),
        ],
        cost_estimate=COST,
        name="dpos",
    )(at, keep, *dqs, *dks, *dvs, *[f for part in fars for f in part], wq, wk, wv, first, conv_before, *gs, *deps)


def front_kernel(conv_ref, bias_ref, x_ref, wq_ref, wk_ref, wv_ref, bq_ref, bv_ref, *refs):
    cb_ref, pos_ref, low_ref, q_ref, kv_ref = refs[-5:]
    before = conv_ref[...].T + bias_ref[...]
    cb_ref[...] = before
    pos = x_ref[...].astype(jnp.float32) + gelu(before)
    pos_ref[...] = pos
    low = pos.astype(jnp.bfloat16)
    low_ref[...] = low
    width = low.shape[1]
    q_ref[...] = (jnp.dot(low, wq_ref[...], preferred_element_type=jnp.float32) + bq_ref[...]).astype(jnp.bfloat16)
    kv_ref[:, :width] = jnp.dot(low, wk_ref[...], preferred_element_type=jnp.float32).astype(jnp.bfloat16)
    kv_ref[:, width:] = (
        jnp.dot(low, wv_ref[...], preferred_element_type=jnp.float32) + bv_ref[...]
    ).astype(jnp.bfloat16)


def front(conv_t, bias, x, wq, wk, wv, bq, bv, deps):
    W, F = conv_t.shape
    rows = min(256, F)
    block = pl.BlockSpec((rows, W), lambda i: (i, 0))
    whole = pl.BlockSpec((W, W), lambda i: (0, 0))
    vec = pl.BlockSpec((1, W), lambda i: (0, 0))
    return pl.pallas_call(
        front_kernel,
        grid=(F // rows,),
        in_specs=[pl.BlockSpec((W, rows), lambda i: (0, i)), vec, block]
        + [whole] * 3 + [vec] * 2 + [ANY] * len(deps),
        out_specs=[block] * 4 + [pl.BlockSpec((rows, 2 * W), lambda i: (i, 0))],
        out_shape=[
            jax.ShapeDtypeStruct((F, W), jnp.float32),
            jax.ShapeDtypeStruct((F, W), jnp.float32),
            jax.ShapeDtypeStruct((F, W), jnp.bfloat16),
            jax.ShapeDtypeStruct((F, W), jnp.bfloat16),
            jax.ShapeDtypeStruct((F, 2 * W), jnp.bfloat16),
        ],
        cost_estimate=COST,
        name="front",
    )(conv_t, bias.reshape(1, W), x, wq, wk, wv, bq.reshape(1, W), bv.reshape(1, W), *deps)


def picked(refs, index):
    out = refs[0][...]
    for m in range(1, len(refs)):
        out = jnp.where(index == m, refs[m][...], out)
    return out


def mid_kernel(at_ref, keep_ref, attn_ref, pos_ref, *refs, n, ndeps, chunk):
    g_refs, refs = refs[:n], refs[n:]
    (wa_ref, wi_ref, wo_ref, ba_ref, g1_ref, s1_ref, bi_ref, bo_ref, g2_ref, s2_ref), refs = refs[:10], refs[10:]
    out_refs, refs = refs[ndeps : ndeps + n], refs[ndeps + n :]
    (
        first_ref, inner_ref, douter_ref, dinner_ref, dattn_ref, dfirst_ref, dheads_ref,
        inner_sum_ref, sums_ref, slope_ref,
    ) = refs
    keep = (keep_ref[at_ref[0]] > 0).astype(jnp.float32)
    turn = (at_ref[2] - pl.program_id(0) + n) % n
    width = pos_ref.shape[1]
    ff = wi_ref.shape[1]
    pos = pos_ref[...]
    attn_out = jnp.dot(attn_ref[...], wa_ref[...], preferred_element_type=jnp.float32) + ba_ref[...]
    first_normed, first_scale = layer_norm(pos + attn_out)
    first_out = first_normed * g1_ref[...] + s1_ref[...]
    first_low = first_out.astype(jnp.bfloat16)
    first_ref[...] = first_low
    total = None
    for c in range(0, ff, chunk):
        cols = slice(c, c + chunk)
        pre = jnp.dot(first_low, wi_ref[:, cols], preferred_element_type=jnp.float32) + bi_ref[:, cols]
        phi = 0.5 * (1.0 + lax.erf(pre * root_half))
        slope_ref[:, cols] = phi + pre * jnp.exp(-0.5 * pre * pre) * inv_root_two_pi
        low = (pre * phi).astype(jnp.bfloat16)
        inner_ref[:, cols] = low
        part = jnp.dot(low, wo_ref[cols, :], preferred_element_type=jnp.float32)
        total = part if total is None else total + part
    second_normed, second_scale = layer_norm(first_out + (total + bo_ref[...]))
    second_out = second_normed * g2_ref[...] + s2_ref[...]
    layer = (keep * second_out + (1.0 - keep) * pos).astype(jnp.bfloat16)
    for m in range(n):
        @pl.when(turn == m)
        def _(m=m):
            out_refs[m][...] = layer

    grad_layer = keep * picked(g_refs, turn).astype(jnp.float32)
    d_second = norm_back(grad_layer * g2_ref[...], second_normed, second_scale)
    d_outer = d_second.astype(jnp.bfloat16)
    douter_ref[...] = d_outer

    @pl.when(pl.program_id(0) == 0)
    def _():
        inner_sum_ref[...] = jnp.zeros_like(inner_sum_ref)
        sums_ref[...] = jnp.zeros_like(sums_ref)

    d_first_out = d_second
    for c in range(0, ff, chunk):
        cols = slice(c, c + chunk)
        d_inner = (
            lax.dot_general(d_outer, wo_ref[cols, :], (((1,), (1,)), ((), ())), preferred_element_type=jnp.float32)
            * slope_ref[:, cols]
        ).astype(jnp.bfloat16)
        dinner_ref[:, cols] = d_inner
        inner_sum_ref[0:1, cols] += jnp.sum(d_inner.astype(jnp.float32), 0, keepdims=True)
        d_first_out = d_first_out + lax.dot_general(
            d_inner, wi_ref[:, cols], (((1,), (1,)), ((), ())), preferred_element_type=jnp.float32
        )
    d_first = norm_back(d_first_out * g1_ref[...], first_normed, first_scale)
    dfirst_ref[...] = d_first
    d_attn = d_first.astype(jnp.bfloat16)
    dattn_ref[...] = d_attn
    dheads_ref[...] = lax.dot_general(
        d_attn, wa_ref[...], (((1,), (1,)), ((), ())), preferred_element_type=jnp.float32
    ).astype(jnp.bfloat16)
    for k, v in enumerate((
        d_attn.astype(jnp.float32), d_first_out * first_normed, d_first_out,
        d_outer.astype(jnp.float32), grad_layer * second_normed, grad_layer,
    )):
        sums_ref[0:1, k * width : (k + 1) * width] += jnp.sum(v, 0, keepdims=True)


def mid(at, keep, attn_low, pos_out, gs, wa, wi, wo, ba, g1, s1, bi, bo, g2, s2, deps):
    F, W = pos_out.shape
    ff = wi.shape[1]
    n = len(gs)
    rows = F // n
    block = pl.BlockSpec((rows, W), lambda i, at, k: (i, 0))
    wide = pl.BlockSpec((rows, ff), lambda i, at, k: (i, 0))

    def whole(*shape):
        return pl.BlockSpec(shape, lambda i, at, k: (0,) * len(shape))

    vec = whole(1, W)
    out = lambda cols, kind: jax.ShapeDtypeStruct((F, cols), kind)
    bf, fl = jnp.bfloat16, jnp.float32
    return pl.pallas_call(
        functools.partial(mid_kernel, n=n, ndeps=len(deps), chunk=min(768, ff)),
        grid_spec=pltpu.PrefetchScalarGridSpec(
            num_scalar_prefetch=2,
            grid=(F // rows,),
            in_specs=[block, block] + [whole(rows, W)] * n + [whole(W, W), whole(W, ff), whole(ff, W), vec, vec, vec, whole(1, ff), vec, vec, vec]
            + [ANY] * len(deps),
            out_specs=[whole(rows, W)] * n + [block, wide, block, wide, block, block, block, whole(8, ff), whole(8, 6 * W)],
            scratch_shapes=[pltpu.VMEM((rows, ff), jnp.float32)],
        ),
        out_shape=[
            *[jax.ShapeDtypeStruct((rows, W), bf)] * n, out(W, bf), out(ff, bf), out(W, bf), out(ff, bf), out(W, bf), out(W, fl), out(W, bf),
            jax.ShapeDtypeStruct((8, ff), fl), jax.ShapeDtypeStruct((8, 6 * W), fl),
        ],
        cost_estimate=COST,
        name="mid",
    )(
        at, keep, attn_low, pos_out, *gs, wa, wi, wo, ba.reshape(1, W), g1.reshape(1, W), s1.reshape(1, W),
        bi.reshape(1, ff), bo.reshape(1, W), g2.reshape(1, W), s2.reshape(1, W), *deps,
    )


def place(ext, before, gaps, length):
    rows, have = ext.shape
    ext = jnp.concatenate([ext, jnp.zeros((rows, length - have), ext.dtype)], 1) if length > have else ext
    if length > have:
        before = jnp.concatenate([before, jnp.full((before.shape[0], length - have), -1, before.dtype)], 1)
    total = None
    for k in range(gaps + 1):
        moved = ext if k == 0 else pltpu.roll(ext, HALO * k, 1)
        here = (before if k == 0 else pltpu.roll(before, HALO * k, 1))[0:1, :] == k
        total = jnp.where(here, moved, jnp.zeros((), ext.dtype) if total is None else total)
    return total


def window_of(seg_ref, wide_ref, row, member, F):
    T = seg_ref.shape[1]
    wide_ref[...] = jnp.zeros_like(wide_ref)
    wide_ref[:, 128 : 128 + T] = jnp.broadcast_to(seg_ref[pl.ds(row % 8, 1), :], (8, T))
    start = pl.multiple_of(member * F, 128)
    window = wide_ref[:, pl.ds(start, F + 256)]
    return pltpu.roll(window, F + 256 - HALO, 1)[:, : F + 2 * HALO]


def ordinals(window, F):
    lane = lax.broadcasted_iota(jnp.int32, window.shape, 1)
    local = (lane >= HALO) & (lane < HALO + F)
    most = jnp.max(jnp.where(local, window, 0), axis=1, keepdims=True)
    first = jnp.sum(jnp.where(lane == HALO, window, 0), axis=1, keepdims=True)
    last = jnp.sum(jnp.where(lane == HALO + F - 1, window, 0), axis=1, keepdims=True)
    number = jnp.where(window > 0, window, most + 1)
    number_first = jnp.where(first > 0, first, most + 1)
    number_last = jnp.where(last > 0, last, most + 1)
    before = number - number_first
    before = jnp.where((lane < HALO) & (window != first), -1, before)
    right = jnp.where(window == last, number_last - number_first, -1)
    return jnp.where(lane >= HALO + F, right, before)


def column(row):
    return row.astype(jnp.float32).T[:, 0:1]


def build_x_kernel(at_ref, seg_ref, *refs, n, nlow, nhigh, team, F, gaps, spread):
    row, member = at_ref[0], at_ref[1]
    j = at_ref[2]
    got, lows, highs = refs[:n], refs[n : n + nlow], refs[n + nlow : n + nlow + nhigh]
    x_ref, spread_ref, sel_ref, qc_ref, kc_ref, wide_ref = refs[-6:]
    zero = jnp.zeros((), jnp.bfloat16)
    blocks = []
    for w in range(n):
        part = got[0][...]
        for m in range(1, n):
            part = jnp.where((j - w + n) % n == m, got[m][...], part)
        blocks.append(part)

    def edge(parts, on):
        part = parts[0][...]
        for m in range(1, len(parts)):
            part = jnp.where(j == m, parts[m][...], part)
        return jnp.where(on, part, zero)

    window = window_of(seg_ref, wide_ref, row, member, F)
    before = ordinals(window, F)
    ext = jnp.concatenate([edge(lows, member > 0)] + blocks + [edge(highs, member < team - 1)], 0)
    ext_t = jnp.where(window[0:1, :] > 0, ext.T, zero)
    spread_ref[...] = place(ext_t, before, gaps, spread)
    local = pltpu.roll(window, F + 2 * HALO - HALO, 1)[:, :F]
    before_local = pltpu.roll(before, F + 2 * HALO - HALO, 1)[:, :F]
    which = lax.broadcasted_iota(jnp.int32, (8, F), 0)
    sel_ref[...] = (before_local == which).astype(jnp.float32)
    seg_col = column(local)
    length = F // n
    for w in range(n):
        rows = slice(w * length, (w + 1) * length)
        x_ref[rows, :] = jnp.where(seg_col[rows] > 0, blocks[w], zero)
    lane = lax.broadcasted_iota(jnp.int32, (1, 128), 1) % 64
    qc_ref[...] = (seg_col == lane.astype(jnp.float32)).astype(jnp.bfloat16)
    for s in range(team):
        start = pl.multiple_of(128 + (member - s + team) % team * F, 128)
        keys = column(wide_ref[:, pl.ds(start, F)])
        kc_ref[s * F : (s + 1) * F, :] = jnp.where(
            (keys == lane.astype(jnp.float32)) & (lane > 0), 0.0, -1e30
        ).astype(jnp.bfloat16)


def build_x(at, segments, got, lows, highs, team, F, gaps, spread, deps):
    n, W = len(got), got[0].shape[1]
    T = segments.shape[1]
    whole = pl.BlockSpec(memory_space=pltpu.VMEM)
    out = lambda r, c, kind: jax.ShapeDtypeStruct((r, c), kind)

    def full(r, c):
        return pl.BlockSpec((r, c), lambda i, at: (0, 0))

    return pl.pallas_call(
        functools.partial(
            build_x_kernel, n=n, nlow=len(lows), nhigh=len(highs), team=team, F=F, gaps=gaps, spread=spread
        ),
        grid_spec=pltpu.PrefetchScalarGridSpec(
            num_scalar_prefetch=1,
            grid=(1,),
            in_specs=[pl.BlockSpec((8, T), lambda i, at: (at[0] // 8, 0))]
            + [full(*a.shape) for a in (*got, *lows, *highs)] + [ANY] * len(deps),
            out_specs=[full(F, W), full(W, spread), full(8, F), full(F, 128), full(team * F, 128)],
            scratch_shapes=[pltpu.VMEM((8, T + 256), jnp.int32)],
        ),
        out_shape=[
            out(F, W, jnp.bfloat16), out(W, spread, jnp.bfloat16), out(8, F, jnp.float32),
            out(F, 128, jnp.bfloat16), out(team * F, 128, jnp.bfloat16),
        ],
        cost_estimate=COST,
        name="build_x",
    )(at, segments, *got, *lows, *highs, *deps)


def build_d_kernel(at_ref, seg_ref, d_ref, *refs, edges, team, F, gaps, length):
    row, member = at_ref[0], at_ref[1]
    out_ref, wide_ref = refs[-2:]
    window = window_of(seg_ref, wide_ref, row, member, F)
    before = ordinals(window, F)
    zero = jnp.zeros((), jnp.bfloat16)
    if edges:
        low, high = refs[0][...], refs[1][...]
        ext = jnp.concatenate(
            [jnp.where(member > 0, low, zero), d_ref[...], jnp.where(member < team - 1, high, zero)], 0
        ).T
    else:
        ext = d_ref[...].T
        before = pltpu.roll(before, F + 2 * HALO - HALO, 1)[:, :F]
    out_ref[...] = place(ext, before, gaps, length)


def build_d(at, segments, d, edges, team, gaps, length, deps=()):
    F, W = d.shape
    T = segments.shape[1]

    def full(r, c):
        return pl.BlockSpec((r, c), lambda i, at: (0, 0))

    return pl.pallas_call(
        functools.partial(build_d_kernel, edges=bool(edges), team=team, F=F, gaps=gaps, length=length),
        grid_spec=pltpu.PrefetchScalarGridSpec(
            num_scalar_prefetch=1,
            grid=(1,),
            in_specs=[pl.BlockSpec((8, T), lambda i, at: (at[0] // 8, 0)), full(F, W)]
            + [full(*a.shape) for a in edges] + [ANY] * len(deps),
            out_specs=full(W, length),
            scratch_shapes=[pltpu.VMEM((8, T + 256), jnp.int32)],
        ),
        out_shape=jax.ShapeDtypeStruct((W, length), jnp.bfloat16),
        cost_estimate=COST,
        name="build_d",
    )(at, segments, d, *edges, *deps)


def widen_kernel(*refs, n):
    for k in range(n):
        refs[len(refs) - n + k][...] = refs[k][...].astype(jnp.float32)


def widen(arrays, deps):
    whole = pl.BlockSpec(memory_space=pltpu.VMEM)
    size = sum(a.size for a in arrays)
    return pl.pallas_call(
        functools.partial(widen_kernel, n=len(arrays)),
        in_specs=[whole] * len(arrays) + [ANY] * len(deps),
        out_specs=[whole] * len(arrays),
        out_shape=[jax.ShapeDtypeStruct(a.shape, jnp.float32) for a in arrays],
        cost_estimate=COST,
        name="widen",
    )(*arrays, *deps)


def grad_in_kernel(at_ref, seg_ref, pos_ref, *refs, n, nback, F):
    backs, out_refs, wide_ref = refs[:nback], refs[-1 - n : -1], refs[-1]
    window = window_of(seg_ref, wide_ref, at_ref[0], at_ref[1], F)
    live = column(pltpu.roll(window, F + 2 * HALO - HALO, 1)[:, :F]) > 0
    back = jnp.concatenate([b[...] for b in backs], 0).T
    total = jnp.where(live, pos_ref[...] + back, 0.0).astype(jnp.bfloat16)
    rows = F // n
    for w in range(n):
        for m in range(n):
            @pl.when((at_ref[2] - w + n) % n == m)
            def _(w=w, m=m):
                out_refs[m][...] = total[w * rows : (w + 1) * rows, :]


def grad_in(at, segments, pos, backs, n, deps):
    F, W = pos.shape
    T = segments.shape[1]

    def full(r, c):
        return pl.BlockSpec((r, c), lambda i, at: (0, 0))

    return pl.pallas_call(
        functools.partial(grad_in_kernel, n=n, nback=len(backs), F=F),
        grid_spec=pltpu.PrefetchScalarGridSpec(
            num_scalar_prefetch=1,
            grid=(1,),
            in_specs=[pl.BlockSpec((8, T), lambda i, at: (at[0] // 8, 0)), full(F, W)]
            + [full(*b.shape) for b in backs] + [ANY] * len(deps),
            out_specs=[full(F // n, W)] * n,
            scratch_shapes=[pltpu.VMEM((8, T + 256), jnp.int32)],
        ),
        out_shape=[jax.ShapeDtypeStruct((F // n, W), jnp.bfloat16)] * n,
        cost_estimate=COST,
        name="grad_in",
    )(at, segments, pos, *backs, *deps)


def stack_back_kernel(at_ref, *refs, n):
    index = (pl.program_id(0) - at_ref[0] + n) % n
    refs[-1][0] = picked(refs[:n], index)


def stack_back(at, blocks, deps):
    n = len(blocks)
    L, W = blocks[0].shape
    return pl.pallas_call(
        functools.partial(stack_back_kernel, n=n),
        grid_spec=pltpu.PrefetchScalarGridSpec(
            num_scalar_prefetch=1,
            grid=(n,),
            in_specs=[pl.BlockSpec((L, W), lambda i, at: (0, 0))] * n + [ANY] * len(deps),
            out_specs=pl.BlockSpec((1, L, W), lambda i, at: (i, 0, 0)),
        ),
        out_shape=jax.ShapeDtypeStruct((n, L, W), blocks[0].dtype),
        cost_estimate=COST,
        name="stack_back",
    )(at, *blocks, *deps)

HEAD = 64

def nt(a, b):
    return lax.dot_general(a, b, (((1,), (1,)), ((), ())), preferred_element_type=jnp.float32)

def attn_fwd_kernel(*refs, P, chunk):
    q_ref, qc_ref, kc_ref = refs[:3]
    k_refs = refs[3:3+P]
    v_refs = refs[3+P:3+2*P]
    o_ref, lse_ref, ka_ref, va_ref = refs[-4:]
    F = q_ref.shape[0]
    low_k = lax.broadcasted_iota(jnp.int32, (F, 128), 1) < HEAD
    low_q = lax.broadcasted_iota(jnp.int32, (chunk, 128), 1) < HEAD
    one = jnp.ones((), jnp.bfloat16)
    for h in range(2):
        pick = low_k if h == 0 else jnp.logical_not(low_k)
        for p in range(P):
            ka_ref[h, p*F:(p+1)*F, :] = jnp.where(pick, k_refs[p][...], kc_ref[p*F:(p+1)*F, :])
            va_ref[h, p*F:(p+1)*F, :] = jnp.where(pick, v_refs[p][...], one)
    for c in range(F // chunk):
        rows = slice(c*chunk, (c+1)*chunk)
        q = q_ref[rows, :] * jnp.asarray(0.125, jnp.bfloat16)
        outs, lses = [], []
        for h in range(2):
            pick = low_q if h == 0 else jnp.logical_not(low_q)
            qa = jnp.where(pick, q, qc_ref[rows, :])
            s = nt(qa, ka_ref[h])
            m = jnp.maximum(jnp.max(s, axis=1, keepdims=True), -1e20)
            e = jnp.exp(s - m).astype(jnp.bfloat16)
            o = jnp.dot(e, va_ref[h], preferred_element_type=jnp.float32)
            l = jnp.maximum(o[:, HEAD:HEAD+1] if h == 0 else o[:, 0:1], 1.0)
            outs.append(o * (1.0 / l))
            lses.append(m + jnp.log(l))
        o_ref[rows, :] = jnp.where(low_q, outs[0], outs[1]).astype(o_ref.dtype)
        lse_ref[rows, :] = jnp.where(low_q, lses[0], lses[1])

def attn_fwd(q, kvs, qc, kc, deps, chunk=128):
    F, W = q.shape
    P = len(kvs)
    T = P * F
    npair = W // 128
    return pl.pallas_call(
        functools.partial(attn_fwd_kernel, P=P, chunk=min(chunk, F)),
        grid=(npair,),
        in_specs=[pl.BlockSpec((F, 128), lambda a: (0, a)),
                  pl.BlockSpec((F, 128), lambda a: (0, 0)),
                  pl.BlockSpec((T, 128), lambda a: (0, 0))]
                 + [pl.BlockSpec((F, 128), lambda a: (0, a))] * P
                 + [pl.BlockSpec((F, 128), lambda a, n=npair: (0, a + n))] * P
                 + [ANY] * len(deps),
        out_specs=[pl.BlockSpec((F, 128), lambda a: (0, a)), pl.BlockSpec((F, 128), lambda a: (0, a))],
        out_shape=[jax.ShapeDtypeStruct((F, W), jnp.bfloat16), jax.ShapeDtypeStruct((F, W), jnp.float32)],
        scratch_shapes=[pltpu.VMEM((2, T, 128), jnp.bfloat16), pltpu.VMEM((2, T, 128), jnp.bfloat16)],
        cost_estimate=COST,
        name="attn_fwd",
    )(q, qc, kc, *kvs, *kvs, *deps)

def attn_bwd_kernel(*refs, P, chunk):
    q_ref, do_ref, o_ref, lse_ref, qc_ref, kc_ref = refs[:6]
    k_refs = refs[6:6+P]
    v_refs = refs[6+P:6+2*P]
    dq_ref, dk_ref, dv_ref = refs[-2-P:1-P]
    far_refs = refs[1-P:]
    F = q_ref.shape[0]
    low_q = lax.broadcasted_iota(jnp.int32, (F, 128), 1) < HEAD
    low_c = lax.broadcasted_iota(jnp.int32, (chunk, 128), 1) < HEAD
    q = q_ref[...] * jnp.asarray(0.125, jnp.bfloat16)
    do = do_ref[...]
    lse_t = lse_ref[...].T
    prod_t = (do.astype(jnp.float32) * o_ref[...].astype(jnp.float32)).T
    lse_row = [lse_t[h*HEAD:h*HEAD+1, :] for h in range(2)]
    delta_row = [jnp.sum(prod_t[h*HEAD:(h+1)*HEAD, :], axis=0, keepdims=True) for h in range(2)]
    qa = [jnp.where(low_q if h == 0 else jnp.logical_not(low_q), q, qc_ref[...]) for h in range(2)]
    zero = jnp.zeros((), jnp.bfloat16)
    dqt = [jnp.zeros((HEAD, F), jnp.float32) for _ in range(2)]
    for p in range(P):
        for c in range(F // chunk):
            rows = slice(c*chunk, (c+1)*chunk)
            k = k_refs[p][rows, :]
            v = v_refs[p][rows, :]
            kc = kc_ref[p*F + c*chunk: p*F + (c+1)*chunk, :]
            kt = k.T
            dks, dvs = [], []
            for h in range(2):
                pick = low_c if h == 0 else jnp.logical_not(low_c)
                st = nt(jnp.where(pick, k, kc), qa[h])
                pt = jnp.exp(st - lse_row[h])
                dpt = nt(jnp.where(pick, v, zero), do)
                dst = (pt * (dpt - delta_row[h])).astype(jnp.bfloat16)
                dvs.append(jnp.dot(pt.astype(jnp.bfloat16), do, preferred_element_type=jnp.float32))
                dks.append(jnp.dot(dst, q, preferred_element_type=jnp.float32))
                dqt[h] = dqt[h] + jnp.dot(kt[h*HEAD:(h+1)*HEAD, :], dst, preferred_element_type=jnp.float32)
            dk = jnp.where(low_c, dks[0], dks[1])
            dv = jnp.where(low_c, dvs[0], dvs[1])
            if p == 0:
                dk_ref[rows, :] = dk
                dv_ref[rows, :] = dv
            else:
                far_refs[p-1][0, rows, :] = dk.astype(jnp.bfloat16)
                far_refs[p-1][1, rows, :] = dv.astype(jnp.bfloat16)
    dq = jnp.concatenate(dqt, axis=0).T * 0.125
    dq_ref[...] = dq.astype(dq_ref.dtype)

def attn_bwd(q, do, o, lse, kvs, qc, kc, first, count, deps, chunk=128):
    F, W = q.shape
    P = len(kvs)
    T = P * F
    npair = W // 128
    own = pl.BlockSpec((F, 128), lambda a: (0, a + first))
    out = pl.BlockSpec((F, 128), lambda a: (0, a))
    return pl.pallas_call(
        functools.partial(attn_bwd_kernel, P=P, chunk=min(chunk, F)),
        grid=(count,),
        in_specs=[own, own, own, own,
                  pl.BlockSpec((F, 128), lambda a: (0, 0)),
                  pl.BlockSpec((T, 128), lambda a: (0, 0))]
                 + [own] * P
                 + [pl.BlockSpec((F, 128), lambda a, n=npair: (0, a + first + n))] * P
                 + [ANY] * len(deps),
        out_specs=[out] * 3 + [pl.BlockSpec((2, F, 128), lambda a: (0, 0, a))] * (P - 1),
        out_shape=[jax.ShapeDtypeStruct((F, 128 * count), t) for t in (jnp.bfloat16, jnp.float32, jnp.float32)]
                  + [jax.ShapeDtypeStruct((2, F, 128 * count), jnp.bfloat16)] * (P - 1),
        cost_estimate=COST,
        name="attn_bwd",
    )(q, do, o, lse, qc, kc, *kvs, *kvs, *deps)

HALO = 64
UTT_LEAST = 256
root_half = 0.7071067811865476
inv_root_two_pi = 0.3989422804014327
f32 = jnp.float32
bf16 = jnp.bfloat16


def layer_norm(hidden):
    centred = hidden - jnp.mean(hidden, axis=-1, keepdims=True)
    inv_scale = lax.rsqrt(jnp.mean(centred * centred, axis=-1, keepdims=True) + 1e-05)
    return (centred * inv_scale, inv_scale)


def norm_back(grad_normed, normed, inv_scale):
    return inv_scale * (
        grad_normed
        - jnp.mean(grad_normed, axis=-1, keepdims=True)
        - normed * jnp.mean(grad_normed * normed, axis=-1, keepdims=True)
    )


def gelu(entries):
    return 0.5 * entries * (1.0 + lax.erf(entries * root_half))


def gelu_slope(entries):
    return (
        0.5 * (1.0 + lax.erf(entries * root_half))
        + entries * jnp.exp(-0.5 * entries * entries) * inv_root_two_pi
    )


def mm(a, b):
    return jnp.dot(a, b, preferred_element_type=f32)


def mm_back(a, b):
    return lax.dot_general(a, b, (((1,), (1,)), ((), ())), preferred_element_type=f32)


def wgrad(a, b):
    return lax.dot_general(a, b, (((0,), (0,)), ((), ())), preferred_element_type=f32)


class Plan:
    def __init__(self, dp, seq, rows_dev):
        self.dp, self.seq, self.n = dp, seq, rows_dev
        self.q = seq // (2 * rows_dev)
        self.P = 2 * self.q
        assert dp % 2 == 0 and self.q * 2 * rows_dev == seq and rows_dev > 1

    def out_pairs(self, m):
        pairs = []
        for d in range(self.dp):
            for z in range(self.seq):
                rho = self.n * (d % 2) + (z + m) % self.n
                u = z // self.n
                pairs.append((d * self.seq + z, self.member(d // 2, rho, u)))
        return pairs

    def edge_pairs(self):
        heads = [[] for _ in range(self.n)]
        tails = [[] for _ in range(self.n)]
        for d in range(self.dp):
            for z in range(self.seq):
                u = z // self.n
                for j in range(self.n):
                    rho = self.n * (d % 2) + j
                    if z % self.n == self.n - 1 and u + 1 < self.P:
                        tails[j].append((d * self.seq + z, self.member(d // 2, rho, u + 1)))
                    if z % self.n == 0 and u > 0:
                        heads[j].append((d * self.seq + z, self.member(d // 2, rho, u - 1)))
        return heads, tails

    def member(self, e, rho, u):
        return (2 * e + u % 2) * self.seq + rho * self.q + u // 2

    def team_pairs(self, shift, wrap):
        pairs = []
        for e in range(self.dp // 2):
            for rho in range(2 * self.n):
                for u in range(self.P):
                    to = u + shift
                    if wrap or 0 <= to < self.P:
                        pairs.append((self.member(e, rho, u), self.member(e, rho, to % self.P)))
        return pairs


BOTH = ("dp", "seq")


def on_device(
    frames,
    output_gradient,
    segments,
    layer_keep,
    conv_weight,
    convolution_bias,
    query_matrix,
    query_offset_bias,
    key_matrix,
    value_matrix,
    value_offset_bias,
    attn_weight,
    attn_bias,
    first_gain,
    first_shift,
    inner_weight,
    inner_bias,
    outer_weight,
    outer_bias,
    second_gain,
    second_shift,
):
    rows_dev, local_len, width = frames.shape
    total_rows, row_len = segments.shape
    dp_count, seq_count = lax.axis_size("dp"), lax.axis_size("seq")
    dp_index, seq_index = lax.axis_index("dp"), lax.axis_index("seq")
    plan = Plan(dp_count, seq_count, rows_dev)
    n, q, team = plan.n, plan.q, plan.P
    F = row_len // team
    taps, _, gw = conv_weight.shape
    tap_blocks = taps // DK
    rho = seq_index // q
    member = (seq_index % q) * 2 + dp_index % 2
    row_id = (dp_index // 2) * (2 * n) + rho

    def pick(parts, index):
        out = parts[0]
        for k in range(1, len(parts)):
            out = jnp.where(index == k, parts[k], out)
        return out

    def blocks_to_team(a):
        got = []
        for m in range(n):
            sent = pick([a[j] for j in range(n)], (seq_index + m) % n)
            got.append(lax.ppermute(sent, BOTH, plan.out_pairs(m)))
        return got

    def from_team(sent):
        back = [
            lax.ppermute(sent[m], BOTH, [(t, s) for s, t in plan.out_pairs(m)]) for m in range(n)
        ]
        return jnp.stack([pick(back, (row - seq_index) % n) for row in range(n)], 0)

    def edges_to_team(a):
        heads, tails = plan.edge_pairs()
        lows, highs = [], []
        for j in range(n):
            tail, head = a[j, local_len - HALO :], a[j, :HALO]
            if team == 2:
                got = lax.ppermute(
                    jnp.where(seq_index % n == 0, head, tail), BOTH, heads[j] + tails[j]
                )
                lows.append(got)
                highs.append(got)
            else:
                lows.append(lax.ppermute(tail, BOTH, tails[j]))
                highs.append(lax.ppermute(head, BOTH, heads[j]))
        return lows, highs

    def edges(a):
        if team == 2:
            got = lax.ppermute(
                jnp.where(member == 0, a[F - HALO :], a[:HALO]), BOTH, plan.team_pairs(1, True)
            )
            return got, got
        low = lax.ppermute(a[F - HALO :], BOTH, plan.team_pairs(1, False))
        high = lax.ppermute(a[:HALO], BOTH, plan.team_pairs(-1, False))
        return low, high

    def pairs_of(axis, bit):
        pairs = []
        for d in range(dp_count):
            for z in range(seq_count):
                to = (d ^ bit, z) if axis == "dp" else (d, z ^ bit)
                pairs.append((d * seq_count + z, to[0] * seq_count + to[1]))
        return pairs

    def halve(a, axis, index, bit, high, low):
        mine = (index // bit) % 2
        a = a.reshape((high, 2, low) + a.shape[1:])
        sent = pick([a[:, 0], a[:, 1]], 1 - mine).reshape((high * low,) + a.shape[3:])
        kept = pick([a[:, 0], a[:, 1]], mine).reshape(sent.shape)
        return kept, lax.ppermute(sent, BOTH, pairs_of(axis, bit)), sent

    class Scatter:
        def __init__(self, halves, swap, many=1):
            bits = [1 << i for i in range(dp_count.bit_length() - 1)]
            order = [1] + (bits[1:] if swap else bits[:0:-1])
            left = list(reversed(bits))
            self.steps = []
            for bit in order:
                at = left.index(bit)
                self.steps.append((bit, many * 2**at, 2 ** (len(left) - 1 - at)))
                left.remove(bit)
            self.steps.pop(0)
            self.sent, self.kept = halves
            self.got = lax.ppermute(self.sent, BOTH, pairs_of("dp", 1))

        def step(self, *deps):
            bit, high, low = self.steps.pop(0)
            mine = ((dp_index // bit) % 2).astype(jnp.int32).reshape(1)
            self.sent, self.kept = join_split(self.kept, self.got, mine, high, low, deps)
            self.got = lax.ppermute(self.sent, BOTH, pairs_of("dp", bit))

        def last(self, *deps):
            while self.steps:
                self.step(*deps)
            return join_last(self.kept, self.got, deps)

    class SeqSum:
        def __init__(self, a):
            self.shape = a.shape
            self.a = a.astype(bf16).reshape(seq_count, -1, a.shape[1])
            bits = [1 << i for i in range(seq_count.bit_length() - 1)]
            left = list(reversed(bits))
            self.steps = []
            for bit in bits:
                at = left.index(bit)
                self.steps.append((bit, 2**at, 2 ** (len(left) - 1 - at)))
                left.remove(bit)
            self.back = list(reversed(bits))
            bit, high, low = self.steps.pop(0)
            self.kept, self.got, self.sent = halve(self.a, "seq", seq_index, bit, high, low)

        def step(self, *deps):
            if self.steps:
                bit, high, low = self.steps.pop(0)
                mine = ((seq_index // bit) % 2).astype(jnp.int32).reshape(1)
                self.sent, self.kept = join_split(self.kept, self.got, mine, high, low, deps)
                self.got = lax.ppermute(self.sent, BOTH, pairs_of("seq", bit))

        def whole(self):
            self.add()
            return self.finish()

        def add(self, *deps):
            while self.steps:
                self.step(*deps)
            self.a = join_last(self.kept, self.got, deps).reshape(self.kept.shape)

        def finish(self, *deps):
            a = self.a
            for bit in self.back:
                other = lax.ppermute(a, BOTH, pairs_of("seq", bit))
                low_half = (seq_index // bit) % 2 == 0
                pair = jnp.where(low_half, jnp.stack([a, other], 1), jnp.stack([other, a], 1))
                a = pair.reshape((-1,) + a.shape[1:])
            return a.reshape(self.shape)

    def by_dp(a):
        return a.reshape(dp_count, -1, a.shape[-1])

    def by_share(a):
        a = a.reshape(dp_count, width // dp_count, a.shape[1])
        out, sent = [], []
        for k in range(dp_count):
            piece = lax.dynamic_index_in_dim(a, dp_index ^ k, 0, keepdims=False)
            sent.append(piece)
            out.append(piece if k == 0 else lax.ppermute(piece, BOTH, pairs_of("dp", k)))
        return out, sent

    weight_tr = prep(conv_weight)

    x_blocks = blocks_to_team(frames)
    x_lows, x_highs = edges_to_team(frames)
    g_blocks = blocks_to_team(output_gradient)

    gaps = 1 + max(F - 2, 0) // UTT_LEAST
    spread = -(-(F + 2 * HALO + HALO * gaps) // 128) * 128
    out_spread = -(-(F + HALO * gaps) // 128) * 128
    (
        convolution_bias, query_offset_bias, value_offset_bias, attn_bias, first_gain, first_shift,
        inner_bias, outer_bias, second_gain, second_shift,
    ) = vectors = [
        v.reshape(1, -1)
        for v in (
            convolution_bias, query_offset_bias, value_offset_bias, attn_bias, first_gain, first_shift,
            inner_bias, outer_bias, second_gain, second_shift,
        )
    ]
    where_at = jnp.stack([row_id, member, rho % n]).astype(jnp.int32)
    x, spread_x, select, q_codes, k_codes = build_x(
        where_at, segments, x_blocks, x_lows, x_highs, team, F, gaps, spread, (weight_tr,)
    )
    conv_t = conv(spread_x, weight_tr, select, F, gaps)
    x_shares = lax.all_to_all(
        spread_x.reshape(dp_count, width // dp_count, spread), "dp", 0, 0, tiled=True
    )

    conv_before, pos_out, pos_low, query, kv = front(
        conv_t, convolution_bias, x, query_matrix, key_matrix, value_matrix, query_offset_bias,
        value_offset_bias, (x_shares, *g_blocks),
    )
    kvs = [kv] + [lax.ppermute(kv, BOTH, plan.team_pairs(s, True)) for s in range(1, team)]
    attn_low, lse = attn_fwd(query, kvs, q_codes, k_codes, (), 256)

    outs = mid(
        where_at, layer_keep, attn_low, pos_out, g_blocks, attn_weight, inner_weight, outer_weight,
        attn_bias, first_gain, first_shift, inner_bias, outer_bias, second_gain, second_shift, (),
    )
    layer_out = from_team(outs[:n])
    (
        first_low, inner_low, grad_outer_low, grad_inner_low, grad_attn_low, grad_first_sum,
        grad_heads, inner_sums, mid_sums,
    ) = outs[n:]
    core = (dp_index % 2).astype(jnp.int32).reshape(1)
    ff_share = inner_weight.shape[1] // dp_count
    by_rows = ff_share % 128 != 0
    outer_t = wg_plain(grad_outer_low, inner_low, 2, 0)
    outer_share = lax.psum_scatter(outer_t, "dp", scatter_dimension=0, tiled=True)
    extras = (inner_sums, mid_sums)
    pairs = width // 128
    grads = []
    deps = (outer_t,)
    grads.append(attn_bwd(query, grad_heads, attn_low, lse, kvs, q_codes, k_codes, 0, pairs, deps, 256))
    fars = [
        [lax.ppermute(g[2 + s], BOTH, plan.team_pairs(-s, True)) for s in range(1, team)]
        for g in grads
    ]
    if by_rows:
        inner_t = wg_plain(grad_inner_low, first_low, 1, 0, (grads[0][0],))
    else:
        inner_t = wg_plain(first_low, grad_inner_low, 2, ff_share, (grads[0][0],)).reshape(-1, ff_share)
    inner_share = lax.psum_scatter(inner_t, "dp", scatter_dimension=0, tiled=True)
    low_qk, low_v, grad_pos, grad_conv_low, qk_sums, v_sums = dpos(
        where_at, layer_keep, *[[g[k] for g in grads] for k in range(3)], fars, query_matrix,
        key_matrix, value_matrix, grad_first_sum, g_blocks, conv_before, (inner_t,),
    )

    d_pieces = build_d(where_at, segments, grad_conv_low, (), team, gaps, out_spread).reshape(
        dp_count, width // dp_count, out_spread
    )
    d_shares = lax.all_to_all(d_pieces, "dp", 0, 0, tiled=True)
    low, high = edges(grad_conv_low)
    slots = 2 * dp_count // 2
    qk_sum = Scatter(
        wg_rows(core, low_qk, pos_low, 2, dp_count, 1, (qk_sums,), (d_pieces,)), True, 2
    )
    halves = wg_rows(core, low_v, pos_low, 1, dp_count, 1, (v_sums,), (qk_sum.sent,), slots)
    halves = wg_rows(core, grad_attn_low, attn_low, 1, dp_count, 1, extras, (), slots, 1, halves)
    va_sum = Scatter(halves, False, 2)
    spread_d = build_d(
        where_at, segments, grad_conv_low, (low, high), team, gaps, spread, (va_sum.sent,)
    )
    part = conv_dw(x_shares, d_shares, gw, tap_blocks, (spread_d,))
    conv_sum = SeqSum(part)
    qk_sum.step(conv_sum.sent)
    va_sum.step(qk_sum.sent)
    groups = width // gw
    outer_z = SeqSum(outer_share)
    back_a = conv_dx(
        spread_d, weight_tr, select, F, gaps, 0, groups // 2, (outer_z.sent, va_sum.sent)
    )
    conv_sum.step(back_a)
    inner_z = SeqSum(inner_share)
    outer_z.step(conv_sum.sent)
    qk_sum.step(outer_z.sent)
    va_sum.step(qk_sum.sent)
    back_b = conv_dx(
        spread_d, weight_tr, select, F, gaps, groups // 2, groups - groups // 2,
        (va_sum.sent, inner_z.sent),
    )
    conv_sum.add(back_b, layer_out)
    qk_share = qk_sum.last(conv_sum.a)
    va_share = va_sum.last(qk_share)
    inner_z.step(va_share)
    proj = SeqSum(jnp.concatenate([qk_share, va_share], 0))
    outer_z.add(inner_z.sent)
    sent = grad_in(
        where_at, segments, grad_pos, (back_a, back_b), n, (outer_z.a, proj.sent)
    )
    grad_input = from_team(sent)
    proj.step(sent[0])
    outer_sum = outer_z.finish()
    conv_sum = conv_sum.finish()
    inner_z.add(proj.sent)
    proj.add(inner_z.a)
    grad_conv_weight = finish_dw(conv_sum, gw, tap_blocks)
    proj_pack = proj.finish().astype(f32)
    grad_conv_bias = conv_sum.reshape(-1, tap_blocks * gw + 32, DK * gw)[:, tap_blocks * gw, :gw].reshape(-1).astype(f32)
    o_g, i_g = widen((outer_sum, inner_z.finish()), (grad_conv_bias,))
    o_g = o_g.T
    i_g = i_g.T if by_rows else i_g

    share = width // dp_count
    ff = inner_bias.shape[1]
    pieces = proj_pack.reshape(4, -1, width)
    q_g, k_g, v_g, a_g = (pieces[k, :share].T for k in range(4))
    small = pieces[3, share : share + ff // width + 6]
    inner_bias_share = lax.dynamic_slice_in_dim(
        small[: ff // width].reshape(-1), dp_index * (ff // dp_count), ff // dp_count
    )
    rows_ = jnp.concatenate(
        [small[ff // width :], pieces[0, share : share + 1], pieces[2, share : share + 1]]
    )
    rows_ = lax.dynamic_slice_in_dim(rows_, dp_index * share, share, 1)
    vecs = [rows_[6], rows_[7]] + [rows_[k] for k in range(6)] + [grad_conv_bias]
    return (
        layer_out,
        grad_input,
        grad_conv_weight,
        vecs[8],
        q_g,
        vecs[0],
        k_g,
        v_g,
        vecs[1],
        a_g,
        vecs[2],
        vecs[3],
        vecs[4],
        i_g,
        inner_bias_share,
        o_g,
        vecs[5],
        vecs[6],
        vecs[7],
    )


def solution(mesh):
    rows = P("dp", "seq", None)
    by_col, vec = P(None, "dp"), P("dp")
    out_specs = (
        rows, rows, P(None, "dp", None), vec, by_col, vec, by_col, by_col, vec, by_col, vec, vec,
        vec, by_col, vec, by_col, vec, vec, vec,
    )
    return jax.shard_map(
        on_device, mesh=mesh, in_specs=(rows, rows) + (P(),) * 19, out_specs=out_specs, check_vma=False
    )
```

```python
import functools
import jax
import jax.numpy as jnp
from jax import lax
from jax.experimental import pallas as pl
from jax.experimental.pallas import tpu as pltpu
from jax.sharding import PartitionSpec as P


DK = 16
COST = pl.CostEstimate(flops=1000, bytes_accessed=1000, transcendentals=0)
ANY = pl.BlockSpec(memory_space=pl.ANY)

def prep_kernel(w_ref, wt_ref):
    gw = w_ref.shape[1]
    slots = w_ref.shape[2] // gw
    lane = lax.broadcasted_iota(jnp.int32, (gw, 128), 1)
    tiles = w_ref.shape[2] // 128
    for half in range(DK // slots):
        sums = [[None] * tiles for _ in range(slots)]
        for slot in range(slots):
            w = w_ref[half * slots + slot]
            for g in range(slots):
                turn = (slot - g) % slots
                moved = w if turn == 0 else pltpu.roll(w, gw * turn, 1)
                for t in range(tiles):
                    lo, hi = gw * slot - 128 * t, gw * (slot + 1) - 128 * t
                    if hi <= 0 or lo >= 128:
                        continue
                    part = moved[:, 128 * t : 128 * (t + 1)]
                    old = sums[g][t]
                    sums[g][t] = part if old is None else jnp.where(lane >= lo, part, old)
        for g in range(slots):
            for t in range(tiles):
                at = half * slots * gw + 128 * t
                wt_ref[g, :, at : at + 128] = sums[g][t]


def prep(w):
    k, width, gw = w.shape
    groups = width // gw
    nb = k // DK
    slots = 8
    assert (slots * gw) % 128 == 0 and DK % slots == 0 and groups % slots == 0
    return pl.pallas_call(
        prep_kernel,
        grid=(groups // slots, nb),
        in_specs=[pl.BlockSpec((DK, gw, slots * gw), lambda i, b: (b, 0, i))],
        out_specs=pl.BlockSpec((slots, gw, DK * gw), lambda i, b: (i, b, 0)),
        out_shape=jax.ShapeDtypeStruct((groups, nb * gw, DK * gw), w.dtype),
        cost_estimate=COST,
        name="prep",
    )(jnp.transpose(w, (0, 2, 1)))

def ungap(acc, sel_ref, F, nbound):
    out = acc[:, :F]
    for n in range(1, nbound + 1):
        moved = pltpu.roll(acc, acc.shape[1] - HALO * n, 1)[:, :F]
        out = jnp.where(sel_ref[n : n + 1, :] > 0, moved, out)
    return out


def conv_kernel(xt_ref, wt_ref, sel_ref, out_ref, *refs, nb, gw, F, nbound, G):
    stacks, sums = refs[:G], refs[G:]
    tin = xt_ref.shape[1]
    for g in range(G):
        x = xt_ref[g*gw:(g+1)*gw, :]
        for dk in range(DK):
            stacks[g][gw*dk:gw*(dk+1), :] = x if dk == 0 else pltpu.roll(x, tin - dk, 1)
    for g in range(G):
        sums[g][...] = jnp.dot(wt_ref[g], stacks[g][...], preferred_element_type=jnp.float32)
    for g in range(G):
        acc = sums[g][0:gw, :]
        for b in range(1, nb):
            acc = acc + pltpu.roll(sums[g][gw*b:gw*(b+1), :], tin - DK*b, 1)
        out_ref[g*gw:(g+1)*gw, :] = ungap(acc, sel_ref, F, nbound)


def conv(xt, wt, sel, F, nbound, G=2):
    width, tin = xt.shape
    g, nbgw, dkgw = wt.shape
    gw = width // g
    return pl.pallas_call(
        functools.partial(conv_kernel, nb=nbgw // gw, gw=gw, F=F, nbound=nbound, G=G),
        grid=(g // G,),
        in_specs=[pl.BlockSpec((G*gw, tin), lambda i: (i, 0)),
                  pl.BlockSpec((G, nbgw, dkgw), lambda i: (i, 0, 0)),
                  pl.BlockSpec(sel.shape, lambda i: (0, 0))],
        out_specs=pl.BlockSpec((G*gw, F), lambda i: (i, 0)),
        out_shape=jax.ShapeDtypeStruct((width, F), jnp.float32),
        scratch_shapes=[pltpu.VMEM((dkgw, tin), jnp.bfloat16)] * G + [pltpu.VMEM((nbgw, tin), jnp.float32)] * G,
        cost_estimate=COST,
        name="conv_fwd",
    )(xt, wt, sel)


def dx_kernel(dt_ref, wt_ref, sel_ref, *refs, nb, gw, F, nbound, G):
    out_ref, refs = refs[-1 - 2*G], refs[-2*G:]
    stacks, sums = refs[:G], refs[G:]
    tin = dt_ref.shape[1]
    for g in range(G):
        d = dt_ref[g*gw:(g+1)*gw, :]
        for b in range(nb):
            stacks[g][gw*b:gw*(b+1), :] = d if b == 0 else pltpu.roll(d, DK*b, 1)
    for g in range(G):
        sums[g][...] = jnp.dot(wt_ref[g].T, stacks[g][...], preferred_element_type=jnp.float32)
    for g in range(G):
        acc = sums[g][0:gw, :]
        for dk in range(1, DK):
            acc = acc + pltpu.roll(sums[g][gw*dk:gw*(dk+1), :], dk, 1)
        out_ref[g*gw:(g+1)*gw, :] = ungap(acc[:, 2*HALO:], sel_ref, F, nbound)


def conv_dx(dt, wt, sel, F, nbound, first, count, deps, G=2):
    width, tin = dt.shape
    g, nbgw, dkgw = wt.shape
    gw = width // g
    first = first // G
    return pl.pallas_call(
        functools.partial(dx_kernel, nb=nbgw // gw, gw=gw, F=F, nbound=nbound, G=G),
        grid=(count // G,),
        in_specs=[pl.BlockSpec((G*gw, tin), lambda i: (i + first, 0)),
                  pl.BlockSpec((G, nbgw, dkgw), lambda i: (i + first, 0, 0)),
                  pl.BlockSpec(sel.shape, lambda i: (0, 0))] + [ANY] * len(deps),
        out_specs=pl.BlockSpec((G*gw, F), lambda i: (i, 0)),
        out_shape=jax.ShapeDtypeStruct((count * gw, F), jnp.float32),
        scratch_shapes=[pltpu.VMEM((nbgw, tin), jnp.bfloat16)] * G + [pltpu.VMEM((dkgw, tin), jnp.float32)] * G,
        cost_estimate=COST,
        name="conv_dx",
    )(dt, wt, sel, *deps)


def dw_kernel(*refs, nb, gw, m):
    x_refs, d_refs = refs[:m], refs[m : 2 * m]
    out_ref, a0_ref, ds_ref = refs[-3:]
    tin = x_refs[0].shape[2]
    tout = d_refs[0].shape[2]
    ones = jnp.ones((16, tout), jnp.bfloat16)
    bias = None
    for s in range(m):
        x, d = x_refs[s][0], d_refs[s][0]
        part = lax.dot_general(ones, d, (((1,), (1,)), ((), ())), preferred_element_type=jnp.float32)
        bias = part if bias is None else bias + part
        d = jnp.concatenate([d, jnp.zeros((gw, tin - tout), d.dtype)], axis=1)
        slot = s % 2
        for dk in range(DK):
            a0_ref[slot, gw*dk:gw*(dk+1), :] = x if dk == 0 else pltpu.roll(x, tin - dk, 1)
        for b in range(nb):
            ds_ref[slot, gw*b:gw*(b+1), :] = d if b == 0 else pltpu.roll(d, DK*b, 1)
        p = lax.dot_general(
            ds_ref[slot], a0_ref[slot], (((1,), (1,)), ((), ())), preferred_element_type=jnp.float32
        )
        if s == 0:
            out_ref[: nb*gw, :] = p
        else:
            out_ref[: nb*gw, :] += p
    out_ref[nb*gw :, :] = jnp.zeros((out_ref.shape[0] - nb*gw, out_ref.shape[1]), jnp.float32)
    out_ref[nb*gw : nb*gw + 16, :gw] = bias


def conv_dw(xs, ds, gw, nb, deps):
    m, channels, tin = xs.shape
    tout = ds.shape[2]
    rows = nb*gw + 32
    flops = 2 * m * nb*gw * DK*gw * tin
    return pl.pallas_call(
        functools.partial(dw_kernel, nb=nb, gw=gw, m=m),
        grid=(channels // gw,),
        in_specs=[pl.BlockSpec((1, gw, tin), lambda i, k=k: (k, i, 0)) for k in range(m)]
        + [pl.BlockSpec((1, gw, tout), lambda i, k=k: (k, i, 0)) for k in range(m)]
        + [ANY] * len(deps),
        out_specs=pl.BlockSpec((rows, DK*gw), lambda i: (i, 0)),
        scratch_shapes=[pltpu.VMEM((2, DK*gw, tin), jnp.bfloat16), pltpu.VMEM((2, nb*gw, tin), jnp.bfloat16)],
        out_shape=jax.ShapeDtypeStruct((channels // gw * rows, DK*gw), jnp.float32),
        cost_estimate=COST,
        name="conv_dw",
    )(*([xs] * m), *([ds] * m), *deps)


def join_kernel(mine_ref, ks_ref, kk_ref, gs_ref, gk_ref, *refs):
    sent_ref, kept_ref = refs[-2:]
    sent_ref[...] = (ks_ref[...].astype(jnp.float32) + gs_ref[...].astype(jnp.float32)).astype(sent_ref.dtype)
    kept_ref[...] = (kk_ref[...].astype(jnp.float32) + gk_ref[...].astype(jnp.float32)).astype(kept_ref.dtype)


def pieces_of(rows, cols):
    while rows * cols > 640 * 1024 and rows % 32 == 0:
        rows //= 2
    while rows * cols > 640 * 1024 and cols % 256 == 0:
        cols //= 2
    return rows, cols


def join_split(kept, got, mine, high, low, deps):
    n, rows, cols = kept.shape
    r, c = pieces_of(rows, cols)

    def half(other):
        def at(i, j, k, mine_ref):
            side = 1 - mine_ref[0] if other else mine_ref[0]
            return ((i // low * 2 + side) * low + i % low, j, k)

        return pl.BlockSpec((1, r, c), at)

    out = pl.BlockSpec((1, r, c), lambda i, j, k, mine_ref: (i, j, k))
    shape = jax.ShapeDtypeStruct((n // 2, rows, cols), kept.dtype)
    return pl.pallas_call(
        join_kernel,
        grid_spec=pltpu.PrefetchScalarGridSpec(
            num_scalar_prefetch=1,
            grid=(n // 2, rows // r, cols // c),
            in_specs=[half(True), half(False), half(True), half(False)] + [ANY] * len(deps),
            out_specs=[out, out],
        ),
        out_shape=[shape, shape],
        cost_estimate=COST,
        name="join",
    )(mine, kept, kept, got, got, *deps)


def join_last_kernel(k_ref, g_ref, *refs):
    refs[-1][...] = (k_ref[...].astype(jnp.float32) + g_ref[...].astype(jnp.float32)).astype(refs[-1].dtype)


def join_last(kept, got, deps):
    n, rows, cols = kept.shape
    r, c = pieces_of(rows, cols)
    block = pl.BlockSpec((1, r, c), lambda i, j, k: (i, j, k))
    return pl.pallas_call(
        join_last_kernel,
        grid=(n, rows // r, cols // c),
        in_specs=[block, block] + [ANY] * len(deps),
        out_specs=block,
        out_shape=jax.ShapeDtypeStruct(kept.shape, kept.dtype),
        cost_estimate=COST,
        name="join_last",
    )(kept, got, *deps).reshape(-1, kept.shape[-1])


def finish_kernel(p_ref, *refs, nb, gw):
    out_ref, e_ref, q_ref = refs[-3:]
    dkgw = DK * gw

    @pl.when(pl.program_id(0) == 0)
    def _():
        row = lax.broadcasted_iota(jnp.int32, (dkgw, dkgw), 0)
        col = lax.broadcasted_iota(jnp.int32, (1, dkgw), 1)
        e_ref[...] = (row == (col % DK) * gw + col // DK).astype(e_ref.dtype)

    per = 128 // DK
    lane_block = lax.broadcasted_iota(jnp.int32, (gw, 128), 1) // DK
    q_ref[...] = jnp.dot(
        p_ref[: nb * gw, :], e_ref[...], preferred_element_type=jnp.float32
    ).astype(q_ref.dtype)
    for tile in range(dkgw // 128):
        outs = [None] * per
        for b in range(nb):
            piece = q_ref[gw*b:gw*(b+1), 128*tile:128*(tile+1)]
            for i in range(per):
                turn = (b - i) % per
                moved = piece if turn == 0 else pltpu.roll(piece, DK * turn, 1)
                outs[i] = moved if outs[i] is None else jnp.where(lane_block == b, moved, outs[i])
        for i in range(per):
            out_ref[tile * per + i] = outs[i].astype(out_ref.dtype)


def finish_dw(p, gw, nb):
    assert nb * DK == 128
    rows = nb*gw + 32
    g = p.shape[0] // rows
    out = pl.pallas_call(
        functools.partial(finish_kernel, nb=nb, gw=gw),
        grid=(g,),
        in_specs=[pl.BlockSpec((rows, DK*gw), lambda i: (i, 0))],
        out_specs=pl.BlockSpec((gw, gw, 128), lambda i: (i, 0, 0)),
        out_shape=jax.ShapeDtypeStruct((g*gw, gw, 128), jnp.float32),
        scratch_shapes=[pltpu.VMEM((DK*gw, DK*gw), jnp.bfloat16), pltpu.VMEM((nb*gw, DK*gw), jnp.bfloat16)],
        cost_estimate=COST,
        name="finish_dw",
    )(p)
    return jnp.transpose(out, (2, 0, 1))


def wg_rows_kernel(mine_ref, lhs_ref, rhs_ref, *refs, many, dp, nextra, ndeps):
    extra_refs = refs[:nextra]
    sent_ref, kept_ref, lt_ref, ls_ref, lk_ref = refs[nextra + ndeps :]
    half = many * dp // 2
    share = lhs_ref.shape[1] // (many * dp)
    cols = sent_ref.shape[2]
    mine = mine_ref[0]

    @pl.when(pl.program_id(0) == 0)
    def _():
        lt_ref[...] = lhs_ref[...].T
        for i in range(half):
            for to_ref, side in ((ls_ref, 1 - mine), (lk_ref, mine)):
                at = pl.multiple_of((2 * i + side) * share, 16)
                to_ref[i * share : (i + 1) * share, :] = lt_ref[pl.ds(at, share), :]

    for out_ref, l_ref in ((sent_ref, ls_ref), (kept_ref, lk_ref)):
        total = jnp.dot(l_ref[...], rhs_ref[...], preferred_element_type=jnp.float32)
        for i in range(half):
            out_ref[i, :share, :] = total[i * share : (i + 1) * share, :].astype(out_ref.dtype)
    if nextra:
        for m in range(many):
            rows = []
            for r in extra_refs:
                if many > 1:
                    rows.append(r[0:1, m * cols : (m + 1) * cols])
                else:
                    rows += [r[0:1, k * cols : (k + 1) * cols] for k in range(r.shape[1] // cols)]
            rows.append(jnp.zeros((16 - len(rows), cols), jnp.float32))
            block = jnp.concatenate(rows, 0).astype(jnp.bfloat16)
            for i in range(dp // 2):
                sent_ref[m * dp // 2 + i, share:, :] = block
                kept_ref[m * dp // 2 + i, share:, :] = block


def wg_rows(mine, lhs, rhs, many, dp, chunks, extras=(), deps=(), slots=None, first=0, into=()):
    F, M = lhs.shape
    N = rhs.shape[1]
    share = M // (many * dp)
    half = many * dp // 2
    rows = share + (16 if extras else 0)
    out = pl.BlockSpec((half, rows, N // chunks), lambda i, m: (first, 0, i))
    shape = jax.ShapeDtypeStruct((slots or half, rows, N), jnp.bfloat16)
    deps = tuple(into) + tuple(deps)
    at = 3 + len(extras)
    return pl.pallas_call(
        functools.partial(wg_rows_kernel, many=many, dp=dp, nextra=len(extras), ndeps=len(deps)),
        input_output_aliases={at: 0, at + 1: 1} if into else {},
        grid_spec=pltpu.PrefetchScalarGridSpec(
            num_scalar_prefetch=1,
            grid=(chunks,),
            in_specs=[
                pl.BlockSpec((F, M), lambda i, m: (0, 0)),
                pl.BlockSpec((F, N // chunks), lambda i, m: (0, i)),
            ]
            + [pl.BlockSpec(e.shape, lambda i, m: (0, 0)) for e in extras]
            + [ANY] * len(deps),
            out_specs=[out, out],
            scratch_shapes=[
                pltpu.VMEM((M, F), jnp.bfloat16),
                pltpu.VMEM((half * share, F), jnp.bfloat16),
                pltpu.VMEM((half * share, F), jnp.bfloat16),
            ],
        ),
        out_shape=[shape, shape],
        cost_estimate=COST,
        name="wg_rows",
    )(mine, lhs, rhs, *extras, *deps)


def wg_plain_kernel(lhs_ref, rhs_ref, *refs, share):
    out_ref, lt_ref = refs[-2:]

    @pl.when(pl.program_id(0) == 0)
    def _():
        lt_ref[...] = lhs_ref[...].T

    total = jnp.dot(lt_ref[...], rhs_ref[...], preferred_element_type=jnp.float32).astype(jnp.bfloat16)
    if share:
        for k in range(out_ref.shape[0]):
            out_ref[k] = total[:, k * share : (k + 1) * share]
    else:
        out_ref[...] = total


def wg_plain(lhs, rhs, chunks, share, deps=()):
    F, M = lhs.shape
    N = rhs.shape[1]
    cols = N // chunks
    if share:
        spec = pl.BlockSpec((cols // share, M, share), lambda i: (i, 0, 0))
        shape = jax.ShapeDtypeStruct((N // share, M, share), jnp.bfloat16)
    else:
        spec = pl.BlockSpec((M, cols), lambda i: (0, i))
        shape = jax.ShapeDtypeStruct((M, N), jnp.bfloat16)
    return pl.pallas_call(
        functools.partial(wg_plain_kernel, share=share),
        grid=(chunks,),
        in_specs=[pl.BlockSpec((F, M), lambda i: (0, 0)), pl.BlockSpec((F, cols), lambda i: (0, i))]
        + [ANY] * len(deps),
        out_specs=spec,
        scratch_shapes=[pltpu.VMEM((M, F), jnp.bfloat16)],
        out_shape=shape,
        cost_estimate=COST,
        name="wg_plain",
    )(lhs, rhs, *deps)


def dpos_kernel(at_ref, keep_ref, *refs, parts, far, n, ndeps):
    qs, ks, vs = refs[:parts], refs[parts : 2 * parts], refs[2 * parts : 3 * parts]
    far_refs, refs = refs[3 * parts : (3 + far) * parts], refs[(3 + far) * parts :]
    wq_ref, wk_ref, wv_ref, first_ref, conv_ref = refs[:5]
    g_refs = refs[5 : 5 + n]
    low_ref, lowv_ref, pos_ref, d_ref, qk_ref, v_ref = refs[5 + n + ndeps :]
    turn = (at_ref[2] - pl.program_id(0) + n) % n
    dq = jnp.concatenate([r[...] for r in qs], 1)
    dks, dvs = [], []
    for p in range(parts):
        dk, dv = ks[p][...], vs[p][...]
        for r in far_refs[p * far : (p + 1) * far]:
            dk = dk + r[0].astype(jnp.float32)
            dv = dv + r[1].astype(jnp.float32)
        dks.append(dk.astype(jnp.bfloat16))
        dvs.append(dv.astype(jnp.bfloat16))
    dk, dv = jnp.concatenate(dks, 1), jnp.concatenate(dvs, 1)
    width = dq.shape[1]
    low_ref[:, :width] = dq
    low_ref[:, width:] = dk
    lowv_ref[...] = dv
    total = first_ref[...] + (1.0 - (keep_ref[at_ref[0]] > 0).astype(jnp.float32)) * picked(g_refs, turn).astype(jnp.float32)
    for low, w_ref in ((dq, wq_ref), (dk, wk_ref), (dv, wv_ref)):
        total = total + lax.dot_general(
            low, w_ref[...], (((1,), (1,)), ((), ())), preferred_element_type=jnp.float32
        )
    pos_ref[...] = total
    d_ref[...] = (total * gelu_slope(conv_ref[...])).astype(d_ref.dtype)
    sums = [jnp.sum(low.astype(jnp.float32), 0, keepdims=True) for low in (dq, dk, dv)]

    @pl.when(pl.program_id(0) == 0)
    def _():
        qk_ref[...] = jnp.zeros_like(qk_ref)
        v_ref[...] = jnp.zeros_like(v_ref)

    qk_ref[0:1, :width] += sums[0]
    qk_ref[0:1, width:] += sums[1]
    v_ref[0:1, :] += sums[2]


def dpos(at, keep, dqs, dks, dvs, fars, wq, wk, wv, first, gs, conv_before, deps):
    F, W = first.shape
    n = len(gs)
    rows = F // n
    parts = len(dqs)
    part = pl.BlockSpec((rows, W // parts), lambda i, at, k: (i, 0))
    block = pl.BlockSpec((rows, W), lambda i, at, k: (i, 0))
    whole = pl.BlockSpec((W, W), lambda i, at, k: (0, 0))
    return pl.pallas_call(
        functools.partial(dpos_kernel, parts=parts, far=len(fars[0]), n=n, ndeps=len(deps)),
        grid_spec=pltpu.PrefetchScalarGridSpec(
            num_scalar_prefetch=2,
            grid=(F // rows,),
            in_specs=[part] * (3 * parts)
            + [pl.BlockSpec((2, rows, W // parts), lambda i, at, k: (0, i, 0))] * (parts * len(fars[0]))
            + [whole] * 3 + [block] * 2 + [pl.BlockSpec((rows, W), lambda i, at, k: (0, 0))] * n + [ANY] * len(deps),
            out_specs=[
                pl.BlockSpec((rows, 2 * W), lambda i, at, k: (i, 0)), block, block, block,
                pl.BlockSpec((8, 2 * W), lambda i, at, k: (0, 0)),
                pl.BlockSpec((8, W), lambda i, at, k: (0, 0)),
            ],
        ),
        out_shape=[
            jax.ShapeDtypeStruct((F, 2 * W), jnp.bfloat16),
            jax.ShapeDtypeStruct((F, W), jnp.bfloat16),
            jax.ShapeDtypeStruct((F, W), jnp.float32),
            jax.ShapeDtypeStruct((F, W), jnp.bfloat16),
            jax.ShapeDtypeStruct((8, 2 * W), jnp.float32),
            jax.ShapeDtypeStruct((8, W), jnp.float32),
        ],
        cost_estimate=COST,
        name="dpos",
    )(at, keep, *dqs, *dks, *dvs, *[f for part in fars for f in part], wq, wk, wv, first, conv_before, *gs, *deps)


def front_kernel(conv_ref, bias_ref, x_ref, wq_ref, wk_ref, wv_ref, bq_ref, bv_ref, *refs):
    cb_ref, pos_ref, low_ref, q_ref, kv_ref = refs[-5:]
    before = conv_ref[...].T + bias_ref[...]
    cb_ref[...] = before
    pos = x_ref[...].astype(jnp.float32) + gelu(before)
    pos_ref[...] = pos
    low = pos.astype(jnp.bfloat16)
    low_ref[...] = low
    width = low.shape[1]
    q_ref[...] = (jnp.dot(low, wq_ref[...], preferred_element_type=jnp.float32) + bq_ref[...]).astype(jnp.bfloat16)
    kv_ref[:, :width] = jnp.dot(low, wk_ref[...], preferred_element_type=jnp.float32).astype(jnp.bfloat16)
    kv_ref[:, width:] = (
        jnp.dot(low, wv_ref[...], preferred_element_type=jnp.float32) + bv_ref[...]
    ).astype(jnp.bfloat16)


def front(conv_t, bias, x, wq, wk, wv, bq, bv, deps):
    W, F = conv_t.shape
    rows = min(256, F)
    block = pl.BlockSpec((rows, W), lambda i: (i, 0))
    whole = pl.BlockSpec((W, W), lambda i: (0, 0))
    vec = pl.BlockSpec((1, W), lambda i: (0, 0))
    return pl.pallas_call(
        front_kernel,
        grid=(F // rows,),
        in_specs=[pl.BlockSpec((W, rows), lambda i: (0, i)), vec, block]
        + [whole] * 3 + [vec] * 2 + [ANY] * len(deps),
        out_specs=[block] * 4 + [pl.BlockSpec((rows, 2 * W), lambda i: (i, 0))],
        out_shape=[
            jax.ShapeDtypeStruct((F, W), jnp.float32),
            jax.ShapeDtypeStruct((F, W), jnp.float32),
            jax.ShapeDtypeStruct((F, W), jnp.bfloat16),
            jax.ShapeDtypeStruct((F, W), jnp.bfloat16),
            jax.ShapeDtypeStruct((F, 2 * W), jnp.bfloat16),
        ],
        cost_estimate=COST,
        name="front",
    )(conv_t, bias.reshape(1, W), x, wq, wk, wv, bq.reshape(1, W), bv.reshape(1, W), *deps)


def picked(refs, index):
    out = refs[0][...]
    for m in range(1, len(refs)):
        out = jnp.where(index == m, refs[m][...], out)
    return out


def mid_kernel(at_ref, keep_ref, attn_ref, pos_ref, *refs, n, ndeps, chunk):
    g_refs, refs = refs[:n], refs[n:]
    (wa_ref, wi_ref, wo_ref, ba_ref, g1_ref, s1_ref, bi_ref, bo_ref, g2_ref, s2_ref), refs = refs[:10], refs[10:]
    out_refs, refs = refs[ndeps : ndeps + n], refs[ndeps + n :]
    (
        first_ref, inner_ref, douter_ref, dinner_ref, dattn_ref, dfirst_ref, dheads_ref,
        inner_sum_ref, sums_ref, slope_ref,
    ) = refs
    keep = (keep_ref[at_ref[0]] > 0).astype(jnp.float32)
    turn = (at_ref[2] - pl.program_id(0) + n) % n
    width = pos_ref.shape[1]
    ff = wi_ref.shape[1]
    pos = pos_ref[...]
    attn_out = jnp.dot(attn_ref[...], wa_ref[...], preferred_element_type=jnp.float32) + ba_ref[...]
    first_normed, first_scale = layer_norm(pos + attn_out)
    first_out = first_normed * g1_ref[...] + s1_ref[...]
    first_low = first_out.astype(jnp.bfloat16)
    first_ref[...] = first_low
    total = None
    for c in range(0, ff, chunk):
        cols = slice(c, c + chunk)
        pre = jnp.dot(first_low, wi_ref[:, cols], preferred_element_type=jnp.float32) + bi_ref[:, cols]
        phi = 0.5 * (1.0 + lax.erf(pre * root_half))
        slope_ref[:, cols] = phi + pre * jnp.exp(-0.5 * pre * pre) * inv_root_two_pi
        low = (pre * phi).astype(jnp.bfloat16)
        inner_ref[:, cols] = low
        part = jnp.dot(low, wo_ref[cols, :], preferred_element_type=jnp.float32)
        total = part if total is None else total + part
    second_normed, second_scale = layer_norm(first_out + (total + bo_ref[...]))
    second_out = second_normed * g2_ref[...] + s2_ref[...]
    layer = (keep * second_out + (1.0 - keep) * pos).astype(jnp.bfloat16)
    for m in range(n):
        @pl.when(turn == m)
        def _(m=m):
            out_refs[m][...] = layer

    grad_layer = keep * picked(g_refs, turn).astype(jnp.float32)
    d_second = norm_back(grad_layer * g2_ref[...], second_normed, second_scale)
    d_outer = d_second.astype(jnp.bfloat16)
    douter_ref[...] = d_outer

    @pl.when(pl.program_id(0) == 0)
    def _():
        inner_sum_ref[...] = jnp.zeros_like(inner_sum_ref)
        sums_ref[...] = jnp.zeros_like(sums_ref)

    d_first_out = d_second
    for c in range(0, ff, chunk):
        cols = slice(c, c + chunk)
        d_inner = (
            lax.dot_general(d_outer, wo_ref[cols, :], (((1,), (1,)), ((), ())), preferred_element_type=jnp.float32)
            * slope_ref[:, cols]
        ).astype(jnp.bfloat16)
        dinner_ref[:, cols] = d_inner
        inner_sum_ref[0:1, cols] += jnp.sum(d_inner.astype(jnp.float32), 0, keepdims=True)
        d_first_out = d_first_out + lax.dot_general(
            d_inner, wi_ref[:, cols], (((1,), (1,)), ((), ())), preferred_element_type=jnp.float32
        )
    d_first = norm_back(d_first_out * g1_ref[...], first_normed, first_scale)
    dfirst_ref[...] = d_first
    d_attn = d_first.astype(jnp.bfloat16)
    dattn_ref[...] = d_attn
    dheads_ref[...] = lax.dot_general(
        d_attn, wa_ref[...], (((1,), (1,)), ((), ())), preferred_element_type=jnp.float32
    ).astype(jnp.bfloat16)
    for k, v in enumerate((
        d_attn.astype(jnp.float32), d_first_out * first_normed, d_first_out,
        d_outer.astype(jnp.float32), grad_layer * second_normed, grad_layer,
    )):
        sums_ref[0:1, k * width : (k + 1) * width] += jnp.sum(v, 0, keepdims=True)


def mid(at, keep, attn_low, pos_out, gs, wa, wi, wo, ba, g1, s1, bi, bo, g2, s2, deps):
    F, W = pos_out.shape
    ff = wi.shape[1]
    n = len(gs)
    rows = F // n
    block = pl.BlockSpec((rows, W), lambda i, at, k: (i, 0))
    wide = pl.BlockSpec((rows, ff), lambda i, at, k: (i, 0))

    def whole(*shape):
        return pl.BlockSpec(shape, lambda i, at, k: (0,) * len(shape))

    vec = whole(1, W)
    out = lambda cols, kind: jax.ShapeDtypeStruct((F, cols), kind)
    bf, fl = jnp.bfloat16, jnp.float32
    return pl.pallas_call(
        functools.partial(mid_kernel, n=n, ndeps=len(deps), chunk=min(768, ff)),
        grid_spec=pltpu.PrefetchScalarGridSpec(
            num_scalar_prefetch=2,
            grid=(F // rows,),
            in_specs=[block, block] + [whole(rows, W)] * n + [whole(W, W), whole(W, ff), whole(ff, W), vec, vec, vec, whole(1, ff), vec, vec, vec]
            + [ANY] * len(deps),
            out_specs=[whole(rows, W)] * n + [block, wide, block, wide, block, block, block, whole(8, ff), whole(8, 6 * W)],
            scratch_shapes=[pltpu.VMEM((rows, ff), jnp.float32)],
        ),
        out_shape=[
            *[jax.ShapeDtypeStruct((rows, W), bf)] * n, out(W, bf), out(ff, bf), out(W, bf), out(ff, bf), out(W, bf), out(W, fl), out(W, bf),
            jax.ShapeDtypeStruct((8, ff), fl), jax.ShapeDtypeStruct((8, 6 * W), fl),
        ],
        cost_estimate=COST,
        name="mid",
    )(
        at, keep, attn_low, pos_out, *gs, wa, wi, wo, ba.reshape(1, W), g1.reshape(1, W), s1.reshape(1, W),
        bi.reshape(1, ff), bo.reshape(1, W), g2.reshape(1, W), s2.reshape(1, W), *deps,
    )


def place(ext, before, gaps, length):
    rows, have = ext.shape
    ext = jnp.concatenate([ext, jnp.zeros((rows, length - have), ext.dtype)], 1) if length > have else ext
    if length > have:
        before = jnp.concatenate([before, jnp.full((before.shape[0], length - have), -1, before.dtype)], 1)
    total = None
    for k in range(gaps + 1):
        moved = ext if k == 0 else pltpu.roll(ext, HALO * k, 1)
        here = (before if k == 0 else pltpu.roll(before, HALO * k, 1))[0:1, :] == k
        total = jnp.where(here, moved, jnp.zeros((), ext.dtype) if total is None else total)
    return total


def window_of(seg_ref, wide_ref, row, member, F):
    T = seg_ref.shape[1]
    wide_ref[...] = jnp.zeros_like(wide_ref)
    wide_ref[:, 128 : 128 + T] = jnp.broadcast_to(seg_ref[pl.ds(row % 8, 1), :], (8, T))
    start = pl.multiple_of(member * F, 128)
    window = wide_ref[:, pl.ds(start, F + 256)]
    return pltpu.roll(window, F + 256 - HALO, 1)[:, : F + 2 * HALO]


def ordinals(window, F):
    lane = lax.broadcasted_iota(jnp.int32, window.shape, 1)
    local = (lane >= HALO) & (lane < HALO + F)
    most = jnp.max(jnp.where(local, window, 0), axis=1, keepdims=True)
    first = jnp.sum(jnp.where(lane == HALO, window, 0), axis=1, keepdims=True)
    last = jnp.sum(jnp.where(lane == HALO + F - 1, window, 0), axis=1, keepdims=True)
    number = jnp.where(window > 0, window, most + 1)
    number_first = jnp.where(first > 0, first, most + 1)
    number_last = jnp.where(last > 0, last, most + 1)
    before = number - number_first
    before = jnp.where((lane < HALO) & (window != first), -1, before)
    right = jnp.where(window == last, number_last - number_first, -1)
    return jnp.where(lane >= HALO + F, right, before)


def column(row):
    return row.astype(jnp.float32).T[:, 0:1]


def build_x_kernel(at_ref, seg_ref, *refs, n, nlow, nhigh, team, F, gaps, spread):
    row, member = at_ref[0], at_ref[1]
    j = at_ref[2]
    got, lows, highs = refs[:n], refs[n : n + nlow], refs[n + nlow : n + nlow + nhigh]
    x_ref, spread_ref, sel_ref, qc_ref, kc_ref, wide_ref = refs[-6:]
    zero = jnp.zeros((), jnp.bfloat16)
    blocks = []
    for w in range(n):
        part = got[0][...]
        for m in range(1, n):
            part = jnp.where((j - w + n) % n == m, got[m][...], part)
        blocks.append(part)

    def edge(parts, on):
        part = parts[0][...]
        for m in range(1, len(parts)):
            part = jnp.where(j == m, parts[m][...], part)
        return jnp.where(on, part, zero)

    window = window_of(seg_ref, wide_ref, row, member, F)
    before = ordinals(window, F)
    ext = jnp.concatenate([edge(lows, member > 0)] + blocks + [edge(highs, member < team - 1)], 0)
    ext_t = jnp.where(window[0:1, :] > 0, ext.T, zero)
    spread_ref[...] = place(ext_t, before, gaps, spread)
    local = pltpu.roll(window, F + 2 * HALO - HALO, 1)[:, :F]
    before_local = pltpu.roll(before, F + 2 * HALO - HALO, 1)[:, :F]
    which = lax.broadcasted_iota(jnp.int32, (8, F), 0)
    sel_ref[...] = (before_local == which).astype(jnp.float32)
    seg_col = column(local)
    length = F // n
    for w in range(n):
        rows = slice(w * length, (w + 1) * length)
        x_ref[rows, :] = jnp.where(seg_col[rows] > 0, blocks[w], zero)
    lane = lax.broadcasted_iota(jnp.int32, (1, 128), 1) % 64
    qc_ref[...] = (seg_col == lane.astype(jnp.float32)).astype(jnp.bfloat16)
    for s in range(team):
        start = pl.multiple_of(128 + (member - s + team) % team * F, 128)
        keys = column(wide_ref[:, pl.ds(start, F)])
        kc_ref[s * F : (s + 1) * F, :] = jnp.where(
            (keys == lane.astype(jnp.float32)) & (lane > 0), 0.0, -1e30
        ).astype(jnp.bfloat16)


def build_x(at, segments, got, lows, highs, team, F, gaps, spread, deps):
    n, W = len(got), got[0].shape[1]
    T = segments.shape[1]
    whole = pl.BlockSpec(memory_space=pltpu.VMEM)
    out = lambda r, c, kind: jax.ShapeDtypeStruct((r, c), kind)

    def full(r, c):
        return pl.BlockSpec((r, c), lambda i, at: (0, 0))

    return pl.pallas_call(
        functools.partial(
            build_x_kernel, n=n, nlow=len(lows), nhigh=len(highs), team=team, F=F, gaps=gaps, spread=spread
        ),
        grid_spec=pltpu.PrefetchScalarGridSpec(
            num_scalar_prefetch=1,
            grid=(1,),
            in_specs=[pl.BlockSpec((8, T), lambda i, at: (at[0] // 8, 0))]
            + [full(*a.shape) for a in (*got, *lows, *highs)] + [ANY] * len(deps),
            out_specs=[full(F, W), full(W, spread), full(8, F), full(F, 128), full(team * F, 128)],
            scratch_shapes=[pltpu.VMEM((8, T + 256), jnp.int32)],
        ),
        out_shape=[
            out(F, W, jnp.bfloat16), out(W, spread, jnp.bfloat16), out(8, F, jnp.float32),
            out(F, 128, jnp.bfloat16), out(team * F, 128, jnp.bfloat16),
        ],
        cost_estimate=COST,
        name="build_x",
    )(at, segments, *got, *lows, *highs, *deps)


def build_d_kernel(at_ref, seg_ref, d_ref, *refs, edges, team, F, gaps, length):
    row, member = at_ref[0], at_ref[1]
    out_ref, wide_ref = refs[-2:]
    window = window_of(seg_ref, wide_ref, row, member, F)
    before = ordinals(window, F)
    zero = jnp.zeros((), jnp.bfloat16)
    if edges:
        low, high = refs[0][...], refs[1][...]
        ext = jnp.concatenate(
            [jnp.where(member > 0, low, zero), d_ref[...], jnp.where(member < team - 1, high, zero)], 0
        ).T
    else:
        ext = d_ref[...].T
        before = pltpu.roll(before, F + 2 * HALO - HALO, 1)[:, :F]
    out_ref[...] = place(ext, before, gaps, length)


def build_d(at, segments, d, edges, team, gaps, length, deps=()):
    F, W = d.shape
    T = segments.shape[1]

    def full(r, c):
        return pl.BlockSpec((r, c), lambda i, at: (0, 0))

    return pl.pallas_call(
        functools.partial(build_d_kernel, edges=bool(edges), team=team, F=F, gaps=gaps, length=length),
        grid_spec=pltpu.PrefetchScalarGridSpec(
            num_scalar_prefetch=1,
            grid=(1,),
            in_specs=[pl.BlockSpec((8, T), lambda i, at: (at[0] // 8, 0)), full(F, W)]
            + [full(*a.shape) for a in edges] + [ANY] * len(deps),
            out_specs=full(W, length),
            scratch_shapes=[pltpu.VMEM((8, T + 256), jnp.int32)],
        ),
        out_shape=jax.ShapeDtypeStruct((W, length), jnp.bfloat16),
        cost_estimate=COST,
        name="build_d",
    )(at, segments, d, *edges, *deps)


def widen_kernel(*refs, n):
    for k in range(n):
        refs[len(refs) - n + k][...] = refs[k][...].astype(jnp.float32)


def widen(arrays, deps):
    whole = pl.BlockSpec(memory_space=pltpu.VMEM)
    size = sum(a.size for a in arrays)
    return pl.pallas_call(
        functools.partial(widen_kernel, n=len(arrays)),
        in_specs=[whole] * len(arrays) + [ANY] * len(deps),
        out_specs=[whole] * len(arrays),
        out_shape=[jax.ShapeDtypeStruct(a.shape, jnp.float32) for a in arrays],
        cost_estimate=COST,
        name="widen",
    )(*arrays, *deps)


def grad_in_kernel(at_ref, seg_ref, pos_ref, *refs, n, nback, F):
    backs, out_refs, wide_ref = refs[:nback], refs[-1 - n : -1], refs[-1]
    window = window_of(seg_ref, wide_ref, at_ref[0], at_ref[1], F)
    live = column(pltpu.roll(window, F + 2 * HALO - HALO, 1)[:, :F]) > 0
    back = jnp.concatenate([b[...] for b in backs], 0).T
    total = jnp.where(live, pos_ref[...] + back, 0.0).astype(jnp.bfloat16)
    rows = F // n
    for w in range(n):
        for m in range(n):
            @pl.when((at_ref[2] - w + n) % n == m)
            def _(w=w, m=m):
                out_refs[m][...] = total[w * rows : (w + 1) * rows, :]


def grad_in(at, segments, pos, backs, n, deps):
    F, W = pos.shape
    T = segments.shape[1]

    def full(r, c):
        return pl.BlockSpec((r, c), lambda i, at: (0, 0))

    return pl.pallas_call(
        functools.partial(grad_in_kernel, n=n, nback=len(backs), F=F),
        grid_spec=pltpu.PrefetchScalarGridSpec(
            num_scalar_prefetch=1,
            grid=(1,),
            in_specs=[pl.BlockSpec((8, T), lambda i, at: (at[0] // 8, 0)), full(F, W)]
            + [full(*b.shape) for b in backs] + [ANY] * len(deps),
            out_specs=[full(F // n, W)] * n,
            scratch_shapes=[pltpu.VMEM((8, T + 256), jnp.int32)],
        ),
        out_shape=[jax.ShapeDtypeStruct((F // n, W), jnp.bfloat16)] * n,
        cost_estimate=COST,
        name="grad_in",
    )(at, segments, pos, *backs, *deps)


def stack_back_kernel(at_ref, *refs, n):
    index = (pl.program_id(0) - at_ref[0] + n) % n
    refs[-1][0] = picked(refs[:n], index)


def stack_back(at, blocks, deps):
    n = len(blocks)
    L, W = blocks[0].shape
    return pl.pallas_call(
        functools.partial(stack_back_kernel, n=n),
        grid_spec=pltpu.PrefetchScalarGridSpec(
            num_scalar_prefetch=1,
            grid=(n,),
            in_specs=[pl.BlockSpec((L, W), lambda i, at: (0, 0))] * n + [ANY] * len(deps),
            out_specs=pl.BlockSpec((1, L, W), lambda i, at: (i, 0, 0)),
        ),
        out_shape=jax.ShapeDtypeStruct((n, L, W), blocks[0].dtype),
        cost_estimate=COST,
        name="stack_back",
    )(at, *blocks, *deps)

HEAD = 64

def nt(a, b):
    return lax.dot_general(a, b, (((1,), (1,)), ((), ())), preferred_element_type=jnp.float32)

def attn_fwd_kernel(*refs, P, chunk):
    q_ref, qc_ref, kc_ref = refs[:3]
    k_refs = refs[3:3+P]
    v_refs = refs[3+P:3+2*P]
    o_ref, lse_ref, ka_ref, va_ref = refs[-4:]
    F = q_ref.shape[0]
    low_k = lax.broadcasted_iota(jnp.int32, (F, 128), 1) < HEAD
    low_q = lax.broadcasted_iota(jnp.int32, (chunk, 128), 1) < HEAD
    one = jnp.ones((), jnp.bfloat16)
    for h in range(2):
        pick = low_k if h == 0 else jnp.logical_not(low_k)
        for p in range(P):
            ka_ref[h, p*F:(p+1)*F, :] = jnp.where(pick, k_refs[p][...], kc_ref[p*F:(p+1)*F, :])
            va_ref[h, p*F:(p+1)*F, :] = jnp.where(pick, v_refs[p][...], one)
    for c in range(F // chunk):
        rows = slice(c*chunk, (c+1)*chunk)
        q = q_ref[rows, :] * jnp.asarray(0.125, jnp.bfloat16)
        outs, lses = [], []
        for h in range(2):
            pick = low_q if h == 0 else jnp.logical_not(low_q)
            qa = jnp.where(pick, q, qc_ref[rows, :])
            s = nt(qa, ka_ref[h])
            m = jnp.maximum(jnp.max(s, axis=1, keepdims=True), -1e20)
            e = jnp.exp(s - m).astype(jnp.bfloat16)
            o = jnp.dot(e, va_ref[h], preferred_element_type=jnp.float32)
            l = jnp.maximum(o[:, HEAD:HEAD+1] if h == 0 else o[:, 0:1], 1.0)
            outs.append(o * (1.0 / l))
            lses.append(m + jnp.log(l))
        o_ref[rows, :] = jnp.where(low_q, outs[0], outs[1]).astype(o_ref.dtype)
        lse_ref[rows, :] = jnp.where(low_q, lses[0], lses[1])

def attn_fwd(q, kvs, qc, kc, deps, chunk=128):
    F, W = q.shape
    P = len(kvs)
    T = P * F
    npair = W // 128
    return pl.pallas_call(
        functools.partial(attn_fwd_kernel, P=P, chunk=min(chunk, F)),
        grid=(npair,),
        in_specs=[pl.BlockSpec((F, 128), lambda a: (0, a)),
                  pl.BlockSpec((F, 128), lambda a: (0, 0)),
                  pl.BlockSpec((T, 128), lambda a: (0, 0))]
                 + [pl.BlockSpec((F, 128), lambda a: (0, a))] * P
                 + [pl.BlockSpec((F, 128), lambda a, n=npair: (0, a + n))] * P
                 + [ANY] * len(deps),
        out_specs=[pl.BlockSpec((F, 128), lambda a: (0, a)), pl.BlockSpec((F, 128), lambda a: (0, a))],
        out_shape=[jax.ShapeDtypeStruct((F, W), jnp.bfloat16), jax.ShapeDtypeStruct((F, W), jnp.float32)],
        scratch_shapes=[pltpu.VMEM((2, T, 128), jnp.bfloat16), pltpu.VMEM((2, T, 128), jnp.bfloat16)],
        cost_estimate=COST,
        name="attn_fwd",
    )(q, qc, kc, *kvs, *kvs, *deps)

def attn_bwd_kernel(*refs, P, chunk):
    q_ref, do_ref, o_ref, lse_ref, qc_ref, kc_ref = refs[:6]
    k_refs = refs[6:6+P]
    v_refs = refs[6+P:6+2*P]
    dq_ref, dk_ref, dv_ref = refs[-2-P:1-P]
    far_refs = refs[1-P:]
    F = q_ref.shape[0]
    low_q = lax.broadcasted_iota(jnp.int32, (F, 128), 1) < HEAD
    low_c = lax.broadcasted_iota(jnp.int32, (chunk, 128), 1) < HEAD
    q = q_ref[...] * jnp.asarray(0.125, jnp.bfloat16)
    do = do_ref[...]
    lse_t = lse_ref[...].T
    prod_t = (do.astype(jnp.float32) * o_ref[...].astype(jnp.float32)).T
    lse_row = [lse_t[h*HEAD:h*HEAD+1, :] for h in range(2)]
    delta_row = [jnp.sum(prod_t[h*HEAD:(h+1)*HEAD, :], axis=0, keepdims=True) for h in range(2)]
    qa = [jnp.where(low_q if h == 0 else jnp.logical_not(low_q), q, qc_ref[...]) for h in range(2)]
    zero = jnp.zeros((), jnp.bfloat16)
    dqt = [jnp.zeros((HEAD, F), jnp.float32) for _ in range(2)]
    for p in range(P):
        for c in range(F // chunk):
            rows = slice(c*chunk, (c+1)*chunk)
            k = k_refs[p][rows, :]
            v = v_refs[p][rows, :]
            kc = kc_ref[p*F + c*chunk: p*F + (c+1)*chunk, :]
            kt = k.T
            dks, dvs = [], []
            for h in range(2):
                pick = low_c if h == 0 else jnp.logical_not(low_c)
                st = nt(jnp.where(pick, k, kc), qa[h])
                pt = jnp.exp(st - lse_row[h])
                dpt = nt(jnp.where(pick, v, zero), do)
                dst = (pt * (dpt - delta_row[h])).astype(jnp.bfloat16)
                dvs.append(jnp.dot(pt.astype(jnp.bfloat16), do, preferred_element_type=jnp.float32))
                dks.append(jnp.dot(dst, q, preferred_element_type=jnp.float32))
                dqt[h] = dqt[h] + jnp.dot(kt[h*HEAD:(h+1)*HEAD, :], dst, preferred_element_type=jnp.float32)
            dk = jnp.where(low_c, dks[0], dks[1])
            dv = jnp.where(low_c, dvs[0], dvs[1])
            if p == 0:
                dk_ref[rows, :] = dk
                dv_ref[rows, :] = dv
            else:
                far_refs[p-1][0, rows, :] = dk.astype(jnp.bfloat16)
                far_refs[p-1][1, rows, :] = dv.astype(jnp.bfloat16)
    dq = jnp.concatenate(dqt, axis=0).T * 0.125
    dq_ref[...] = dq.astype(dq_ref.dtype)

def attn_bwd(q, do, o, lse, kvs, qc, kc, first, count, deps, chunk=128):
    F, W = q.shape
    P = len(kvs)
    T = P * F
    npair = W // 128
    own = pl.BlockSpec((F, 128), lambda a: (0, a + first))
    out = pl.BlockSpec((F, 128), lambda a: (0, a))
    return pl.pallas_call(
        functools.partial(attn_bwd_kernel, P=P, chunk=min(chunk, F)),
        grid=(count,),
        in_specs=[own, own, own, own,
                  pl.BlockSpec((F, 128), lambda a: (0, 0)),
                  pl.BlockSpec((T, 128), lambda a: (0, 0))]
                 + [own] * P
                 + [pl.BlockSpec((F, 128), lambda a, n=npair: (0, a + first + n))] * P
                 + [ANY] * len(deps),
        out_specs=[out] * 3 + [pl.BlockSpec((2, F, 128), lambda a: (0, 0, a))] * (P - 1),
        out_shape=[jax.ShapeDtypeStruct((F, 128 * count), t) for t in (jnp.bfloat16, jnp.float32, jnp.float32)]
                  + [jax.ShapeDtypeStruct((2, F, 128 * count), jnp.bfloat16)] * (P - 1),
        cost_estimate=COST,
        name="attn_bwd",
    )(q, do, o, lse, qc, kc, *kvs, *kvs, *deps)

HALO = 64
UTT_LEAST = 256
root_half = 0.7071067811865476
inv_root_two_pi = 0.3989422804014327
f32 = jnp.float32
bf16 = jnp.bfloat16


def layer_norm(hidden):
    centred = hidden - jnp.mean(hidden, axis=-1, keepdims=True)
    inv_scale = lax.rsqrt(jnp.mean(centred * centred, axis=-1, keepdims=True) + 1e-05)
    return (centred * inv_scale, inv_scale)


def norm_back(grad_normed, normed, inv_scale):
    return inv_scale * (
        grad_normed
        - jnp.mean(grad_normed, axis=-1, keepdims=True)
        - normed * jnp.mean(grad_normed * normed, axis=-1, keepdims=True)
    )


def gelu(entries):
    return 0.5 * entries * (1.0 + lax.erf(entries * root_half))


def gelu_slope(entries):
    return (
        0.5 * (1.0 + lax.erf(entries * root_half))
        + entries * jnp.exp(-0.5 * entries * entries) * inv_root_two_pi
    )


def mm(a, b):
    return jnp.dot(a, b, preferred_element_type=f32)


def mm_back(a, b):
    return lax.dot_general(a, b, (((1,), (1,)), ((), ())), preferred_element_type=f32)


def wgrad(a, b):
    return lax.dot_general(a, b, (((0,), (0,)), ((), ())), preferred_element_type=f32)


class Plan:
    def __init__(self, dp, seq, rows_dev):
        self.dp, self.seq, self.n = dp, seq, rows_dev
        self.q = seq // (2 * rows_dev)
        self.P = 2 * self.q
        assert dp % 2 == 0 and self.q * 2 * rows_dev == seq and rows_dev > 1

    def out_pairs(self, m):
        pairs = []
        for d in range(self.dp):
            for z in range(self.seq):
                rho = self.n * (d % 2) + (z + m) % self.n
                u = z // self.n
                pairs.append((d * self.seq + z, self.member(d // 2, rho, u)))
        return pairs

    def edge_pairs(self):
        heads = [[] for _ in range(self.n)]
        tails = [[] for _ in range(self.n)]
        for d in range(self.dp):
            for z in range(self.seq):
                u = z // self.n
                for j in range(self.n):
                    rho = self.n * (d % 2) + j
                    if z % self.n == self.n - 1 and u + 1 < self.P:
                        tails[j].append((d * self.seq + z, self.member(d // 2, rho, u + 1)))
                    if z % self.n == 0 and u > 0:
                        heads[j].append((d * self.seq + z, self.member(d // 2, rho, u - 1)))
        return heads, tails

    def member(self, e, rho, u):
        return (2 * e + u % 2) * self.seq + rho * self.q + u // 2

    def team_pairs(self, shift, wrap):
        pairs = []
        for e in range(self.dp // 2):
            for rho in range(2 * self.n):
                for u in range(self.P):
                    to = u + shift
                    if wrap or 0 <= to < self.P:
                        pairs.append((self.member(e, rho, u), self.member(e, rho, to % self.P)))
        return pairs


BOTH = ("dp", "seq")


def on_device(
    frames,
    output_gradient,
    segments,
    layer_keep,
    conv_weight,
    convolution_bias,
    query_matrix,
    query_offset_bias,
    key_matrix,
    value_matrix,
    value_offset_bias,
    attn_weight,
    attn_bias,
    first_gain,
    first_shift,
    inner_weight,
    inner_bias,
    outer_weight,
    outer_bias,
    second_gain,
    second_shift,
):
    rows_dev, local_len, width = frames.shape
    total_rows, row_len = segments.shape
    dp_count, seq_count = lax.axis_size("dp"), lax.axis_size("seq")
    dp_index, seq_index = lax.axis_index("dp"), lax.axis_index("seq")
    plan = Plan(dp_count, seq_count, rows_dev)
    n, q, team = plan.n, plan.q, plan.P
    F = row_len // team
    taps, _, gw = conv_weight.shape
    tap_blocks = taps // DK
    rho = seq_index // q
    member = (seq_index % q) * 2 + dp_index % 2
    row_id = (dp_index // 2) * (2 * n) + rho

    def pick(parts, index):
        out = parts[0]
        for k in range(1, len(parts)):
            out = jnp.where(index == k, parts[k], out)
        return out

    def blocks_to_team(a):
        got = []
        for m in range(n):
            sent = pick([a[j] for j in range(n)], (seq_index + m) % n)
            got.append(lax.ppermute(sent, BOTH, plan.out_pairs(m)))
        return got

    def from_team(sent):
        back = [
            lax.ppermute(sent[m], BOTH, [(t, s) for s, t in plan.out_pairs(m)]) for m in range(n)
        ]
        return jnp.stack([pick(back, (row - seq_index) % n) for row in range(n)], 0)

    def edges_to_team(a):
        heads, tails = plan.edge_pairs()
        lows, highs = [], []
        for j in range(n):
            tail, head = a[j, local_len - HALO :], a[j, :HALO]
            if team == 2:
                got = lax.ppermute(
                    jnp.where(seq_index % n == 0, head, tail), BOTH, heads[j] + tails[j]
                )
                lows.append(got)
                highs.append(got)
            else:
                lows.append(lax.ppermute(tail, BOTH, tails[j]))
                highs.append(lax.ppermute(head, BOTH, heads[j]))
        return lows, highs

    def edges(a):
        if team == 2:
            got = lax.ppermute(
                jnp.where(member == 0, a[F - HALO :], a[:HALO]), BOTH, plan.team_pairs(1, True)
            )
            return got, got
        low = lax.ppermute(a[F - HALO :], BOTH, plan.team_pairs(1, False))
        high = lax.ppermute(a[:HALO], BOTH, plan.team_pairs(-1, False))
        return low, high

    def pairs_of(axis, bit):
        pairs = []
        for d in range(dp_count):
            for z in range(seq_count):
                to = (d ^ bit, z) if axis == "dp" else (d, z ^ bit)
                pairs.append((d * seq_count + z, to[0] * seq_count + to[1]))
        return pairs

    def halve(a, axis, index, bit, high, low):
        mine = (index // bit) % 2
        a = a.reshape((high, 2, low) + a.shape[1:])
        sent = pick([a[:, 0], a[:, 1]], 1 - mine).reshape((high * low,) + a.shape[3:])
        kept = pick([a[:, 0], a[:, 1]], mine).reshape(sent.shape)
        return kept, lax.ppermute(sent, BOTH, pairs_of(axis, bit)), sent

    class Scatter:
        def __init__(self, halves, swap, many=1):
            bits = [1 << i for i in range(dp_count.bit_length() - 1)]
            order = [1] + (bits[1:] if swap else bits[:0:-1])
            left = list(reversed(bits))
            self.steps = []
            for bit in order:
                at = left.index(bit)
                self.steps.append((bit, many * 2**at, 2 ** (len(left) - 1 - at)))
                left.remove(bit)
            self.steps.pop(0)
            self.sent, self.kept = halves
            self.got = lax.ppermute(self.sent, BOTH, pairs_of("dp", 1))

        def step(self, *deps):
            bit, high, low = self.steps.pop(0)
            mine = ((dp_index // bit) % 2).astype(jnp.int32).reshape(1)
            self.sent, self.kept = join_split(self.kept, self.got, mine, high, low, deps)
            self.got = lax.ppermute(self.sent, BOTH, pairs_of("dp", bit))

        def last(self, *deps):
            while self.steps:
                self.step(*deps)
            return join_last(self.kept, self.got, deps)

    class SeqSum:
        def __init__(self, a):
            self.shape = a.shape
            self.a = a.astype(bf16).reshape(seq_count, -1, a.shape[1])
            bits = [1 << i for i in range(seq_count.bit_length() - 1)]
            left = list(reversed(bits))
            self.steps = []
            for bit in bits:
                at = left.index(bit)
                self.steps.append((bit, 2**at, 2 ** (len(left) - 1 - at)))
                left.remove(bit)
            self.back = list(reversed(bits))
            bit, high, low = self.steps.pop(0)
            self.kept, self.got, self.sent = halve(self.a, "seq", seq_index, bit, high, low)

        def step(self, *deps):
            if self.steps:
                bit, high, low = self.steps.pop(0)
                mine = ((seq_index // bit) % 2).astype(jnp.int32).reshape(1)
                self.sent, self.kept = join_split(self.kept, self.got, mine, high, low, deps)
                self.got = lax.ppermute(self.sent, BOTH, pairs_of("seq", bit))

        def whole(self):
            self.add()
            return self.finish()

        def add(self, *deps):
            while self.steps:
                self.step(*deps)
            self.a = join_last(self.kept, self.got, deps).reshape(self.kept.shape)

        def finish(self, *deps):
            a = self.a
            for bit in self.back:
                other = lax.ppermute(a, BOTH, pairs_of("seq", bit))
                low_half = (seq_index // bit) % 2 == 0
                pair = jnp.where(low_half, jnp.stack([a, other], 1), jnp.stack([other, a], 1))
                a = pair.reshape((-1,) + a.shape[1:])
            return a.reshape(self.shape)

    def by_dp(a):
        return a.reshape(dp_count, -1, a.shape[-1])

    def by_share(a):
        a = a.reshape(dp_count, width // dp_count, a.shape[1])
        out, sent = [], []
        for k in range(dp_count):
            piece = lax.dynamic_index_in_dim(a, dp_index ^ k, 0, keepdims=False)
            sent.append(piece)
            out.append(piece if k == 0 else lax.ppermute(piece, BOTH, pairs_of("dp", k)))
        return out, sent

    weight_tr = prep(conv_weight)

    x_blocks = blocks_to_team(frames)
    x_lows, x_highs = edges_to_team(frames)
    g_blocks = blocks_to_team(output_gradient)

    gaps = 1 + max(F - 2, 0) // UTT_LEAST
    spread = -(-(F + 2 * HALO + HALO * gaps) // 128) * 128
    out_spread = -(-(F + HALO * gaps) // 128) * 128
    (
        convolution_bias, query_offset_bias, value_offset_bias, attn_bias, first_gain, first_shift,
        inner_bias, outer_bias, second_gain, second_shift,
    ) = vectors = [
        v.reshape(1, -1)
        for v in (
            convolution_bias, query_offset_bias, value_offset_bias, attn_bias, first_gain, first_shift,
            inner_bias, outer_bias, second_gain, second_shift,
        )
    ]
    where_at = jnp.stack([row_id, member, rho % n]).astype(jnp.int32)
    x, spread_x, select, q_codes, k_codes = build_x(
        where_at, segments, x_blocks, x_lows, x_highs, team, F, gaps, spread, (weight_tr,)
    )
    conv_t = conv(spread_x, weight_tr, select, F, gaps)
    x_shares = lax.all_to_all(
        spread_x.reshape(dp_count, width // dp_count, spread), "dp", 0, 0, tiled=True
    )

    conv_before, pos_out, pos_low, query, kv = front(
        conv_t, convolution_bias, x, query_matrix, key_matrix, value_matrix, query_offset_bias,
        value_offset_bias, (x_shares,),
    )
    kvs = [kv] + [lax.ppermute(kv, BOTH, plan.team_pairs(s, True)) for s in range(1, team)]
    attn_low, lse = attn_fwd(query, kvs, q_codes, k_codes, (), 512)

    outs = mid(
        where_at, layer_keep, attn_low, pos_out, g_blocks, attn_weight, inner_weight, outer_weight,
        attn_bias, first_gain, first_shift, inner_bias, outer_bias, second_gain, second_shift, (),
    )
    layer_out = from_team(outs[:n])
    (
        first_low, inner_low, grad_outer_low, grad_inner_low, grad_attn_low, grad_first_sum,
        grad_heads, inner_sums, mid_sums,
    ) = outs[n:]
    core = (dp_index % 2).astype(jnp.int32).reshape(1)
    ff_share = inner_weight.shape[1] // dp_count
    by_rows = ff_share % 128 != 0
    outer_t = wg_plain(grad_outer_low, inner_low, 2, 0)
    outer_share = lax.psum_scatter(outer_t, "dp", scatter_dimension=0, tiled=True)
    extras = (inner_sums, mid_sums)
    pairs = width // 128
    grads = []
    deps = (outer_t,)
    grads.append(attn_bwd(query, grad_heads, attn_low, lse, kvs, q_codes, k_codes, 0, pairs, deps, 512))
    fars = [
        [lax.ppermute(g[2 + s], BOTH, plan.team_pairs(-s, True)) for s in range(1, team)]
        for g in grads
    ]
    if by_rows:
        inner_t = wg_plain(grad_inner_low, first_low, 1, 0, (grads[0][0],))
    else:
        inner_t = wg_plain(first_low, grad_inner_low, 2, ff_share, (grads[0][0],)).reshape(-1, ff_share)
    inner_share = lax.psum_scatter(inner_t, "dp", scatter_dimension=0, tiled=True)
    low_qk, low_v, grad_pos, grad_conv_low, qk_sums, v_sums = dpos(
        where_at, layer_keep, *[[g[k] for g in grads] for k in range(3)], fars, query_matrix,
        key_matrix, value_matrix, grad_first_sum, g_blocks, conv_before, (inner_t,),
    )

    d_pieces = build_d(where_at, segments, grad_conv_low, (), team, gaps, out_spread).reshape(
        dp_count, width // dp_count, out_spread
    )
    d_shares = lax.all_to_all(d_pieces, "dp", 0, 0, tiled=True)
    low, high = edges(grad_conv_low)
    slots = 2 * dp_count // 2
    qk_sum = Scatter(
        wg_rows(core, low_qk, pos_low, 2, dp_count, 1, (qk_sums,), (d_pieces,)), True, 2
    )
    halves = wg_rows(core, low_v, pos_low, 1, dp_count, 1, (v_sums,), (qk_sum.sent,), slots)
    halves = wg_rows(core, grad_attn_low, attn_low, 1, dp_count, 1, extras, (), slots, 1, halves)
    va_sum = Scatter(halves, False, 2)
    spread_d = build_d(
        where_at, segments, grad_conv_low, (low, high), team, gaps, spread, (va_sum.sent,)
    )
    part = conv_dw(x_shares, d_shares, gw, tap_blocks, (spread_d,))
    conv_sum = SeqSum(part)
    qk_sum.step(conv_sum.sent)
    va_sum.step(qk_sum.sent)
    groups = width // gw
    outer_z = SeqSum(outer_share)
    back_a = conv_dx(
        spread_d, weight_tr, select, F, gaps, 0, groups // 2, (outer_z.sent, va_sum.sent)
    )
    conv_sum.step(back_a)
    inner_z = SeqSum(inner_share)
    outer_z.step(conv_sum.sent)
    qk_sum.step(outer_z.sent)
    va_sum.step(qk_sum.sent)
    back_b = conv_dx(
        spread_d, weight_tr, select, F, gaps, groups // 2, groups - groups // 2,
        (va_sum.sent, inner_z.sent),
    )
    conv_sum.add(back_b, layer_out)
    qk_share = qk_sum.last(conv_sum.a)
    va_share = va_sum.last(qk_share)
    inner_z.step(va_share)
    proj = SeqSum(jnp.concatenate([qk_share, va_share], 0))
    outer_z.add(inner_z.sent)
    sent = grad_in(
        where_at, segments, grad_pos, (back_a, back_b), n, (outer_z.a, proj.sent)
    )
    grad_input = from_team(sent)
    proj.step(sent[0])
    outer_sum = outer_z.finish()
    conv_sum = conv_sum.finish()
    inner_z.add(proj.sent)
    proj.add(inner_z.a)
    grad_conv_weight = finish_dw(conv_sum, gw, tap_blocks)
    proj_pack = proj.finish().astype(f32)
    grad_conv_bias = conv_sum.reshape(-1, tap_blocks * gw + 32, DK * gw)[:, tap_blocks * gw, :gw].reshape(-1).astype(f32)
    o_g, i_g = widen((outer_sum, inner_z.finish()), (grad_conv_bias,))
    o_g = o_g.T
    i_g = i_g.T if by_rows else i_g

    share = width // dp_count
    ff = inner_bias.shape[1]
    pieces = proj_pack.reshape(4, -1, width)
    q_g, k_g, v_g, a_g = (pieces[k, :share].T for k in range(4))
    small = pieces[3, share : share + ff // width + 6]
    inner_bias_share = lax.dynamic_slice_in_dim(
        small[: ff // width].reshape(-1), dp_index * (ff // dp_count), ff // dp_count
    )
    rows_ = jnp.concatenate(
        [small[ff // width :], pieces[0, share : share + 1], pieces[2, share : share + 1]]
    )
    rows_ = lax.dynamic_slice_in_dim(rows_, dp_index * share, share, 1)
    vecs = [rows_[6], rows_[7]] + [rows_[k] for k in range(6)] + [grad_conv_bias]
    return (
        layer_out,
        grad_input,
        grad_conv_weight,
        vecs[8],
        q_g,
        vecs[0],
        k_g,
        v_g,
        vecs[1],
        a_g,
        vecs[2],
        vecs[3],
        vecs[4],
        i_g,
        inner_bias_share,
        o_g,
        vecs[5],
        vecs[6],
        vecs[7],
    )


def solution(mesh):
    rows = P("dp", "seq", None)
    by_col, vec = P(None, "dp"), P("dp")
    out_specs = (
        rows, rows, P(None, "dp", None), vec, by_col, vec, by_col, by_col, vec, by_col, vec, vec,
        vec, by_col, vec, by_col, vec, vec, vec,
    )
    return jax.shard_map(
        on_device, mesh=mesh, in_specs=(rows, rows) + (P(),) * 19, out_specs=out_specs, check_vma=False
    )
```
